32 devices in a mesh: net: 2 (over core), batch: 16 (over z, y, x).
Axes of the slice: x: 2, y: 2, z: 4, core: 2. Of those that a mesh axis runs over, the one named last changes fastest.
Arguments:
- states: float32 [17, 180224], P(None, 'batch'), may hold values from -6 to 6
- next_states: float32 [17, 180224], P(None, 'batch'), may hold values from -6 to 6
- actions: float32 [6, 180224], P(None, 'batch'), may hold values from -1 to 1
- rewards: float32 [180224], P('batch'), may hold values from -6 to 6
- finished: int32 [180224], P('batch'), may hold values 0 or 1
- valid_counts: int32 [16], P('batch'), may hold values from 3754 to 11264, as said below
- trunk_input: float32 [2, 17, 256], P('net'), may hold values from -1.5 to 1.5
- trunk_middle: float32 [2, 256, 256], P('net'), may hold values from -0.375 to 0.375
- trunk_vector: float32 [2, 512], P('net'), may hold values from -0.625 to 0.625
- head_weight: float32 [256, 7], replicated, may hold values from -0.375 to 0.375
- head_vector: float32 [13], replicated, may hold values from -1.75 to 1.75
- critic_input: float32 [2, 23, 256], P('net'), may hold values from -1.25 to 1.25
- critic_middle: float32 [2, 256, 256], P('net'), may hold values from -0.375 to 0.375
- critic_vector: float32 [2, 769], P('net'), may hold values from -0.625 to 0.625
- target_input: float32 [2, 23, 256], P('net'), may hold values from -1.25 to 1.25
- target_middle: float32 [2, 256, 256], P('net'), may hold values from -0.375 to 0.375
- target_vector: float32 [2, 769], P('net'), may hold values from -0.625 to 0.625
- mean_trunk_input: float32 [2, 17, 256], P('net'), may hold values from -0.0014648438 to 0.0014648438
- square_trunk_input: float32 [2, 17, 256], P('net'), may hold values from 2.7743252e-09 to 4.4389203e-08
- mean_trunk_middle: float32 [2, 256, 256], P('net'), may hold values from -0.0014648438 to 0.0014648438
- square_trunk_middle: float32 [2, 256, 256], P('net'), may hold values from 2.7743252e-09 to 4.4389203e-08
- mean_trunk_vector: float32 [2, 512], P('net'), may hold values from -0.0014648438 to 0.0014648438
- square_trunk_vector: float32 [2, 512], P('net'), may hold values from 2.7743252e-09 to 4.4389203e-08
- mean_head_weight: float32 [256, 7], replicated, may hold values from -0.0014648438 to 0.0014648438
- square_head_weight: float32 [256, 7], replicated, may hold values from 2.7743252e-09 to 4.4389203e-08
- mean_head_vector: float32 [13], replicated, may hold values from -0.0014648438 to 0.0014648438
- square_head_vector: float32 [13], replicated, may hold values from 2.7743252e-09 to 4.4389203e-08
- mean_critic_input: float32 [2, 23, 256], P('net'), may hold values from -0.0014648438 to 0.0014648438
- square_critic_input: float32 [2, 23, 256], P('net'), may hold values from 2.7743252e-09 to 4.4389203e-08
- mean_critic_middle: float32 [2, 256, 256], P('net'), may hold values from -0.0014648438 to 0.0014648438
- square_critic_middle: float32 [2, 256, 256], P('net'), may hold values from 2.7743252e-09 to 4.4389203e-08
- mean_critic_vector: float32 [2, 769], P('net'), may hold values from -0.0014648438 to 0.0014648438
- square_critic_vector: float32 [2, 769], P('net'), may hold values from 2.7743252e-09 to 4.4389203e-08
Outputs:
- updated_trunk_input: float32 [2, 17, 256], P('net')
- updated_trunk_middle: float32 [2, 256, 256], P('net')
- updated_trunk_vector: float32 [2, 512], P('net')
- updated_head_weight: float32 [256, 7], replicated
- updated_head_vector: float32 [13], replicated
- updated_critic_input: float32 [2, 23, 256], P('net')
- updated_critic_middle: float32 [2, 256, 256], P('net')
- updated_critic_vector: float32 [2, 769], P('net')
- updated_mean_trunk_input: float32 [2, 17, 256], P('net')
- updated_mean_trunk_middle: float32 [2, 256, 256], P('net')
- updated_mean_trunk_vector: float32 [2, 512], P('net')
- updated_mean_head_weight: float32 [256, 7], replicated
- updated_mean_head_vector: float32 [13], replicated
- updated_mean_critic_input: float32 [2, 23, 256], P('net')
- updated_mean_critic_middle: float32 [2, 256, 256], P('net')
- updated_mean_critic_vector: float32 [2, 769], P('net')
- updated_square_trunk_input: float32 [2, 17, 256], P('net')
- updated_square_trunk_middle: float32 [2, 256, 256], P('net')
- updated_square_trunk_vector: float32 [2, 512], P('net')
- updated_square_head_weight: float32 [256, 7], replicated
- updated_square_head_vector: float32 [13], replicated
- updated_square_critic_input: float32 [2, 23, 256], P('net')
- updated_square_critic_middle: float32 [2, 256, 256], P('net')
- updated_square_critic_vector: float32 [2, 769], P('net')
- updated_target_input: float32 [2, 23, 256], P('net')
- updated_target_middle: float32 [2, 256, 256], P('net')
- updated_target_vector: float32 [2, 769], P('net')
- lamb_norms: float32 [2, 8, 2], P('net')
- losses: float32 [5], replicated
The draws below stay inside these ranges and needn't reach their ends.
Inputs may be any that keep to these rules, and one draw needn't show every extreme that they name: `valid_counts`: entries are at least 3754, and run from near 11264 // 3 on its first shard to exactly 11264 on its last.
All inputs are finite; a program needn't handle non-finite values. No bound on the sum of `finished` on one device may be relied on, other than what follows from the above.
Results may differ from the reference program's by a relative error of at most 0.0003.
Values sent between devices are 32-bit elements; how exact they have to be, the bound alone decides.
No kernel may reach another device: no remote copies, remote signals or barrier semaphores. Data moves between devices by JAX's collectives and lax.ppermute only.
A program may use at most 192 MiB of HBM per device.

```python
import math
import jax
import jax.numpy as jnp
from jax import lax

OBS = 17
ACT = 6
HID = 256
ROWS = 11264
STEP = 10
TRANSITIONS = 180224
N_BATCH = 16


def draw_valid_counts(key, part):
    key = jax.random.fold_in(key, 7)
    device_total = TRANSITIONS // ROWS
    position = jnp.arange(device_total, dtype=jnp.int32)
    lowest = ROWS // 3
    rising = lowest + position * (ROWS - lowest - ROWS // 8) // max(device_total - 1, 1)
    jitter = jax.random.randint(key, (device_total,), 0, ROWS // 8 + 1, dtype=jnp.int32)
    result = jnp.minimum(rising + jitter, ROWS)
    return jnp.where(position == device_total - 1, ROWS, result).astype(jnp.int32)


def place_ends(entries, stream_key, smallest, largest):
    place = [jax.random.randint(jax.random.fold_in(stream_key, axis), (), 0, length) for axis, length in enumerate(entries.shape)]
    widest = entries.shape.index(max(entries.shape))
    next_to = place[:widest] + [(place[widest] + 1) % entries.shape[widest]] + place[widest + 1:]
    return entries.at[tuple(place)].set(smallest).at[tuple(next_to)].set(largest)


def block_levels(rng, dims, split, smallest, high):
    level, own = 1.0, jax.random.fold_in(rng, 6)
    for dim, blocks in split:
        draws = jnp.exp(jax.random.uniform(jax.random.fold_in(own, dim), (blocks,), jnp.float32, smallest / len(split), high / len(split)))
        level = level * jnp.repeat(draws, dims[dim] // blocks).reshape([-1 if axis == dim else 1 for axis in range(len(dims))])
    return level


def noise(rng, dims, deviation, reach, cuts=(), kind=jnp.bfloat16):
    drawn = deviation * jax.random.normal(rng, dims, jnp.float32)
    if cuts:
        drawn = drawn * block_levels(rng, dims, cuts, -0.22, 0.18)
    return jnp.clip(drawn, -reach, reach).astype(kind)


def setup_inputs(seed: int = 0) -> dict:
    splits = jax.random.split(jax.random.key(seed), 34)
    return {
        "states": noise(splits[0], (OBS, TRANSITIONS), 1.0, 6.0, ((1, 16),), jnp.float32),
        "next_states": noise(splits[1], (OBS, TRANSITIONS), 1.0, 6.0, ((1, 16),), jnp.float32),
        "actions": jnp.clip(jax.random.uniform(splits[2], (ACT, TRANSITIONS), jnp.float32, -1.0, 1.0) * block_levels(splits[2], (ACT, TRANSITIONS), ((1, 16),), -0.4, 0.0), -1.0, 1.0),
        "rewards": noise(splits[3], (TRANSITIONS,), 1.0, 6.0, ((0, 16),), jnp.float32),
        "finished": place_ends((jax.random.randint(splits[4], (TRANSITIONS,), 0, 8) < 1).astype(jnp.int32), jax.random.fold_in(splits[4], 1), 0, 1),
        "valid_counts": draw_valid_counts(jax.random.fold_in(splits[33], 71), 0),
        "trunk_input": noise(splits[6], (2, OBS, HID), OBS ** -0.5, 1.5, ((0, 2),), jnp.float32),
        "trunk_middle": noise(splits[7], (2, HID, HID), HID ** -0.5, 0.375, ((0, 2),), jnp.float32),
        "trunk_vector": noise(splits[8], (2, 2 * HID), 0.1, 0.625, ((0, 2),), jnp.float32),
        "head_weight": noise(splits[9], (HID, 7), HID ** -0.5, 0.375, (), jnp.float32),
        "head_vector": noise(splits[10], (13,), 0.3, 1.75, (), jnp.float32),
        "critic_input": noise(splits[11], (2, OBS + ACT, HID), (OBS + ACT) ** -0.5, 1.25, ((0, 2),), jnp.float32),
        "critic_middle": noise(splits[12], (2, HID, HID), HID ** -0.5, 0.375, ((0, 2),), jnp.float32),
        "critic_vector": noise(splits[13], (2, 3 * HID + 1), 0.1, 0.625, ((0, 2),), jnp.float32),
        "target_input": noise(splits[14], (2, OBS + ACT, HID), (OBS + ACT) ** -0.5, 1.25, ((0, 2),), jnp.float32),
        "target_middle": noise(splits[15], (2, HID, HID), HID ** -0.5, 0.375, ((0, 2),), jnp.float32),
        "target_vector": noise(splits[16], (2, 3 * HID + 1), 0.1, 0.625, ((0, 2),), jnp.float32),
        "mean_trunk_input": noise(splits[17], (2, OBS, HID), (0.11 * TRANSITIONS ** -0.5), 0.0014648438, ((0, 2),), jnp.float32),
        "square_trunk_input": jnp.clip(jnp.exp(math.log(4.438920342408892e-08) - 2.7725887 * jax.random.uniform(splits[18], (2, OBS, HID), jnp.float32) ** block_levels(splits[18], (2, OBS, HID), ((0, 2),), -0.2, 0.2)), 2.7743252140055574e-09, 4.438920342408892e-08),
        "mean_trunk_middle": noise(splits[19], (2, HID, HID), (0.11 * TRANSITIONS ** -0.5), 0.0014648438, ((0, 2),), jnp.float32),
        "square_trunk_middle": jnp.clip(jnp.exp(math.log(4.438920342408892e-08) - 2.7725887 * jax.random.uniform(splits[20], (2, HID, HID), jnp.float32) ** block_levels(splits[20], (2, HID, HID), ((0, 2),), -0.2, 0.2)), 2.7743252140055574e-09, 4.438920342408892e-08),
        "mean_trunk_vector": noise(splits[21], (2, 2 * HID), (0.11 * TRANSITIONS ** -0.5), 0.0014648438, ((0, 2),), jnp.float32),
        "square_trunk_vector": jnp.clip(jnp.exp(math.log(4.438920342408892e-08) - 2.7725887 * jax.random.uniform(splits[22], (2, 2 * HID), jnp.float32) ** block_levels(splits[22], (2, 2 * HID), ((0, 2),), -0.2, 0.2)), 2.7743252140055574e-09, 4.438920342408892e-08),
        "mean_head_weight": noise(splits[23], (HID, 7), (0.11 * TRANSITIONS ** -0.5), 0.0014648438, (), jnp.float32),
        "square_head_weight": jnp.clip(jnp.exp(jax.random.uniform(splits[24], (HID, 7), jnp.float32, math.log(2.7743252140055574e-09), math.log(4.438920342408892e-08))), 2.7743252140055574e-09, 4.438920342408892e-08),
        "mean_head_vector": noise(splits[25], (13,), (0.11 * TRANSITIONS ** -0.5), 0.0014648438, (), jnp.float32),
        "square_head_vector": jnp.clip(jnp.exp(jax.random.uniform(splits[26], (13,), jnp.float32, math.log(2.7743252140055574e-09), math.log(4.438920342408892e-08))), 2.7743252140055574e-09, 4.438920342408892e-08),
        "mean_critic_input": noise(splits[27], (2, OBS + ACT, HID), (0.11 * TRANSITIONS ** -0.5), 0.0014648438, ((0, 2),), jnp.float32),
        "square_critic_input": jnp.clip(jnp.exp(math.log(4.438920342408892e-08) - 2.7725887 * jax.random.uniform(splits[28], (2, OBS + ACT, HID), jnp.float32) ** block_levels(splits[28], (2, OBS + ACT, HID), ((0, 2),), -0.2, 0.2)), 2.7743252140055574e-09, 4.438920342408892e-08),
        "mean_critic_middle": noise(splits[29], (2, HID, HID), (0.11 * TRANSITIONS ** -0.5), 0.0014648438, ((0, 2),), jnp.float32),
        "square_critic_middle": jnp.clip(jnp.exp(math.log(4.438920342408892e-08) - 2.7725887 * jax.random.uniform(splits[30], (2, HID, HID), jnp.float32) ** block_levels(splits[30], (2, HID, HID), ((0, 2),), -0.2, 0.2)), 2.7743252140055574e-09, 4.438920342408892e-08),
        "mean_critic_vector": noise(splits[31], (2, 3 * HID + 1), (0.11 * TRANSITIONS ** -0.5), 0.0014648438, ((0, 2),), jnp.float32),
        "square_critic_vector": jnp.clip(jnp.exp(math.log(4.438920342408892e-08) - 2.7725887 * jax.random.uniform(splits[32], (2, 3 * HID + 1), jnp.float32) ** block_levels(splits[32], (2, 3 * HID + 1), ((0, 2),), -0.2, 0.2)), 2.7743252140055574e-09, 4.438920342408892e-08),
    }


@jax.custom_vjp
def low(v):
    return lax.optimization_barrier(v.astype(jnp.bfloat16)).astype(jnp.float32)

@jax.custom_vjp
def low_back(v):
    return v

def low_keep(v):
    return (low(v), None)

def low_pass(kept, grad):
    return (grad,)

def back_keep(v):
    return (v, None)

def back_low(kept, grad):
    return (low(grad),)
low.defvjp(low_keep, low_pass)
low_back.defvjp(back_keep, back_low)
HIGHEST_PRECISION = lax.Precision.HIGHEST
EXPECTILE = 0.7
DISCOUNT = 0.99
BETA_TEMP = 3.0
WEIGHT_CLIP = 100.0
DECAY_FIRST = 0.9
DECAY_SECOND = 0.999
EPSILON = 1e-06
WEIGHT_DECAY = 0.01
LEARN_RATE = 0.3
TARGET_RATE = 0.005
LOG_TWO_PI = math.log(2.0 * math.pi)

def apply_layer(weight, inputs):
    return jnp.einsum('fh,fr->hr', weight, inputs, precision=HIGHEST_PRECISION)

def trunk_out(weight_first, weight_second, vector, inputs):
    hidden_width = weight_second.shape[0]
    first_act = jax.nn.silu(apply_layer(weight_first, inputs) + vector[:hidden_width, None])
    return jax.nn.silu(apply_layer(weight_second, first_act) + vector[hidden_width:2 * hidden_width, None])

def critic_out(weight_first, weight_second, vector, inputs):
    hidden_width = weight_second.shape[0]
    hidden = trunk_out(weight_first, weight_second, vector, inputs)
    return jnp.einsum('h,hr->r', vector[2 * hidden_width:3 * hidden_width], hidden, precision=HIGHEST_PRECISION) + vector[3 * hidden_width]

def to_blocks(values_in):
    return jnp.transpose(values_in.reshape(values_in.shape[0], N_BATCH, ROWS), (1, 0, 2))

def block_sum(function, parameters, items, start):

    def advance(running, block_item):
        return (running + jax.checkpoint(function)(parameters, block_item), None)
    running, _ = lax.scan(advance, start, items)
    return running

def lamb_step(weight, gradient, mean_old, square_old):
    mean_new = DECAY_FIRST * mean_old + (1.0 - DECAY_FIRST) * gradient
    square_new = DECAY_SECOND * square_old + (1.0 - DECAY_SECOND) * gradient * gradient
    mean_hat = mean_new / (1.0 - DECAY_FIRST ** STEP)
    square_hat = square_new / (1.0 - DECAY_SECOND ** STEP)
    update = mean_hat / (jnp.sqrt(square_hat) + EPSILON) + WEIGHT_DECAY * weight
    weight_norm = jnp.sqrt(jnp.sum(weight * weight))
    update_norm = jnp.sqrt(jnp.sum(update * update))
    updated = weight - LEARN_RATE * (weight_norm / update_norm) * update
    return (updated, mean_new, square_new, jnp.stack([weight_norm, update_norm]))

def value_loss(parameters, block_item):
    weight_first, weight_second, vector, head_matrix, bias_vector = parameters
    state_block, target_block, row_mask = block_item
    hidden = trunk_out(weight_first, weight_second, vector, state_block)
    value_est = jnp.einsum('h,hr->r', head_matrix[:, 0], hidden, precision=HIGHEST_PRECISION) + bias_vector[0]
    value_gap = target_block - value_est
    weight = jnp.where(value_gap < 0.0, 1.0 - EXPECTILE, EXPECTILE)
    return jnp.sum(row_mask * weight * value_gap * value_gap)

def actor_loss(parameters, block_item):
    weight_first, weight_second, vector, head_matrix, bias_vector = parameters
    state_block, action_block, target_block, value_block, row_mask = block_item
    hidden = trunk_out(weight_first, weight_second, vector, state_block)
    action_means = jnp.tanh(jnp.einsum('hk,hr->kr', head_matrix[:, 1:], hidden, precision=HIGHEST_PRECISION) + bias_vector[1:7, None])
    log_std = bias_vector[7:13]
    scaled = (action_block - action_means) * jnp.exp(-log_std)[:, None]
    log_prob = lax.optimization_barrier(jnp.sum(-0.5 * scaled * scaled - log_std[:, None] - 0.5 * LOG_TWO_PI, axis=0))
    weight = jnp.minimum(jnp.exp(BETA_TEMP * (target_block - value_block)), WEIGHT_CLIP)
    return -jnp.sum(row_mask * weight * log_prob)

def critic_loss(parameters, block_item):
    weight_first, weight_second, vector = parameters
    pair_block, reward_block, finish_block, next_value, row_mask = block_item
    bellman_goal = reward_block + DISCOUNT * (1.0 - finish_block) * next_value
    member_sums = []
    for member in range(2):
        bellman_error = critic_out(weight_first[member], weight_second[member], vector[member], pair_block) - bellman_goal
        member_sums.append(jnp.sum(row_mask * bellman_error * bellman_error))
    return jnp.stack(member_sums)

def reference(states, next_states, actions, rewards, finished, valid_counts, trunk_input, trunk_middle, trunk_vector, head_weight, head_vector, critic_input, critic_middle, critic_vector, target_input, target_middle, target_vector, mean_trunk_input, square_trunk_input, mean_trunk_middle, square_trunk_middle, mean_trunk_vector, square_trunk_vector, mean_head_weight, square_head_weight, mean_head_vector, square_head_vector, mean_critic_input, square_critic_input, mean_critic_middle, square_critic_middle, mean_critic_vector, square_critic_vector):
    state_blocks = to_blocks(states)
    next_blocks = to_blocks(next_states)
    action_blocks = to_blocks(actions)
    pair_blocks = jnp.concatenate([state_blocks, action_blocks], axis=1)
    reward_blocks = rewards.reshape(N_BATCH, ROWS)
    finish_blocks = finished.reshape(N_BATCH, ROWS).astype(jnp.float32)
    row_masks = (jnp.arange(ROWS, dtype=jnp.int32)[None, :] < valid_counts[:, None]).astype(jnp.float32)
    total_count = jnp.sum(valid_counts).astype(jnp.float32)

    def fixed_values(block_item):
        state_block, next_block, pair_block = block_item
        target_min = jnp.minimum(critic_out(target_input[0], target_middle[0], target_vector[0], pair_block), critic_out(target_input[1], target_middle[1], target_vector[1], pair_block))
        value_now = jnp.einsum('h,hr->r', head_weight[:, 0], trunk_out(trunk_input[0], trunk_middle[0], trunk_vector[0], state_block), precision=HIGHEST_PRECISION) + head_vector[0]
        value_next = jnp.einsum('h,hr->r', head_weight[:, 0], trunk_out(trunk_input[0], trunk_middle[0], trunk_vector[0], next_block), precision=HIGHEST_PRECISION) + head_vector[0]
        return (target_min, value_now, value_next)
    target_min, value_now, value_next = lax.map(fixed_values, (state_blocks, next_blocks, pair_blocks))
    zero_scalar = jnp.zeros((), jnp.float32)

    def value_total(parameters):
        return block_sum(value_loss, parameters, (state_blocks, target_min, row_masks), zero_scalar)

    def actor_total(parameters):
        return block_sum(actor_loss, parameters, (state_blocks, action_blocks, target_min, value_now, row_masks), zero_scalar)

    def critic_total(parameters):
        return block_sum(critic_loss, parameters, (pair_blocks, reward_blocks, finish_blocks, value_next, row_masks), jnp.zeros((2,), jnp.float32))
    value_sum, value_back = jax.vjp(value_total, (trunk_input[0], trunk_middle[0], trunk_vector[0], head_weight, head_vector))
    value_grads = value_back(1.0 / total_count)[0]
    actor_sum, actor_back = jax.vjp(actor_total, (trunk_input[1], trunk_middle[1], trunk_vector[1], head_weight, head_vector))
    actor_grads = actor_back(1.0 / total_count)[0]
    critic_sums, critic_back = jax.vjp(critic_total, (critic_input, critic_middle, critic_vector))
    critic_grads = critic_back(jnp.full((2,), 1.0, jnp.float32) / total_count)[0]
    stacked_lamb = jax.vmap(lamb_step)
    results = [stacked_lamb(trunk_input, jnp.stack([value_grads[0], actor_grads[0]]), mean_trunk_input, square_trunk_input), stacked_lamb(trunk_middle, jnp.stack([value_grads[1], actor_grads[1]]), mean_trunk_middle, square_trunk_middle), stacked_lamb(trunk_vector, jnp.stack([value_grads[2], actor_grads[2]]), mean_trunk_vector, square_trunk_vector), lamb_step(head_weight, value_grads[3] + actor_grads[3], mean_head_weight, square_head_weight), lamb_step(head_vector, value_grads[4] + actor_grads[4], mean_head_vector, square_head_vector), stacked_lamb(critic_input, critic_grads[0], mean_critic_input, square_critic_input), stacked_lamb(critic_middle, critic_grads[1], mean_critic_middle, square_critic_middle), stacked_lamb(critic_vector, critic_grads[2], mean_critic_vector, square_critic_vector)]
    norm_rows = [jnp.broadcast_to(entry[3], (2, 2)) for entry in results]
    lamb_norms = jnp.stack(norm_rows, axis=1)
    new_target_input = (1.0 - TARGET_RATE) * target_input + TARGET_RATE * results[5][0]
    new_target_middle = (1.0 - TARGET_RATE) * target_middle + TARGET_RATE * results[6][0]
    new_target_vector = (1.0 - TARGET_RATE) * target_vector + TARGET_RATE * results[7][0]
    losses = jnp.stack([value_sum, critic_sums[0], critic_sums[1], actor_sum, total_count])
    return (results[0][0], results[1][0], results[2][0], results[3][0], results[4][0], results[5][0], results[6][0], results[7][0], results[0][1], results[1][1], results[2][1], results[3][1], results[4][1], results[5][1], results[6][1], results[7][1], results[0][2], results[1][2], results[2][2], results[3][2], results[4][2], results[5][2], results[6][2], results[7][2], new_target_input, new_target_middle, new_target_vector, lamb_norms, losses)
```

```python
import functools
import math

import jax
import jax.numpy as jnp
from jax import lax
from jax.experimental import pallas as pl
from jax.experimental.pallas import tpu as pltpu
from jax.sharding import PartitionSpec as P

STEP = 10
EXPECTILE = 0.7
DISCOUNT = 0.99
BETA_TEMP = 3.0
WEIGHT_CLIP = 100.0
DECAY_FIRST = 0.9
DECAY_SECOND = 0.999
EPSILON = 1e-06
WEIGHT_DECAY = 0.01
LEARN_RATE = 0.3
TARGET_RATE = 0.005
LOG_TWO_PI = math.log(2.0 * math.pi)

OBS = 17
ACT = 6
HID = 256
TILE = 256
ROW_TRUNK = 2 * HID
ROW_CRITIC = ROW_TRUNK + 24
ROW_VECTOR = ROW_CRITIC + 24
ROW_HEAD = ROW_VECTOR + 8
PAYLOAD = ROW_HEAD + 8
VMEM_LIMIT = 48 * 2**20

F32 = jnp.float32
BF16 = jnp.bfloat16
NN = (((1,), (0,)), ((), ()))
NT = (((1,), (1,)), ((), ()))


def split(value):
    high = value.astype(BF16)
    return high, (value - high.astype(F32)).astype(BF16)


def dot(left, right, dims=NN):
    return lax.dot_general(left, right, dims, preferred_element_type=F32)


def fold(value):
    total = value[:, :128]
    for start in range(128, value.shape[1], 128):
        total = total + value[:, start : start + 128]
    return total


def wide(value):
    return jnp.concatenate([value] * (TILE // 128), axis=1)


def left_parts(value):
    high, low = split(value)
    return jnp.concatenate([high, low, high], axis=1)


def right_parts(value):
    high, low = split(value)
    return jnp.concatenate([high, high, low], axis=0)


def right_parts_t(value):
    high, low = split(value)
    return jnp.concatenate([high, high, low], axis=1)


def column(row):
    return jnp.transpose(jnp.broadcast_to(row, (128, row.shape[1])))


def main_kernel(
    info, states, next_states, actions, rewards, finished, head_weight, head_vector,
    *refs,
):
    weights, out, scratch = refs[:18], refs[18], refs[19:]
    (
        first, second, back, bias_two, out_weight, head_pack, head_back, head_bias,
        acc_second, acc_first, acc_bias, acc_out, acc_head, acc_rows,
    ) = scratch
    group = info[0]
    start_tile, tile_count, used = info[1], info[2], info[3]

    head_columns = jnp.concatenate([head_weight[...].T, jnp.zeros((1, HID), F32)], axis=0)
    value_row = head_columns[0:1]
    action_rows = jnp.concatenate(
        [head_columns[1:7], jnp.zeros((2, HID), F32)], axis=0
    )
    row_high, row_low = split(jnp.concatenate([action_rows, jnp.zeros((8, HID), F32)], axis=0))
    head_pack[...] = jnp.concatenate([row_high, row_low, row_high], axis=1)
    mean_columns = jnp.transpose(
        jnp.concatenate([action_rows * 0.5, jnp.zeros((120, HID), F32)], axis=0)
    )[:, :16]
    mean_high, mean_low = split(mean_columns)
    head_back[...] = jnp.concatenate(
        [mean_high, mean_low, mean_high], axis=1
    )
    bias_column = jnp.transpose(
        jnp.concatenate(
            [
                jnp.concatenate([head_vector[...], jnp.zeros((1, 128 - 13), F32)], axis=1),
                jnp.zeros((127, 128), F32),
            ],
            axis=0,
        )
    )[:16, 0:1]
    head_bias[...] = jnp.broadcast_to(bias_column, (16, 128))

    def prepare(slot, is_trunk, first_ref, second_ref, vector_ref, out_row, with_back):
        rows = first_ref[0]
        vector = vector_ref[...]
        pieces = [rows]
        if is_trunk:
            pieces.append(jnp.zeros((ACT, HID), F32))
        pieces.append(vector[:, :HID])
        packed = jnp.concatenate(pieces, axis=0) * 0.5
        high = packed.astype(BF16).astype(F32)
        stack = jnp.concatenate(
            [high, high, packed - high, jnp.zeros((128 - 72, HID), F32)], axis=0
        )
        first[slot] = jnp.transpose(stack).astype(BF16)
        matrix = second_ref[0]
        second[slot] = left_parts(jnp.transpose(matrix) * 0.5)
        bias_two[slot] = column(vector[:, HID : 2 * HID] * 0.5)
        if out_row is not None:
            out_weight[slot] = column(out_row)
        if with_back:
            scale = 0.25 * out_row if out_row is not None else 0.5
            back[slot] = left_parts(matrix * scale)

    (
        own_ti, own_tm, own_tv, own_ci, own_cm, own_cv, own_gi, own_gm, own_gv,
        oth_ti, oth_tm, oth_tv, oth_ci, oth_cm, oth_cv, oth_gi, oth_gm, oth_gv,
    ) = weights
    is_value = group == 0

    class Pick:
        def __init__(self, when_value, when_actor):
            self.refs = (when_value, when_actor)

        def __getitem__(self, index):
            return jnp.where(is_value, self.refs[0][index], self.refs[1][index])

    prepare(0, True, Pick(own_ti, oth_ti), Pick(own_tm, oth_tm), Pick(own_tv, oth_tv), value_row, True)
    prepare(1, True, Pick(oth_ti, own_ti), Pick(oth_tm, own_tm), Pick(oth_tv, own_tv), None, True)
    for slot, (a, b, c) in (
        (2, (own_ci, own_cm, own_cv)),
        (3, (oth_ci, oth_cm, oth_cv)),
        (4, (own_gi, own_gm, own_gv)),
        (5, (oth_gi, oth_gm, oth_gv)),
    ):
        prepare(slot, False, a, b, c, c[...][:, 2 * HID : 3 * HID], slot < 4)
    target_bias = [ref[0:1, 3 * HID : 3 * HID + 1] for ref in (own_gv, oth_gv)]
    critic_bias = [ref[0:1, 3 * HID : 3 * HID + 1] for ref in (own_cv, oth_cv)]
    value_bias = head_vector[0:1, 0:1]

    acc_second[...] = jnp.zeros_like(acc_second)
    acc_first[...] = jnp.zeros_like(acc_first)
    acc_bias[...] = jnp.zeros_like(acc_bias)
    acc_out[...] = jnp.zeros_like(acc_out)
    acc_head[...] = jnp.zeros_like(acc_head)
    acc_rows[...] = jnp.zeros_like(acc_rows)

    def tile(index, carry):
        at = pl.ds(pl.multiple_of(index * TILE, TILE), TILE)
        states_t = states[:, at]
        next_t = next_states[:, at]
        actions_t = actions[:, at]
        ones = jnp.ones((1, TILE), F32)

        def line(ref):
            parts = TILE // 128
            return jnp.concatenate(
                [ref[pl.ds(index * parts + part, 1), :] for part in range(parts)], axis=1
            )

        reward = line(rewards)
        done = line(finished).astype(F32)
        place = index * TILE + lax.broadcasted_iota(jnp.int32, (1, TILE), 1)
        valid = (place < used).astype(F32)

        def pack(rows):
            full = jnp.concatenate([rows, actions_t, ones], axis=0)
            high = full.astype(BF16).astype(F32)
            low = full - high
            return jnp.concatenate(
                [high, low, high, jnp.zeros((128 - 72, TILE), F32)], axis=0
            ).astype(BF16)

        pairs = pack(states_t)
        pairs_next = pack(next_t)

        def layer(half):
            t = jnp.tanh(half)
            u = t + 1.0
            a = half * u
            return a, t, u

        def forward(slot, inputs, keep):
            a_one, t, u = layer(dot(first[slot], inputs))
            slope_one = u + a_one * (1.0 - t) if keep else None
            parts = split(a_one)
            z = dot(second[slot], jnp.concatenate([parts[0], parts[0], parts[1]], axis=0))
            a_two, t, u = layer(z + wide(bias_two[slot]))
            slope_two = u + a_two * (1.0 - t) if keep else None
            return parts, slope_one, a_two, slope_two

        def weighted(slot, hidden):
            return jnp.sum(hidden * wide(out_weight[slot]), axis=0, keepdims=True)

        def backward(slot, parts, slope_one, delta_two):
            acc_bias[slot] += fold(delta_two)
            high, low = split(delta_two)
            acc_second[slot] += dot(
                jnp.concatenate([parts[0], parts[1], parts[0]], axis=1),
                jnp.concatenate([high, high, low], axis=1),
                NT,
            )
            delta_one = dot(back[slot], jnp.concatenate([high, high, low], axis=0)) * slope_one
            high, low = split(delta_one)
            acc_first[slot] += dot(
                jnp.concatenate([high, low], axis=1), jnp.concatenate([pairs, pairs], axis=1), NT
            )

        _, _, hidden, _ = forward(0, pairs_next, False)
        value_next = weighted(0, hidden) + value_bias
        goal = reward + DISCOUNT * (1.0 - done) * value_next
        targets = []
        for member in range(2):
            _, _, hidden, _ = forward(4 + member, pairs, False)
            targets.append(weighted(4 + member, hidden) + target_bias[member])
        target_min = jnp.minimum(targets[0], targets[1])
        critic_sums, critic_grads = [], []
        for member in range(2):
            slot = 2 + member
            parts, slope_one, hidden, slope_two = forward(slot, pairs, True)
            error = (weighted(slot, hidden) + critic_bias[member] - goal) * valid
            grad = 2.0 * error
            critic_sums.append(error * error)
            critic_grads.append(grad)
            acc_out[slot] += fold(hidden * grad)
            backward(slot, parts, slope_one, slope_two * grad)
        parts, slope_one, hidden, slope_two = forward(0, pairs, True)
        value_now = weighted(0, hidden) + value_bias
        gap = target_min - value_now
        expect = jnp.where(gap < 0.0, 1.0 - EXPECTILE, EXPECTILE) * valid
        grad = -2.0 * expect * gap
        value_rows = [grad, expect * gap * gap]
        acc_out[0] += fold(hidden * grad)
        backward(0, parts, slope_one, slope_two * grad)
        parts, slope_one, hidden, slope_two = forward(1, pairs, True)
        hidden_high, hidden_low = split(hidden)
        head = dot(head_pack[...], jnp.concatenate([hidden_high, hidden_high, hidden_low], axis=0))[:8]
        bias = wide(head_bias[...])
        mean = jnp.tanh(head[:6] + bias[1:7])
        log_std = bias[7:13]
        inverse = jnp.exp(-log_std)
        scaled = (actions_t - mean) * inverse
        log_prob = jnp.sum(
            -0.5 * scaled * scaled - log_std - 0.5 * LOG_TWO_PI, axis=0, keepdims=True
        )
        weight = jnp.minimum(jnp.exp(BETA_TEMP * gap), WEIGHT_CLIP) * valid
        grad_mean = -weight * scaled * inverse * (1.0 - mean * mean)
        grad_std = -weight * (scaled * scaled - 1.0)
        grads = jnp.concatenate([grad_mean, jnp.zeros((10, TILE), F32)], axis=0)
        grads_high, grads_low = split(grads)
        acc_head[...] += dot(
            jnp.concatenate([hidden_high, hidden_low, hidden_high], axis=1),
            jnp.concatenate([grads_high, grads_high, grads_low], axis=1),
            NT,
        )
        up = dot(head_back[...], jnp.concatenate([grads_high, grads_high, grads_low], axis=0))
        backward(1, parts, slope_one, up * slope_two)
        rows = jnp.concatenate(
            [value_rows[0], grad_mean, grad_std, value_rows[1]]
            + critic_sums
            + [-weight * log_prob, valid]
            + critic_grads
            + [jnp.zeros((4, TILE), F32)],
            axis=0,
        )
        acc_rows[...] += fold(rows)
        return carry

    lax.fori_loop(0, tile_count, lambda i, c: tile(start_tile + 2 * i, c), 0)


    def store(which, row, value):
        count = value.shape[0]
        out[which, pl.ds(row, count), :] = value[:, :128]
        out[which, pl.ds(PAYLOAD + row, count), :] = value[:, 128:]

    def first_grad(slot):
        total = acc_first[slot]
        return jnp.transpose(total + pltpu.roll(total, 104, 1))[:24]

    def lanes(value):
        return jnp.sum(jnp.transpose(value), axis=0, keepdims=True)

    zero_row = jnp.zeros((1, HID), F32)
    row_sums = jnp.sum(
        jnp.transpose(jnp.concatenate([acc_rows[...], jnp.zeros((104, 128), F32)], axis=0)),
        axis=0,
        keepdims=True,
    )
    lane = lax.broadcasted_iota(jnp.int32, (1, 128), 1)
    swapped = jnp.where(
        lane == 14,
        pltpu.roll(row_sums, 127, 1),
        jnp.where(lane == 15, pltpu.roll(row_sums, 1, 1), row_sums),
    )
    shared_row = jnp.where(is_value, row_sums, swapped)
    head_actions = jnp.transpose(
        jnp.concatenate([acc_head[...], jnp.zeros((HID, 112), F32)], axis=1)
    )[:6]
    head_rows = jnp.concatenate([lanes(acc_out[0]), head_actions, zero_row], axis=0)
    out_rows = (value_row * 0.5, None, own_cv[...][:, 2 * HID : 3 * HID] * 0.5, oth_cv[...][:, 2 * HID : 3 * HID] * 0.5)

    def second_grad(slot):
        matrix, bias = acc_second[slot], lanes(acc_bias[slot])
        scale = out_rows[slot]
        return (matrix, bias) if scale is None else (matrix * scale, bias * scale)

    for which in range(2):
        trunk_at = jnp.where(is_value, which, 1 - which)
        trunk_second, trunk_bias = second_grad(which)
        critic_second, critic_bias_two = second_grad(2 + which)
        store(trunk_at, 0, trunk_second)
        store(which, HID, critic_second)
        store(trunk_at, ROW_TRUNK, first_grad(which))
        store(which, ROW_CRITIC, first_grad(2 + which))
        store(trunk_at, ROW_VECTOR, trunk_bias)
        bias_grad = pltpu.roll(row_sums, 128 - 18 - which, 1)
        last = jnp.concatenate([shared_row, jnp.where(lane == 0, bias_grad, 0.0)], axis=1)
        store(
            which,
            ROW_VECTOR + 1,
            jnp.concatenate(
                [critic_bias_two, lanes(acc_out[2 + which]), last] + [zero_row] * 4, axis=0
            ),
        )
        store(which, ROW_HEAD, head_rows)


def run_main(info, data, heads, weights):
    vmem = pl.BlockSpec(memory_space=pltpu.VMEM)
    smem = pl.BlockSpec(memory_space=pltpu.SMEM)
    return pl.pallas_call(
        main_kernel,
        out_shape=jax.ShapeDtypeStruct((2, 2 * PAYLOAD, 128), F32),
        in_specs=[smem] + [vmem] * (len(data) + len(heads) + len(weights)),
        out_specs=vmem,
        scratch_shapes=[
            pltpu.VMEM((6, HID, 128), BF16),
            pltpu.VMEM((6, HID, 3 * HID), BF16),
            pltpu.VMEM((4, HID, 3 * HID), BF16),
            pltpu.VMEM((6, HID, 128), F32),
            pltpu.VMEM((6, HID, 128), F32),
            pltpu.VMEM((16, 3 * HID), BF16),
            pltpu.VMEM((HID, 48), BF16),
            pltpu.VMEM((16, 128), F32),
            pltpu.VMEM((4, HID, HID), F32),
            pltpu.VMEM((4, HID, 128), F32),
            pltpu.VMEM((4, HID, 128), F32),
            pltpu.VMEM((4, HID, 128), F32),
            pltpu.VMEM((HID, 16), F32),
            pltpu.VMEM((24, 128), F32),
        ],
        compiler_params=pltpu.CompilerParams(vmem_limit_bytes=VMEM_LIMIT),
        name="gradients",
    )(info, *data, *heads, *weights)


def lamb_kernel(*refs):
    payload = refs[0]
    params = {name: refs[1 + 3 * i : 4 + 3 * i] for i, name in enumerate(NAMES)}
    targets = refs[25:28]
    outs = refs[28:]

    def rows(start, count):
        return jnp.concatenate(
            [payload[start : start + count, :], payload[PAYLOAD + start : PAYLOAD + start + count, :]],
            axis=1,
        )

    trunk_first = rows(ROW_TRUNK, 24)
    critic_first = rows(ROW_CRITIC, 24)
    vectors = rows(ROW_VECTOR, 8)
    head = rows(ROW_HEAD, 8)
    shared = vectors[3:4, :128]
    after = 1.0 / shared[:, 17:18]
    gradients = (
        trunk_first[:OBS],
        rows(0, HID),
        jnp.concatenate([trunk_first[23:24], vectors[0:1]], axis=1),
        jnp.transpose(jnp.concatenate([head, jnp.zeros((120, HID), F32)], axis=0))[:, :7],
        shared[:, :13],
        critic_first[: OBS + ACT],
        rows(HID, HID),
        jnp.concatenate(
            [critic_first[23:24], vectors[1:2], vectors[2:3], vectors[3:4, 128:129]], axis=1
        ),
    )
    norms = []
    updated = []
    for i, name in enumerate(NAMES):
        stacked = len(params[name][0].shape) == 3
        weight, mean_old, square_old = (
            (ref[0] if stacked else ref[...]) for ref in params[name]
        )
        gradient = gradients[i] * after
        mean_new = DECAY_FIRST * mean_old + (1.0 - DECAY_FIRST) * gradient
        square_new = DECAY_SECOND * square_old + (1.0 - DECAY_SECOND) * gradient * gradient
        mean_hat = mean_new / (1.0 - DECAY_FIRST**STEP)
        square_hat = square_new / (1.0 - DECAY_SECOND**STEP)
        update = mean_hat / (jnp.sqrt(square_hat) + EPSILON) + WEIGHT_DECAY * weight
        total = lambda value: jnp.sum(jnp.sum(value * value, axis=0, keepdims=True), axis=1, keepdims=True)
        weight_norm, update_norm = jnp.sqrt(total(weight)), jnp.sqrt(total(update))
        new = weight - LEARN_RATE * (weight_norm / update_norm) * update
        for at, value in ((i, new), (8 + i, mean_new), (16 + i, square_new)):
            if stacked:
                outs[at][0] = value
            else:
                outs[at][...] = value
        norms.append(jnp.concatenate([weight_norm, update_norm], axis=1))
        updated.append(new)
    for i, ref in enumerate(targets):
        if len(ref.shape) == 3:
            outs[24 + i][0] = (1.0 - TARGET_RATE) * ref[0] + TARGET_RATE * updated[5 + i]
        else:
            outs[24 + i][...] = (1.0 - TARGET_RATE) * ref[...] + TARGET_RATE * updated[5 + i]
    outs[27][0] = jnp.concatenate(norms, axis=0)
    outs[28][...] = pltpu.roll(shared, 128 - 13, 1)[:, :5]


NAMES = (
    "trunk_input", "trunk_middle", "trunk_vector", "head_weight", "head_vector",
    "critic_input", "critic_middle", "critic_vector",
)


def run_lamb(payload, params, targets):
    vmem = pl.BlockSpec(memory_space=pltpu.VMEM)
    flat = [array for triple in params for array in triple]
    shapes = [jax.ShapeDtypeStruct(triple[0].shape, F32) for triple in params]
    outs = shapes * 3 + [jax.ShapeDtypeStruct(t.shape, F32) for t in targets]
    outs += [jax.ShapeDtypeStruct((1, 8, 2), F32), jax.ShapeDtypeStruct((1, 5), F32)]
    return pl.pallas_call(
        lamb_kernel,
        out_shape=outs,
        in_specs=[vmem] * (1 + len(flat) + len(targets)),
        out_specs=[vmem] * len(outs),
        compiler_params=pltpu.CompilerParams(vmem_limit_bytes=VMEM_LIMIT),
        name="update",
    )(payload, *flat, *targets)


def across(value):
    size = lax.axis_size("net")
    return lax.ppermute(value, "net", [(i, size - 1 - i) for i in range(size)])


def shards(
    states, next_states, actions, rewards, finished, valid_counts,
    trunk_input, trunk_middle, trunk_vector, head_weight, head_vector,
    critic_input, critic_middle, critic_vector,
    target_input, target_middle, target_vector,
    mean_trunk_input, square_trunk_input, mean_trunk_middle, square_trunk_middle,
    mean_trunk_vector, square_trunk_vector, mean_head_weight, square_head_weight,
    mean_head_vector, square_head_vector, mean_critic_input, square_critic_input,
    mean_critic_middle, square_critic_middle, mean_critic_vector, square_critic_vector,
):
    group = lax.axis_index("net").astype(jnp.int32)
    row_total = states.shape[1]
    used = valid_counts[0]
    tiles = (used + TILE - 1) // TILE
    info = jnp.stack([group, group, (tiles - group + 1) // 2, used])
    own = (
        trunk_input, trunk_middle, trunk_vector, critic_input, critic_middle, critic_vector,
        target_input, target_middle, target_vector,
    )
    other = tuple(across(array) for array in own)
    payloads = run_main(
        info,
        (
            states, next_states, actions,
            rewards.reshape(row_total // 128, 128), finished.reshape(row_total // 128, 128),
        ),
        (head_weight, head_vector.reshape(1, 13)),
        own + other,
    )
    total = payloads[0] + across(payloads[1])
    parts = lax.axis_size("batch")
    total = total.reshape(parts, 2 * PAYLOAD // parts, 128)
    pieces = lax.all_to_all(total, "batch", 0, 0, tiled=True)
    mine = jnp.sum(pieces, axis=0, keepdims=True)
    full = lax.all_to_all(
        jnp.broadcast_to(mine, total.shape), "batch", 0, 0, tiled=True
    ).reshape(2 * PAYLOAD, 128)
    results = run_lamb(
        full,
        (
            (trunk_input, mean_trunk_input, square_trunk_input),
            (trunk_middle, mean_trunk_middle, square_trunk_middle),
            (trunk_vector, mean_trunk_vector, square_trunk_vector),
            (head_weight, mean_head_weight, square_head_weight),
            (head_vector.reshape(1, 13), mean_head_vector.reshape(1, 13), square_head_vector.reshape(1, 13)),
            (critic_input, mean_critic_input, square_critic_input),
            (critic_middle, mean_critic_middle, square_critic_middle),
            (critic_vector, mean_critic_vector, square_critic_vector),
        ),
        (target_input, target_middle, target_vector),
    )
    results = list(results)
    for at in (4, 12, 20):
        results[at] = results[at].reshape(13)
    results[28] = results[28].reshape(5)
    return tuple(results)


def solution(mesh):
    rows, matrix, vector, none = P(None, "batch"), P("net", None, None), P("net", None), P()
    line = P("batch")
    params = (matrix, matrix, vector, none, none, matrix, matrix, vector)
    moments = tuple(spec for entry in params for spec in (entry, entry))
    target = (matrix, matrix, vector)
    return jax.shard_map(
        shards,
        mesh=mesh,
        in_specs=(rows, rows, rows, line, line, line) + params + target + moments,
        out_specs=params * 3 + target + (matrix, none),
        check_vma=False,
    )
```

```python
import functools
import math

import jax
import jax.numpy as jnp
from jax import lax
from jax.experimental import pallas as pl
from jax.experimental.pallas import tpu as pltpu
from jax.sharding import PartitionSpec as P

STEP = 10
EXPECTILE = 0.7
DISCOUNT = 0.99
BETA_TEMP = 3.0
WEIGHT_CLIP = 100.0
DECAY_FIRST = 0.9
DECAY_SECOND = 0.999
EPSILON = 1e-06
WEIGHT_DECAY = 0.01
LEARN_RATE = 0.3
TARGET_RATE = 0.005
LOG_TWO_PI = math.log(2.0 * math.pi)

OBS = 17
ACT = 6
HID = 256
TILE = 256
WIDTH = 7
ROW_TRUNK = 2 * HID
ROW_CRITIC = ROW_TRUNK + 24
ROW_VECTOR = ROW_CRITIC + 24
ROW_HEAD = ROW_VECTOR + 8
PAYLOAD = ROW_HEAD + 8
VMEM_LIMIT = 62 * 2**20

F32 = jnp.float32
BF16 = jnp.bfloat16
NN = (((1,), (0,)), ((), ()))
NT = (((1,), (1,)), ((), ()))


def split(value):
    high = value.astype(BF16)
    return high, (value - high.astype(F32)).astype(BF16)


def dot(left, right, dims=NN):
    return lax.dot_general(left, right, dims, preferred_element_type=F32)


def fold(value):
    total = value[:, :128]
    for start in range(128, value.shape[1], 128):
        total = total + value[:, start : start + 128]
    return total


def wide(value):
    return jnp.concatenate([value] * (TILE // 128), axis=1)


def left_parts(value):
    high, low = split(value)
    return jnp.concatenate([high, low, high], axis=1)


def right_parts(value):
    high, low = split(value)
    return jnp.concatenate([high, high, low], axis=0)


def right_parts_t(value):
    high, low = split(value)
    return jnp.concatenate([high, high, low], axis=1)


def column(row):
    return jnp.transpose(jnp.broadcast_to(row, (128, row.shape[1])))


def main_kernel(
    info, states, next_states, actions, rewards, finished, head_weight, head_vector,
    *refs,
):
    weights, (out_own, out_other), scratch = refs[:18], refs[18:20], refs[20:]
    (
        first, second, back, bias_two, out_weight, head_pack, head_back, head_bias,
        acc_second, acc_first, acc_bias, acc_out, acc_head, acc_rows,
    ) = scratch
    group = info[0]
    start_tile, tile_count, used = info[1], info[2], info[3]

    head_columns = jnp.concatenate([head_weight[...], jnp.zeros((1, HID), F32)], axis=0)
    value_row = head_columns[0:1]
    action_rows = jnp.concatenate(
        [head_columns[1:7], jnp.zeros((2, HID), F32)], axis=0
    )
    row_high, row_low = split(jnp.concatenate([action_rows, jnp.zeros((8, HID), F32)], axis=0))
    head_pack[...] = jnp.concatenate([row_high, row_low, row_high], axis=1)
    mean_columns = jnp.transpose(
        jnp.concatenate([action_rows * 0.5, jnp.zeros((120, HID), F32)], axis=0)
    )[:, :16]
    mean_high, mean_low = split(mean_columns)
    head_back[...] = jnp.concatenate(
        [mean_high, mean_low, mean_high], axis=1
    )
    bias_column = jnp.transpose(
        jnp.concatenate(
            [
                jnp.concatenate([head_vector[...], jnp.zeros((1, 128 - 13), F32)], axis=1),
                jnp.zeros((127, 128), F32),
            ],
            axis=0,
        )
    )[:16, 0:1]
    head_bias[...] = jnp.broadcast_to(bias_column, (16, 128))

    def prepare(slot, is_trunk, first_ref, second_ref, vector_ref, out_row, with_back):
        rows = first_ref[:, 0, :]
        vector = vector_ref[...]
        pieces = [rows]
        if is_trunk:
            pieces.append(jnp.zeros((ACT, HID), F32))
        pieces.append(vector[:, :HID])
        packed = jnp.concatenate(pieces, axis=0) * 0.5
        high = packed.astype(BF16).astype(F32)
        stack = jnp.concatenate(
            [high, high, packed - high, jnp.zeros((128 - 72, HID), F32)], axis=0
        )
        first[slot] = jnp.transpose(stack).astype(BF16)
        matrix = second_ref[0]
        second[slot] = left_parts(jnp.transpose(matrix) * 0.5)
        bias_two[slot] = column(vector[:, HID : 2 * HID] * 0.5)
        if out_row is not None:
            out_weight[slot] = column(out_row)
        if with_back:
            scale = 0.25 * out_row if out_row is not None else 0.5
            back[slot] = left_parts(matrix * scale)

    (
        own_ti, own_tm, own_tv, own_ci, own_cm, own_cv, own_gi, own_gm, own_gv,
        oth_ti, oth_tm, oth_tv, oth_ci, oth_cm, oth_cv, oth_gi, oth_gm, oth_gv,
    ) = weights
    is_value = group == 0

    class Pick:
        def __init__(self, when_value, when_actor):
            self.refs = (when_value, when_actor)

        def __getitem__(self, index):
            return jnp.where(is_value, self.refs[0][index], self.refs[1][index])

    prepare(0, True, Pick(own_ti, oth_ti), Pick(own_tm, oth_tm), Pick(own_tv, oth_tv), value_row, True)
    prepare(1, True, Pick(oth_ti, own_ti), Pick(oth_tm, own_tm), Pick(oth_tv, own_tv), None, True)
    for slot, (a, b, c) in (
        (2, (own_ci, own_cm, own_cv)),
        (3, (oth_ci, oth_cm, oth_cv)),
        (4, (own_gi, own_gm, own_gv)),
        (5, (oth_gi, oth_gm, oth_gv)),
    ):
        prepare(slot, False, a, b, c, c[...][:, 2 * HID : 3 * HID], slot < 4)
    target_bias = [ref[0:1, 3 * HID : 3 * HID + 1] for ref in (own_gv, oth_gv)]
    critic_bias = [ref[0:1, 3 * HID : 3 * HID + 1] for ref in (own_cv, oth_cv)]
    value_bias = head_vector[0:1, 0:1]

    acc_second[...] = jnp.zeros_like(acc_second)
    acc_first[...] = jnp.zeros_like(acc_first)
    acc_bias[...] = jnp.zeros_like(acc_bias)
    acc_out[...] = jnp.zeros_like(acc_out)
    acc_head[...] = jnp.zeros_like(acc_head)
    acc_rows[...] = jnp.zeros_like(acc_rows)

    def tile(index, carry):
        at = pl.ds(pl.multiple_of(index * TILE, TILE), TILE)
        states_t = states[:, at]
        next_t = next_states[:, at]
        actions_t = actions[:, at]
        ones = jnp.ones((1, TILE), F32)

        def line(ref):
            parts = TILE // 128
            return jnp.concatenate(
                [ref[pl.ds(index * parts + part, 1), :] for part in range(parts)], axis=1
            )

        reward = line(rewards)
        done = line(finished).astype(F32)
        place = index * TILE + lax.broadcasted_iota(jnp.int32, (1, TILE), 1)
        valid = (place < used).astype(F32)

        def pack(rows):
            full = jnp.concatenate([rows, actions_t, ones], axis=0)
            high = full.astype(BF16).astype(F32)
            low = full - high
            return jnp.concatenate(
                [high, low, high, jnp.zeros((128 - 72, TILE), F32)], axis=0
            ).astype(BF16)

        pairs = pack(states_t)
        pairs_next = pack(next_t)

        def layer(half):
            t = jnp.tanh(half)
            u = t + 1.0
            a = half * u
            return a, t, u

        def forward(slot, inputs, keep):
            half = dot(first[slot], inputs)
            yield
            a_one, t, u = layer(half)
            slope_one = u + a_one * (1.0 - t) if keep else None
            parts = split(a_one)
            yield
            z = dot(second[slot], jnp.concatenate([parts[0], parts[0], parts[1]], axis=0))
            yield
            a_two, t, u = layer(z + wide(bias_two[slot]))
            slope_two = u + a_two * (1.0 - t) if keep else None
            return parts, slope_one, a_two, slope_two

        def weighted(slot, hidden):
            return jnp.sum(hidden * wide(out_weight[slot]), axis=0, keepdims=True)

        def backward(slot, parts, slope_one, delta_two):
            acc_bias[slot] += fold(delta_two)
            high, low = split(delta_two)
            yield
            delta_one = dot(back[slot], jnp.concatenate([high, high, low], axis=0))
            acc_second[slot] += dot(
                jnp.concatenate([parts[0], parts[1], parts[0]], axis=1),
                jnp.concatenate([high, high, low], axis=1),
                NT,
            )
            yield
            high, low = split(delta_one * slope_one)
            yield
            acc_first[slot] += dot(
                jnp.concatenate([high, low], axis=1), jnp.concatenate([pairs, pairs], axis=1), NT
            )

        known = {}

        def next_chain():
            _, _, hidden, _ = yield from forward(0, pairs_next, False)
            value_next = weighted(0, hidden) + value_bias
            known["goal"] = reward + DISCOUNT * (1.0 - done) * value_next

        def target_chain(member):
            _, _, hidden, _ = yield from forward(4 + member, pairs, False)
            known["target", member] = weighted(4 + member, hidden) + target_bias[member]

        def critic_chain(member):
            slot = 2 + member
            parts, slope_one, hidden, slope_two = yield from forward(slot, pairs, True)
            error = (weighted(slot, hidden) + critic_bias[member] - known["goal"]) * valid
            grad = 2.0 * error
            known["critic", member] = (error * error, grad)
            acc_out[slot] += fold(hidden * grad)
            yield from backward(slot, parts, slope_one, slope_two * grad)

        def value_chain():
            parts, slope_one, hidden, slope_two = yield from forward(0, pairs, True)
            target_min = jnp.minimum(known["target", 0], known["target", 1])
            gap = target_min - (weighted(0, hidden) + value_bias)
            expect = jnp.where(gap < 0.0, 1.0 - EXPECTILE, EXPECTILE) * valid
            grad = -2.0 * expect * gap
            known["gap"] = gap
            known["value"] = (grad, expect * gap * gap)
            acc_out[0] += fold(hidden * grad)
            yield from backward(0, parts, slope_one, slope_two * grad)

        def actor_chain():
            parts, slope_one, hidden, slope_two = yield from forward(1, pairs, True)
            hidden_high, hidden_low = split(hidden)
            head = dot(
                head_pack[...], jnp.concatenate([hidden_high, hidden_high, hidden_low], axis=0)
            )[:8]
            yield
            bias = wide(head_bias[...])
            mean = jnp.tanh(head[:6] + bias[1:7])
            log_std = bias[7:13]
            inverse = jnp.exp(-log_std)
            scaled = (actions_t - mean) * inverse
            log_prob = jnp.sum(
                -0.5 * scaled * scaled - log_std - 0.5 * LOG_TWO_PI, axis=0, keepdims=True
            )
            weight = jnp.minimum(jnp.exp(BETA_TEMP * known["gap"]), WEIGHT_CLIP) * valid
            grad_mean = -weight * scaled * inverse * (1.0 - mean * mean)
            grad_std = -weight * (scaled * scaled - 1.0)
            known["actor"] = (grad_mean, grad_std, -weight * log_prob)
            grads = jnp.concatenate([grad_mean, jnp.zeros((10, TILE), F32)], axis=0)
            grads_high, grads_low = split(grads)
            acc_head[...] += dot(
                jnp.concatenate([hidden_high, hidden_low, hidden_high], axis=1),
                jnp.concatenate([grads_high, grads_high, grads_low], axis=1),
                NT,
            )
            up = dot(
                head_back[...], jnp.concatenate([grads_high, grads_high, grads_low], axis=0)
            )
            yield
            yield from backward(1, parts, slope_one, up * slope_two)

        waiting = [
            next_chain(), target_chain(0), target_chain(1), critic_chain(0), value_chain(),
            actor_chain(), critic_chain(1),
        ]
        active = []
        while waiting or active:
            while waiting and len(active) < WIDTH:
                active.append(waiting.pop(0))
            for chain in list(active):
                try:
                    next(chain)
                except StopIteration:
                    active.remove(chain)

        rows = jnp.concatenate(
            [known["value"][0], known["actor"][0], known["actor"][1], known["value"][1]]
            + [known["critic", 0][0], known["critic", 1][0], known["actor"][2], valid]
            + [known["critic", 0][1], known["critic", 1][1]]
            + [jnp.zeros((4, TILE), F32)],
            axis=0,
        )
        acc_rows[...] += fold(rows)
        return carry

    lax.fori_loop(0, tile_count, lambda i, c: tile(start_tile + 2 * i, c), 0)


    def store(out, row, value):
        count = value.shape[0]
        out[row : row + count, :] = value[:, :128]
        out[PAYLOAD + row : PAYLOAD + row + count, :] = value[:, 128:]

    def first_grad(slot):
        total = acc_first[slot]
        return jnp.transpose(total + pltpu.roll(total, 104, 1))[:24]

    def lanes(value):
        return jnp.sum(jnp.transpose(value), axis=0, keepdims=True)

    zero_row = jnp.zeros((1, HID), F32)
    row_sums = jnp.sum(
        jnp.transpose(jnp.concatenate([acc_rows[...], jnp.zeros((104, 128), F32)], axis=0)),
        axis=0,
        keepdims=True,
    )
    lane = lax.broadcasted_iota(jnp.int32, (1, 128), 1)
    swapped = jnp.where(
        lane == 14,
        pltpu.roll(row_sums, 127, 1),
        jnp.where(lane == 15, pltpu.roll(row_sums, 1, 1), row_sums),
    )
    shared_row = jnp.where(is_value, row_sums, swapped)
    head_actions = jnp.transpose(
        jnp.concatenate([acc_head[...], jnp.zeros((HID, 112), F32)], axis=1)
    )[:6]
    head_rows = jnp.concatenate([lanes(acc_out[0]), head_actions, zero_row], axis=0)
    out_rows = (value_row * 0.5, None, own_cv[...][:, 2 * HID : 3 * HID] * 0.5, oth_cv[...][:, 2 * HID : 3 * HID] * 0.5)

    def second_grad(slot):
        matrix, bias = acc_second[slot], lanes(acc_bias[slot])
        scale = out_rows[slot]
        return (matrix, bias) if scale is None else (matrix * scale, bias * scale)

    trunk = [second_grad(slot) + (first_grad(slot),) for slot in range(2)]
    for which, out in enumerate((out_own, out_other)):
        trunk_second, trunk_bias, trunk_first = (
            jnp.where(is_value, trunk[which][k], trunk[1 - which][k]) for k in range(3)
        )
        critic_second, critic_bias_two = second_grad(2 + which)
        store(out, 0, trunk_second)
        store(out, HID, critic_second)
        store(out, ROW_TRUNK, trunk_first)
        store(out, ROW_CRITIC, first_grad(2 + which))
        bias_grad = pltpu.roll(row_sums, 128 - 18 - which, 1)
        last = jnp.concatenate([shared_row, jnp.where(lane == 0, bias_grad, 0.0)], axis=1)
        store(
            out,
            ROW_VECTOR,
            jnp.concatenate(
                [trunk_bias, critic_bias_two, lanes(acc_out[2 + which]), last] + [zero_row] * 4,
                axis=0,
            ),
        )
        store(out, ROW_HEAD, head_rows)


def run_main(info, data, heads, weights):
    vmem = pl.BlockSpec(memory_space=pltpu.VMEM)
    smem = pl.BlockSpec(memory_space=pltpu.SMEM)
    return pl.pallas_call(
        main_kernel,
        out_shape=[jax.ShapeDtypeStruct((2 * PAYLOAD, 128), F32)] * 2,
        in_specs=[smem] + [vmem] * (len(data) + len(heads) + len(weights)),
        out_specs=[vmem, vmem],
        scratch_shapes=[
            pltpu.VMEM((6, HID, 128), BF16),
            pltpu.VMEM((6, HID, 3 * HID), BF16),
            pltpu.VMEM((4, HID, 3 * HID), BF16),
            pltpu.VMEM((6, HID, 128), F32),
            pltpu.VMEM((6, HID, 128), F32),
            pltpu.VMEM((16, 3 * HID), BF16),
            pltpu.VMEM((HID, 48), BF16),
            pltpu.VMEM((16, 128), F32),
            pltpu.VMEM((4, HID, HID), F32),
            pltpu.VMEM((4, HID, 128), F32),
            pltpu.VMEM((4, HID, 128), F32),
            pltpu.VMEM((4, HID, 128), F32),
            pltpu.VMEM((HID, 16), F32),
            pltpu.VMEM((24, 128), F32),
        ],
        compiler_params=pltpu.CompilerParams(vmem_limit_bytes=VMEM_LIMIT),
        name="gradients",
    )(info, *data, *heads, *weights)


def read(ref):
    if len(ref.shape) == 2:
        return ref[...]
    return ref[:, 0, :] if ref.shape[1] == 1 else ref[0]


def write(ref, value):
    if len(ref.shape) == 2:
        ref[...] = value
    elif ref.shape[1] == 1:
        ref[:, 0, :] = value
    else:
        ref[0] = value


def lamb_kernel(*refs):
    payload = refs[0]
    params = {name: refs[1 + 3 * i : 4 + 3 * i] for i, name in enumerate(NAMES)}
    targets = refs[25:28]
    outs = refs[28:]

    def rows(start, count):
        return jnp.concatenate(
            [payload[start : start + count, :], payload[PAYLOAD + start : PAYLOAD + start + count, :]],
            axis=1,
        )

    trunk_first = rows(ROW_TRUNK, 24)
    critic_first = rows(ROW_CRITIC, 24)
    vectors = rows(ROW_VECTOR, 8)
    head = rows(ROW_HEAD, 8)
    shared = vectors[3:4, :128]
    after = 1.0 / shared[:, 17:18]
    gradients = (
        trunk_first[:OBS],
        rows(0, HID),
        jnp.concatenate([trunk_first[23:24], vectors[0:1]], axis=1),
        head[:7],
        shared[:, :13],
        critic_first[: OBS + ACT],
        rows(HID, HID),
        jnp.concatenate(
            [critic_first[23:24], vectors[1:2], vectors[2:3], vectors[3:4, 128:129]], axis=1
        ),
    )
    norms = []
    updated = []
    for i, name in enumerate(NAMES):
        weight, mean_old, square_old = (read(ref) for ref in params[name])
        gradient = gradients[i] * after
        mean_new = DECAY_FIRST * mean_old + (1.0 - DECAY_FIRST) * gradient
        square_new = DECAY_SECOND * square_old + (1.0 - DECAY_SECOND) * gradient * gradient
        mean_hat = mean_new / (1.0 - DECAY_FIRST**STEP)
        square_hat = square_new / (1.0 - DECAY_SECOND**STEP)
        update = mean_hat / (jnp.sqrt(square_hat) + EPSILON) + WEIGHT_DECAY * weight
        total = lambda value: jnp.sum(jnp.sum(value * value, axis=0, keepdims=True), axis=1, keepdims=True)
        weight_norm, update_norm = jnp.sqrt(total(weight)), jnp.sqrt(total(update))
        new = weight - LEARN_RATE * (weight_norm / update_norm) * update
        for at, value in ((i, new), (8 + i, mean_new), (16 + i, square_new)):
            write(outs[at], value)
        norms.append((weight_norm, update_norm))
        updated.append(new)
    for i, ref in enumerate(targets):
        write(outs[24 + i], (1.0 - TARGET_RATE) * read(ref) + TARGET_RATE * updated[5 + i])
    lane = lax.broadcasted_iota(jnp.int32, (1, 8), 1)
    for row in range(2):
        line = jnp.zeros((1, 8), F32)
        for i, pair in enumerate(norms):
            line = jnp.where(lane == i, pair[row], line)
        outs[27][0, row : row + 1, :] = line
    outs[28][...] = pltpu.roll(shared, 128 - 13, 1)[:, :5]


NAMES = (
    "trunk_input", "trunk_middle", "trunk_vector", "head_weight", "head_vector",
    "critic_input", "critic_middle", "critic_vector",
)


def run_lamb(payload, params, targets):
    vmem = pl.BlockSpec(memory_space=pltpu.VMEM)
    flat = [array for triple in params for array in triple]
    shapes = [jax.ShapeDtypeStruct(triple[0].shape, F32) for triple in params]
    outs = shapes * 3 + [jax.ShapeDtypeStruct(t.shape, F32) for t in targets]
    outs += [jax.ShapeDtypeStruct((1, 2, 8), F32), jax.ShapeDtypeStruct((1, 5), F32)]
    return pl.pallas_call(
        lamb_kernel,
        out_shape=outs,
        in_specs=[vmem] * (1 + len(flat) + len(targets)),
        out_specs=[vmem] * len(outs),
        compiler_params=pltpu.CompilerParams(vmem_limit_bytes=VMEM_LIMIT),
        name="update",
    )(payload, *flat, *targets)


def across(value):
    size = lax.axis_size("net")
    return lax.ppermute(value, "net", [(i, size - 1 - i) for i in range(size)])


def summed(value):
    size = lax.axis_size("batch")
    if size % 2:
        return lax.psum(value, "batch")
    half = size // 2
    groups = [list(range(half)), list(range(half, size))]
    rows = value.shape[0]
    each = -(-rows // half)
    if each * half != rows:
        value = jnp.concatenate([value, jnp.zeros((each * half - rows, 128), F32)], axis=0)
    pieces = lax.all_to_all(
        value.reshape(half, each, 128), "batch", 0, 0, axis_index_groups=groups, tiled=True
    )
    mine = jnp.sum(pieces, axis=0)
    mine = mine + lax.ppermute(mine, "batch", [(i, (i + half) % size) for i in range(size)])
    full = lax.all_to_all(
        jnp.broadcast_to(mine[None], (half, each, 128)), "batch", 0, 0,
        axis_index_groups=groups, tiled=True,
    )
    return full.reshape(each * half, 128)[:rows]


def shards(
    states, next_states, actions, rewards, finished, valid_counts,
    trunk_input, trunk_middle, trunk_vector, head_weight, head_vector,
    critic_input, critic_middle, critic_vector,
    target_input, target_middle, target_vector,
    mean_trunk_input, square_trunk_input, mean_trunk_middle, square_trunk_middle,
    mean_trunk_vector, square_trunk_vector, mean_head_weight, square_head_weight,
    mean_head_vector, square_head_vector, mean_critic_input, square_critic_input,
    mean_critic_middle, square_critic_middle, mean_critic_vector, square_critic_vector,
):
    group = lax.axis_index("net").astype(jnp.int32)
    row_total = states.shape[1]
    used = valid_counts[0]
    tiles = (used + TILE - 1) // TILE
    info = jnp.stack([group, group, (tiles - group + 1) // 2, used])

    def turned(array):
        if array.ndim == 3 and array.shape[1] != HID:
            return jnp.transpose(array, (1, 0, 2))
        if array.ndim == 2 and array.shape[0] == HID:
            return array.T
        return array.reshape(1, -1) if array.ndim == 1 else array

    def back(array, like):
        if like.ndim == 3 and like.shape[1] != HID:
            return jnp.transpose(array, (1, 0, 2))
        if like.ndim == 2 and like.shape[0] == HID:
            return array.T
        return array.reshape(like.shape)

    params = [
        tuple(turned(array) for array in triple)
        for triple in (
            (trunk_input, mean_trunk_input, square_trunk_input),
            (trunk_middle, mean_trunk_middle, square_trunk_middle),
            (trunk_vector, mean_trunk_vector, square_trunk_vector),
            (head_weight, mean_head_weight, square_head_weight),
            (head_vector, mean_head_vector, square_head_vector),
            (critic_input, mean_critic_input, square_critic_input),
            (critic_middle, mean_critic_middle, square_critic_middle),
            (critic_vector, mean_critic_vector, square_critic_vector),
        )
    ]
    targets = tuple(turned(array) for array in (target_input, target_middle, target_vector))
    own = tuple(params[i][0] for i in (0, 1, 2, 5, 6, 7)) + targets
    other = tuple(across(array) for array in own)
    lines = (row_total // 128, 128)
    own_part, other_part = run_main(
        info,
        (states, next_states, actions, rewards.reshape(lines), finished.reshape(lines)),
        (params[3][0], params[4][0]),
        own + other,
    )
    results = list(run_lamb(summed(own_part + across(other_part)), params, targets))
    likes = (
        trunk_input, trunk_middle, trunk_vector, head_weight, head_vector,
        critic_input, critic_middle, critic_vector,
    ) * 3 + (target_input, target_middle, target_vector)
    final = [back(array, like) for array, like in zip(results, likes)]
    return tuple(final) + (jnp.transpose(results[27], (0, 2, 1)), results[28].reshape(5))


def solution(mesh):
    rows, matrix, vector, none = P(None, "batch"), P("net", None, None), P("net", None), P()
    line = P("batch")
    params = (matrix, matrix, vector, none, none, matrix, matrix, vector)
    moments = tuple(spec for entry in params for spec in (entry, entry))
    target = (matrix, matrix, vector)
    return jax.shard_map(
        shards,
        mesh=mesh,
        in_specs=(rows, rows, rows, line, line, line) + params + target + moments,
        out_specs=params * 3 + target + (matrix, none),
        check_vma=False,
    )
```

```python
import functools
import math

import jax
import jax.numpy as jnp
from jax import lax
from jax.experimental import pallas as pl
from jax.experimental.pallas import tpu as pltpu
from jax.sharding import PartitionSpec as P

STEP = 10
EXPECTILE = 0.7
DISCOUNT = 0.99
BETA_TEMP = 3.0
WEIGHT_CLIP = 100.0
DECAY_FIRST = 0.9
DECAY_SECOND = 0.999
EPSILON = 1e-06
WEIGHT_DECAY = 0.01
LEARN_RATE = 0.3
TARGET_RATE = 0.005
BAND = 32
LOG_TWO_PI = math.log(2.0 * math.pi)

OBS = 17
ACT = 6
HID = 256
TILE = 256
WIDTH = 7
UNROLL = 2
ROW_TRUNK = 2 * HID
ROW_CRITIC = ROW_TRUNK + 24
ROW_VECTOR = ROW_CRITIC + 24
ROW_HEAD = ROW_VECTOR + 8
PAYLOAD = ROW_HEAD + 8
VMEM_LIMIT = 64 * 2**20 - 2**17

META_ROW = OBS + ACT
NEXT_ROW = META_ROW + 1
PACK_ROWS = NEXT_ROW + OBS + 2
TRUNK, CRITIC, TARGET = range(3)
SMALL_ROW = 3 * HID
WEIGHT_ROWS = SMALL_ROW + 3 * 32
EXTRA_ROWS = 384
HEAD_START = 2

F32 = jnp.float32
BF16 = jnp.bfloat16
NN = (((1,), (0,)), ((), ()))
NT = (((1,), (1,)), ((), ()))


def split(value):
    high = value.astype(BF16)
    return high, (value - high.astype(F32)).astype(BF16)


def dot(left, right, dims=NN):
    return lax.dot_general(left, right, dims, preferred_element_type=F32)


def fold(value):
    total = value[:, :128]
    for start in range(128, value.shape[1], 128):
        total = total + value[:, start : start + 128]
    return total


def wide(value):
    return jnp.concatenate([value] * (TILE // 128), axis=1)


def left_parts(value):
    return jnp.concatenate(split(value), axis=0)


def column(row):
    return jnp.transpose(jnp.broadcast_to(row, (128, row.shape[1])))


def room_of(row_total):
    total, least = row_total // TILE, -(-(row_total // 3) // TILE)
    return max(1, -(-(total - (total + least) // 2) // 2))


def plan(count_ref, size, row_total):
    group, index = lax.axis_index("net"), lax.axis_index("batch")
    used = count_ref[0]
    tiles = (used + TILE - 1) // TILE
    total, room, lowest = row_total // TILE, room_of(row_total), row_total // 3
    guess = (
        lowest
        + (size - 1 - index) * (row_total - lowest - row_total // 8) // max(size - 1, 1)
        + row_total // 16
    )
    kept = (used + guess + EXTRA_ROWS + 2 * TILE - 1) // (2 * TILE)
    kept = jnp.minimum(jnp.maximum(kept, tiles - 2 * room), tiles)
    kept = jnp.where(tiles - kept < 2, tiles, kept)
    upper = 2 * index >= size
    kept = jnp.where(upper, kept, tiles)
    sent = tiles - kept
    first = (sent + 1) // 2
    mine = jnp.minimum((kept + HEAD_START) // 2, kept)
    leading = group == 0
    start = kept + jnp.where(leading, 0, first)
    return dict(
        group=group, used=used, upper=upper,
        own_start=jnp.where(leading, 0, mine), own_count=jnp.where(leading, mine, kept - mine),
        sent_start=start, sent_count=jnp.where(leading, first, sent - first),
        window=jnp.minimum(start, total - room),
    )


def pack_kernel(size, count_ref, states, next_states, actions, rewards, finished, *refs):
    weights, (weight_out, row_out), (state_part, next_part, action_part, small_part, matrix_part, arrive) = (
        refs[:9], refs[9:11], refs[11:],
    )
    row_total = states.shape[1]
    room = room_of(row_total)
    here = plan(count_ref, size, row_total)
    at = pl.ds(pl.multiple_of(here["window"] * TILE, TILE), room * TILE)
    copies = [
        pltpu.make_async_copy(source.at[:, at], target, arrive.at[k])
        for k, (source, target) in enumerate(
            ((states, state_part), (next_states, next_part), (actions, action_part))
        )
    ]
    matrices = [
        pltpu.make_async_copy(weights[3 * net + 1].at[0], matrix_part.at[net], arrive.at[3 + net])
        for net in range(3)
    ]
    leaving = [
        pltpu.make_async_copy(
            matrix_part.at[net], weight_out.at[net * HID : (net + 1) * HID, :], arrive.at[7 + net]
        )
        for net in range(3)
    ]
    for copy in matrices + copies:
        copy.start()
    for net in range(3):
        rows, _, vector = weights[3 * net : 3 * net + 3]
        row = 32 * net
        width = rows.shape[0]
        pieces = [rows[:, 0, :]]
        if width < META_ROW:
            pieces.append(jnp.zeros((META_ROW - width, HID), F32))
        pieces.append(vector[:, :HID])
        small_part[row : row + 24, :] = jnp.concatenate(pieces, axis=0)
        pieces = [vector[:, HID : 2 * HID]]
        if vector.shape[1] > 2 * HID:
            pieces.append(vector[:, 2 * HID : 3 * HID])
            pieces.append(jnp.broadcast_to(vector[:, 3 * HID : 3 * HID + 1], (1, HID)))
        pieces.append(jnp.zeros((8 - len(pieces), HID), F32))
        small_part[row + 24 : row + 32, :] = jnp.concatenate(pieces, axis=0)
    small = pltpu.make_async_copy(small_part, weight_out.at[SMALL_ROW:, :], arrive.at[6])
    small.start()
    for arriving, copy in zip(matrices, leaving):
        arriving.wait()
        copy.start()

    def line(ref):
        first = here["window"] * (TILE // 128)
        return jnp.concatenate(
            [ref[pl.ds(first + k, 1), :] for k in range(room * TILE // 128)], axis=1
        )

    lane = lax.broadcasted_iota(jnp.int32, (1, room * TILE), 1)
    meta = jnp.zeros((1, room * TILE), F32)
    for k, number in enumerate(
        (
            here["sent_start"] - here["window"], here["sent_count"],
            here["used"] - here["window"] * TILE,
        )
    ):
        meta = jnp.where(lane == k, number.astype(F32), meta)
    for copy in copies:
        copy.wait()
    row_out[: META_ROW + 1, :] = jnp.concatenate([state_part[...], action_part[...], meta], axis=0)
    row_out[NEXT_ROW:, :] = jnp.concatenate(
        [next_part[...], line(rewards), line(finished).astype(F32)], axis=0
    )
    for copy in leaving + [small]:
        copy.wait()


def run_pack(counts, data, weights):
    vmem = pl.BlockSpec(memory_space=pltpu.VMEM)
    smem = pl.BlockSpec(memory_space=pltpu.SMEM)
    hbm = pl.BlockSpec(memory_space=pl.ANY)
    span = room_of(data[0].shape[1]) * TILE
    return pl.pallas_call(
        functools.partial(pack_kernel, lax.axis_size("batch")),
        out_shape=[
            jax.ShapeDtypeStruct((WEIGHT_ROWS, HID), F32),
            jax.ShapeDtypeStruct((PACK_ROWS, span), F32),
        ],
        in_specs=[smem] + [hbm] * 3 + [vmem] * 2 + [vmem, hbm, vmem] * 3,
        out_specs=[hbm, vmem],
        scratch_shapes=[
            pltpu.VMEM((OBS, span), F32),
            pltpu.VMEM((OBS, span), F32),
            pltpu.VMEM((ACT, span), F32),
            pltpu.VMEM((WEIGHT_ROWS - SMALL_ROW, HID), F32),
            pltpu.VMEM((3, HID, HID), F32),
            pltpu.SemaphoreType.DMA((10,)),
        ],
        compiler_params=pltpu.CompilerParams(vmem_limit_bytes=VMEM_LIMIT),
        name="messages",
    )(counts, *data, *weights)


def main_kernel(size, count_ref, *refs):
    sources, refs, (*data, arrive) = refs[:5], refs[5:-6], refs[-6:]
    states, next_states, actions, rewards, finished = data
    copies = [
        pltpu.make_async_copy(source, target, arrive.at[k])
        for k, (source, target) in enumerate(zip(sources, data))
    ]
    for copy in copies:
        copy.start()

    def ready():
        for copy in copies:
            copy.wait()

    def line(ref, index):
        parts = TILE // 128
        return jnp.concatenate(
            [ref[pl.ds(index * parts + part, 1), :] for part in range(parts)], axis=1
        )

    def rows_of(index, at):
        return (
            states[:, at], next_states[:, at], actions[:, at],
            line(rewards, index), line(finished, index).astype(F32),
        )

    here = plan(count_ref, size, states.shape[1])
    gradients(
        here["group"], here["own_start"], here["own_count"], here["used"], rows_of, ready, None,
        *refs,
    )


def moved_kernel(size, packed_ref, *refs):
    inputs, outs, scratch = refs[:6], refs[6:8], refs[8:22]
    packed, *buffers, meta_part, arrive = refs[22:]

    def add(start, count, used):
        copies = [
            pltpu.make_async_copy(source, target, arrive.at[k])
            for k, (source, target) in enumerate(zip((packed_ref,) + inputs, [packed] + buffers))
        ]
        for copy in copies:
            copy.start()
        for copy in copies:
            copy.wait()

        def rows_of(index, at):
            return (
                packed[:OBS, at], packed[NEXT_ROW : NEXT_ROW + OBS, at], packed[OBS:META_ROW, at],
                packed[NEXT_ROW + OBS : NEXT_ROW + OBS + 1, at], packed[PACK_ROWS - 1 : PACK_ROWS, at],
            )

        sums = buffers[:2]
        gradients(
            lax.axis_index("net"), start, count, used, rows_of, lambda: None, sums,
            *buffers[2:], *sums, *scratch,
        )
        copies = [
            pltpu.make_async_copy(source, target, arrive.at[k])
            for k, (source, target) in enumerate(zip(sums, outs))
        ]
        for copy in copies:
            copy.start()
        for copy in copies:
            copy.wait()

    @pl.when(2 * lax.axis_index("batch") < size)
    def _():
        copy = pltpu.make_async_copy(
            packed_ref.at[META_ROW - 7 : META_ROW + 1, :128], meta_part, arrive.at[0]
        )
        copy.start()
        copy.wait()
        meta = meta_part[7:8, :]
        place = lax.broadcasted_iota(jnp.int32, (1, 128), 1)
        start, count, used = (
            jnp.sum(jnp.where(place == k, meta, 0.0)).astype(jnp.int32) for k in range(3)
        )
        pl.when(count > 0)(lambda: add(start, count, used))


def gradients(
    group, start_tile, tile_count, used, rows_of, ready, before, head_weight, head_vector, *refs
):
    (own, other), (out_own, out_other), scratch = refs[:2], refs[2:4], refs[4:]
    (
        first, second, back, bias_two, out_weight, head_pack, head_back, head_bias,
        acc_second, acc_first, acc_bias, acc_out, acc_head, acc_rows,
    ) = scratch

    head_columns = jnp.concatenate([head_weight[...], jnp.zeros((1, HID), F32)], axis=0)
    value_row = head_columns[0:1]
    action_rows = jnp.concatenate(
        [head_columns[1:7], jnp.zeros((2, HID), F32)], axis=0
    )
    row_high, row_low = split(jnp.concatenate([action_rows, jnp.zeros((8, HID), F32)], axis=0))
    head_pack[...] = jnp.concatenate([row_high, row_low], axis=0)
    mean_columns = jnp.transpose(
        jnp.concatenate([action_rows * 0.5, jnp.zeros((120, HID), F32)], axis=0)
    )[:, :16]
    mean_high, mean_low = split(mean_columns)
    head_back[...] = jnp.concatenate(
        [mean_high, mean_low, mean_high], axis=1
    )
    bias_column = jnp.transpose(
        jnp.concatenate(
            [
                jnp.concatenate([head_vector[...], jnp.zeros((1, 128 - 13), F32)], axis=1),
                jnp.zeros((127, 128), F32),
            ],
            axis=0,
        )
    )[:16, 0:1]
    head_bias[...] = jnp.broadcast_to(bias_column, (16, 128))

    is_value = group == 0

    def prepare(slot, net, take, out_row, with_back):
        row = SMALL_ROW + 32 * net
        packed = take(row, 24) * 0.5
        high = packed.astype(BF16).astype(F32)
        stack = jnp.concatenate(
            [high, high, packed - high, jnp.zeros((128 - 72, HID), F32)], axis=0
        )
        first[slot] = jnp.transpose(stack).astype(BF16)
        matrix = take(net * HID, HID)
        second[slot] = left_parts(jnp.transpose(matrix) * 0.5)
        bias_two[slot] = column(take(row + 24, 1) * 0.5)
        if out_row is not None:
            out_weight[slot] = column(out_row)
        if with_back:
            back[slot] = left_parts(matrix * (0.25 * out_row if out_row is not None else 0.5))

    def picked(first_ref, second_ref):
        return lambda row, count: jnp.where(
            is_value, first_ref[row : row + count, :], second_ref[row : row + count, :]
        )

    def small(ref, net, row):
        return ref[SMALL_ROW + 32 * net + 24 + row : SMALL_ROW + 32 * net + 25 + row, :]

    prepare(0, TRUNK, picked(own, other), value_row, True)
    prepare(1, TRUNK, picked(other, own), None, True)
    for slot, ref, net in (
        (2, own, CRITIC), (3, other, CRITIC), (4, own, TARGET), (5, other, TARGET),
    ):
        take = lambda row, count, ref=ref: ref[row : row + count, :]
        prepare(slot, net, take, small(ref, net, 1), slot < 4)
    target_bias = [small(ref, TARGET, 2)[:, :1] for ref in (own, other)]
    critic_bias = [small(ref, CRITIC, 2)[:, :1] for ref in (own, other)]
    value_bias = head_vector[0:1, 0:1]

    acc_second[...] = jnp.zeros_like(acc_second)
    acc_first[...] = jnp.zeros_like(acc_first)
    acc_bias[...] = jnp.zeros_like(acc_bias)
    acc_out[...] = jnp.zeros_like(acc_out)
    acc_head[...] = jnp.zeros_like(acc_head)
    acc_rows[...] = jnp.zeros_like(acc_rows)

    def chains(index):
        at = pl.ds(pl.multiple_of(index * TILE, TILE), TILE)
        states_t, next_t, actions_t, reward, done = rows_of(index, at)
        ones = jnp.ones((1, TILE), F32)
        place = index * TILE + lax.broadcasted_iota(jnp.int32, (1, TILE), 1)
        valid = (place < used).astype(F32)

        def pack(rows):
            full = jnp.concatenate([rows, actions_t, ones], axis=0)
            high = full.astype(BF16).astype(F32)
            low = full - high
            return jnp.concatenate(
                [high, low, high, jnp.zeros((128 - 72, TILE), F32)], axis=0
            ).astype(BF16)

        pairs = pack(states_t)
        pairs_next = pack(next_t)

        def product(ref, slot, high, low):
            both = dot(ref[slot], high)
            return both[:HID] + both[HID:] + dot(ref[slot, :HID], low)

        def layer(half):
            t = jnp.tanh(half)
            u = t + 1.0
            a = half * u
            return a, t, u

        def forward(slot, inputs, keep):
            half = dot(first[slot], inputs)
            yield
            a_one, t, u = layer(half)
            slope_one = u + a_one * (1.0 - t) if keep else None
            parts = split(a_one)
            yield
            z = product(second, slot, parts[0], parts[1])
            yield
            a_two, t, u = layer(z + wide(bias_two[slot]))
            slope_two = u + a_two * (1.0 - t) if keep else None
            return parts, slope_one, a_two, slope_two

        def weighted(slot, hidden):
            return jnp.sum(hidden * wide(out_weight[slot]), axis=0, keepdims=True)

        def backward(slot, parts, slope_one, delta_two):
            acc_bias[slot] += fold(delta_two)
            high, low = split(delta_two)
            yield
            delta_one = product(back, slot, high, low)
            acc_second[slot] += dot(
                jnp.concatenate([parts[0], parts[1], parts[0]], axis=1),
                jnp.concatenate([high, high, low], axis=1),
                NT,
            )
            yield
            high, low = split(delta_one * slope_one)
            yield
            rows = pairs[:48]
            acc_first[slot] += dot(
                jnp.concatenate([rows, rows], axis=1), jnp.concatenate([high, low], axis=1), NT
            )

        known = {}

        def next_chain():
            _, _, hidden, _ = yield from forward(0, pairs_next, False)
            value_next = weighted(0, hidden) + value_bias
            known["goal"] = reward + DISCOUNT * (1.0 - done) * value_next

        def target_chain(member):
            _, _, hidden, _ = yield from forward(4 + member, pairs, False)
            known["target", member] = weighted(4 + member, hidden) + target_bias[member]

        def critic_chain(member):
            slot = 2 + member
            parts, slope_one, hidden, slope_two = yield from forward(slot, pairs, True)
            error = (weighted(slot, hidden) + critic_bias[member] - known["goal"]) * valid
            grad = 2.0 * error
            known["critic", member] = (error * error, grad)
            acc_out[slot] += fold(hidden * grad)
            yield from backward(slot, parts, slope_one, slope_two * grad)

        def value_chain():
            parts, slope_one, hidden, slope_two = yield from forward(0, pairs, True)
            target_min = jnp.minimum(known["target", 0], known["target", 1])
            gap = target_min - (weighted(0, hidden) + value_bias)
            expect = jnp.where(gap < 0.0, 1.0 - EXPECTILE, EXPECTILE) * valid
            grad = -2.0 * expect * gap
            known["gap"] = gap
            known["value"] = (grad, expect * gap * gap)
            acc_out[0] += fold(hidden * grad)
            yield from backward(0, parts, slope_one, slope_two * grad)

        def actor_chain():
            parts, slope_one, hidden, slope_two = yield from forward(1, pairs, True)
            hidden_high, hidden_low = split(hidden)
            both = dot(head_pack[...], hidden_high)
            head = both[:8] + both[16:24] + dot(head_pack[:16], hidden_low)[:8]
            yield
            bias = wide(head_bias[...])
            mean = jnp.tanh(head[:6] + bias[1:7])
            log_std = bias[7:13]
            inverse = jnp.exp(-log_std)
            scaled = (actions_t - mean) * inverse
            log_prob = jnp.sum(
                -0.5 * scaled * scaled - log_std - 0.5 * LOG_TWO_PI, axis=0, keepdims=True
            )
            weight = jnp.minimum(jnp.exp(BETA_TEMP * known["gap"]), WEIGHT_CLIP) * valid
            grad_mean = -weight * scaled * inverse * (1.0 - mean * mean)
            grad_std = -weight * (scaled * scaled - 1.0)
            known["actor"] = (grad_mean, grad_std, -weight * log_prob)
            grads = jnp.concatenate([grad_mean, jnp.zeros((10, TILE), F32)], axis=0)
            grads_high, grads_low = split(grads)
            acc_head[...] += dot(jnp.concatenate([grads_high, grads_low], axis=0), hidden_high, NT)
            acc_head[:16] += dot(grads_high, hidden_low, NT)
            up = dot(
                head_back[...], jnp.concatenate([grads_high, grads_high, grads_low], axis=0)
            )
            yield
            yield from backward(1, parts, slope_one, up * slope_two)

        def finish():
            rows = jnp.concatenate(
                [known["value"][0], known["actor"][0], known["actor"][1], known["value"][1]]
                + [known["critic", 0][0], known["critic", 1][0], known["actor"][2], valid]
                + [known["critic", 0][1], known["critic", 1][1]]
                + [jnp.zeros((4, TILE), F32)],
                axis=0,
            )
            acc_rows[...] += fold(rows)

        return [
            next_chain(), target_chain(0), target_chain(1), critic_chain(0), value_chain(),
            actor_chain(), critic_chain(1),
        ], finish

    def tiles(indices):
        parts = [chains(index) for index in indices]
        waiting = [(chain, part) for part in parts for chain in part[0]]
        left = {id(part): len(part[0]) for part in parts}
        active = []
        while waiting or active:
            while waiting and len(active) < WIDTH:
                active.append(waiting.pop(0))
            for entry in list(active):
                chain, part = entry
                try:
                    next(chain)
                except StopIteration:
                    active.remove(entry)
                    left[id(part)] -= 1
                    if left[id(part)] == 0:
                        part[1]()

    def several(i, carry):
        tiles([start_tile + UNROLL * i + k for k in range(UNROLL)])
        return carry

    def single(i, carry):
        tiles([start_tile + i])
        return carry

    ready()
    rounds = tile_count // UNROLL
    lax.fori_loop(0, rounds, several, 0)
    if UNROLL > 1:
        lax.fori_loop(rounds * UNROLL, tile_count, single, 0)


    def store(out, row, value):
        count = value.shape[0]
        for half in range(2):
            at = slice(half * PAYLOAD + row, half * PAYLOAD + row + count)
            part = value[:, half * 128 : half * 128 + 128]
            if before is not None:
                part = part + before[0 if out is out_own else 1][at, :]
            out[at, :] = part

    def first_grad(slot):
        return acc_first[slot, :24] + acc_first[slot, 24:]

    def lanes(value):
        return jnp.sum(jnp.transpose(value), axis=0, keepdims=True)

    zero_row = jnp.zeros((1, HID), F32)
    row_sums = jnp.sum(
        jnp.transpose(jnp.concatenate([acc_rows[...], jnp.zeros((104, 128), F32)], axis=0)),
        axis=0,
        keepdims=True,
    )
    lane = lax.broadcasted_iota(jnp.int32, (1, 128), 1)
    swapped = jnp.where(
        lane == 14,
        pltpu.roll(row_sums, 127, 1),
        jnp.where(lane == 15, pltpu.roll(row_sums, 1, 1), row_sums),
    )
    shared_row = jnp.where(is_value, row_sums, swapped)
    head_actions = acc_head[:6] + acc_head[16:22]
    head_rows = jnp.concatenate([lanes(acc_out[0]), head_actions, zero_row], axis=0)
    out_rows = (
        value_row * 0.5, None, small(own, CRITIC, 1) * 0.5, small(other, CRITIC, 1) * 0.5,
    )

    def second_grad(slot):
        matrix, bias = acc_second[slot], lanes(acc_bias[slot])
        scale = out_rows[slot]
        return (matrix, bias) if scale is None else (matrix * scale, bias * scale)

    trunk = [second_grad(slot) + (first_grad(slot),) for slot in range(2)]
    for which, out in enumerate((out_own, out_other)):
        trunk_second, trunk_bias, trunk_first = (
            jnp.where(is_value, trunk[which][k], trunk[1 - which][k]) for k in range(3)
        )
        critic_second, critic_bias_two = second_grad(2 + which)
        store(out, 0, trunk_second)
        store(out, HID, critic_second)
        store(out, ROW_TRUNK, trunk_first)
        store(out, ROW_CRITIC, first_grad(2 + which))
        bias_grad = pltpu.roll(row_sums, 128 - 18 - which, 1)
        last = jnp.concatenate([shared_row, jnp.where(lane == 0, bias_grad, 0.0)], axis=1)
        store(
            out,
            ROW_VECTOR,
            jnp.concatenate(
                [trunk_bias, critic_bias_two, lanes(acc_out[2 + which]), last] + [zero_row] * 4,
                axis=0,
            ),
        )
        store(out, ROW_HEAD, head_rows)


def run_main(data, heads, weights, counts=None):
    moved = counts is None
    vmem = pl.BlockSpec(memory_space=pltpu.VMEM)
    smem = pl.BlockSpec(memory_space=pltpu.SMEM)
    operands = (*data, *heads, *weights)
    size = lax.axis_size("batch")
    if moved:
        body, place, specs = moved_kernel, pl.BlockSpec(memory_space=pl.ANY), []
        extra = {"input_output_aliases": {1: 0, 2: 1}}
        buffers = [pltpu.VMEM(array.shape, array.dtype) for array in operands]
        buffers += [pltpu.VMEM((8, 128), F32), pltpu.SemaphoreType.DMA((len(operands),))]
    else:
        body, place, extra = main_kernel, vmem, {}
        specs = [smem] + [pl.BlockSpec(memory_space=pl.ANY)] * len(data)
        buffers = [pltpu.VMEM(array.shape, array.dtype) for array in data]
        buffers.append(pltpu.SemaphoreType.DMA((len(data),)))
        operands = (counts,) + operands
    return pl.pallas_call(
        functools.partial(body, size),
        out_shape=[jax.ShapeDtypeStruct((2 * PAYLOAD, 128), F32)] * 2,
        in_specs=specs + [place] * (len(operands) - len(specs)),
        out_specs=[place] * 2,
        scratch_shapes=[
            pltpu.VMEM((6, HID, 128), BF16),
            pltpu.VMEM((6, 2 * HID, HID), BF16),
            pltpu.VMEM((4, 2 * HID, HID), BF16),
            pltpu.VMEM((6, HID, 128), F32),
            pltpu.VMEM((6, HID, 128), F32),
            pltpu.VMEM((32, HID), BF16),
            pltpu.VMEM((HID, 48), BF16),
            pltpu.VMEM((16, 128), F32),
            pltpu.VMEM((4, HID, HID), F32),
            pltpu.VMEM((4, 48, HID), F32),
            pltpu.VMEM((4, HID, 128), F32),
            pltpu.VMEM((4, HID, 128), F32),
            pltpu.VMEM((32, HID), F32),
            pltpu.VMEM((24, 128), F32),
        ]
        + buffers,
        **extra,
        compiler_params=pltpu.CompilerParams(vmem_limit_bytes=VMEM_LIMIT),
        cost_estimate=pl.CostEstimate(
            flops=10**10, bytes_accessed=5 * 10**6, transcendentals=10**7
        ),
        name="moved_gradients" if moved else "gradients",
    )(*operands)


def read(ref):
    if len(ref.shape) == 2:
        return ref[...]
    return ref[:, 0, :] if ref.shape[1] == 1 else ref[0]


def write(ref, value):
    if len(ref.shape) == 2:
        ref[...] = value
    elif ref.shape[1] == 1:
        ref[:, 0, :] = value
    else:
        ref[0] = value


def lamb_kernel(*refs):
    count = 1 + 3 * len(NAMES) + 3
    sources, targets_out, buffers = refs[:count], refs[count : count + 29], refs[count + 29 :]
    inputs, outs = buffers[:count], buffers[count : count + 29]
    steps, arrive, leave = buffers[count + 29 :]
    copies = [
        pltpu.make_async_copy(source, target, arrive.at[k])
        for k, (source, target) in enumerate(zip(sources, inputs))
    ]
    stages = ([0, 4, 5, 6], [19, 20, 21], [1, 2, 3, *range(7, 19), *range(22, count)])
    for stage in stages:
        for k in stage:
            copies[k].start()
    for k in stages[0]:
        copies[k].wait()
    sent = []

    def send(places):
        for at in places:
            copy = pltpu.make_async_copy(outs[at], targets_out[at], leave.at[at])
            copy.start()
            sent.append(copy)

    payload = inputs[0]
    params = [inputs[1 + 3 * i : 4 + 3 * i] for i in range(len(NAMES))]
    targets = inputs[count - 3 :]

    def rows(start, count):
        return jnp.concatenate(
            [payload[start : start + count, :], payload[PAYLOAD + start : PAYLOAD + start + count, :]],
            axis=1,
        )

    trunk_first = rows(ROW_TRUNK, 24)
    critic_first = rows(ROW_CRITIC, 24)
    vectors = rows(ROW_VECTOR, 8)
    head = rows(ROW_HEAD, 8)
    shared = vectors[3:4, :128]
    after = 1.0 / shared[:, 17:18]
    gradients = (
        trunk_first[:OBS],
        None,
        jnp.concatenate([trunk_first[23:24], vectors[0:1]], axis=1),
        head[:7],
        shared[:, :13],
        critic_first[: OBS + ACT],
        None,
        jnp.concatenate(
            [critic_first[23:24], vectors[1:2], vectors[2:3], vectors[3:4, 128:129]], axis=1
        ),
    )
    def moments(weight, gradient, mean_old, square_old):
        mean_new = DECAY_FIRST * mean_old + (1.0 - DECAY_FIRST) * gradient
        square_new = DECAY_SECOND * square_old + (1.0 - DECAY_SECOND) * gradient * gradient
        mean_hat = mean_new * (1.0 / (1.0 - DECAY_FIRST**STEP))
        square_hat = square_new * (1.0 / (1.0 - DECAY_SECOND**STEP))
        update = mean_hat / (jnp.sqrt(square_hat) + EPSILON) + WEIGHT_DECAY * weight
        return mean_new, square_new, update

    def total(value):
        return jnp.sum(jnp.sum(value * value, axis=0, keepdims=True), axis=1, keepdims=True)

    norms = {}
    updates = {}
    for i in (1, 6, 0, 2, 3, 4, 5, 7):
        if i in (6, 0):
            for k in stages[1 if i == 6 else 2]:
                copies[k].wait()
        weight_ref, mean_ref, square_ref = params[i]
        if i in (1, 6):
            weight_sum, update_sum = jnp.zeros((8, HID), F32), jnp.zeros((8, HID), F32)
            for band in range(0, HID, BAND):
                at = slice(band, band + BAND)
                weight = weight_ref[0, at, :]
                gradient = rows((0 if i == 1 else HID) + band, BAND) * after
                mean_new, square_new, update = moments(
                    weight, gradient, mean_ref[0, at, :], square_ref[0, at, :]
                )
                outs[8 + i][0, at, :] = mean_new
                outs[16 + i][0, at, :] = square_new
                steps[0 if i == 1 else 1, at, :] = update
                for k in range(0, BAND, 8):
                    weight_sum += weight[k : k + 8] * weight[k : k + 8]
                    update_sum += update[k : k + 8] * update[k : k + 8]
            over = lambda part: jnp.sum(
                jnp.sum(part, axis=0, keepdims=True), axis=1, keepdims=True
            )
            norms[i] = (jnp.sqrt(over(weight_sum)), jnp.sqrt(over(update_sum)))
            send((8 + i, 16 + i))
        else:
            weight = read(weight_ref)
            mean_new, square_new, updates[i] = moments(
                weight, gradients[i] * after, read(mean_ref), read(square_ref)
            )
            write(outs[8 + i], mean_new)
            write(outs[16 + i], square_new)
            norms[i] = (jnp.sqrt(total(weight)), jnp.sqrt(total(updates[i])))
    send([8 + k + i for i in (0, 2, 3, 4, 5, 7) for k in (0, 8)])
    for i, name in enumerate(NAMES):
        scale = LEARN_RATE * (norms[i][0] / norms[i][1])
        if i in (1, 6):
            for band in range(0, HID, BAND):
                at = slice(band, band + BAND)
                new = params[i][0][0, at, :] - scale * steps[0 if i == 1 else 1, at, :]
                outs[i][0, at, :] = new
                if i == 6:
                    outs[25][0, at, :] = (
                        (1.0 - TARGET_RATE) * targets[1][0, at, :] + TARGET_RATE * new
                    )
        else:
            new = read(params[i][0]) - scale * updates[i]
            write(outs[i], new)
            if i >= 5:
                write(
                    outs[19 + i], (1.0 - TARGET_RATE) * read(targets[i - 5]) + TARGET_RATE * new
                )
    lane = lax.broadcasted_iota(jnp.int32, (1, 8), 1)
    for row in range(2):
        line = jnp.zeros((1, 8), F32)
        for i, pair in norms.items():
            line = jnp.where(lane == i, pair[row], line)
        outs[27][0, row : row + 1, :] = line
    outs[28][...] = pltpu.roll(shared, 128 - 13, 1)[:, :5]
    send([*range(8), *range(24, 29)])
    for copy in sent:
        copy.wait()


NAMES = (
    "trunk_input", "trunk_middle", "trunk_vector", "head_weight", "head_vector",
    "critic_input", "critic_middle", "critic_vector",
)


def run_lamb(payload, params, targets):
    hbm = pl.BlockSpec(memory_space=pl.ANY)
    flat = [array for triple in params for array in triple]
    shapes = [jax.ShapeDtypeStruct(triple[0].shape, F32) for triple in params]
    outs = shapes * 3 + [jax.ShapeDtypeStruct(t.shape, F32) for t in targets]
    outs += [jax.ShapeDtypeStruct((1, 2, 8), F32), jax.ShapeDtypeStruct((1, 5), F32)]
    operands = (payload, *flat, *targets)
    return pl.pallas_call(
        lamb_kernel,
        out_shape=outs,
        in_specs=[hbm] * len(operands),
        out_specs=[hbm] * len(outs),
        scratch_shapes=[pltpu.VMEM(array.shape, array.dtype) for array in (*operands, *outs)]
        + [
            pltpu.VMEM((2, HID, HID), F32),
            pltpu.SemaphoreType.DMA((len(operands),)),
            pltpu.SemaphoreType.DMA((len(outs),)),
        ],
        compiler_params=pltpu.CompilerParams(vmem_limit_bytes=VMEM_LIMIT),
        name="update",
    )(*operands)


def across(value):
    size = lax.axis_size("net")
    return lax.ppermute(value, "net", [(i, size - 1 - i) for i in range(size)])


def summed(value):
    size = lax.axis_size("batch")
    if size % 2:
        return lax.psum(value, "batch")
    half = size // 2
    groups = [list(range(half)), list(range(half, size))]
    rows = value.shape[0]
    each = -(-rows // half)
    if each * half != rows:
        value = jnp.concatenate([value, jnp.zeros((each * half - rows, 128), F32)], axis=0)
    pieces = lax.all_to_all(
        value.reshape(half, each, 128), "batch", 0, 0, axis_index_groups=groups, tiled=True
    )
    mine = jnp.sum(pieces, axis=0)
    mine = mine + lax.ppermute(mine, "batch", [(i, (i + half) % size) for i in range(size)])
    full = lax.all_to_all(
        jnp.broadcast_to(mine[None], (half, each, 128)), "batch", 0, 0,
        axis_index_groups=groups, tiled=True,
    )
    return full.reshape(each * half, 128)[:rows]


def shards(
    states, next_states, actions, rewards, finished, valid_counts,
    trunk_input, trunk_middle, trunk_vector, head_weight, head_vector,
    critic_input, critic_middle, critic_vector,
    target_input, target_middle, target_vector,
    mean_trunk_input, square_trunk_input, mean_trunk_middle, square_trunk_middle,
    mean_trunk_vector, square_trunk_vector, mean_head_weight, square_head_weight,
    mean_head_vector, square_head_vector, mean_critic_input, square_critic_input,
    mean_critic_middle, square_critic_middle, mean_critic_vector, square_critic_vector,
):
    def turned(array):
        if array.ndim == 3 and array.shape[1] != HID:
            return jnp.transpose(array, (1, 0, 2))
        if array.ndim == 2 and array.shape[0] == HID:
            return array.T
        return array.reshape(1, -1) if array.ndim == 1 else array

    def back(array, like):
        if like.ndim == 3 and like.shape[1] != HID:
            return jnp.transpose(array, (1, 0, 2))
        if like.ndim == 2 and like.shape[0] == HID:
            return array.T
        return array.reshape(like.shape)

    params = [
        tuple(turned(array) for array in triple)
        for triple in (
            (trunk_input, mean_trunk_input, square_trunk_input),
            (trunk_middle, mean_trunk_middle, square_trunk_middle),
            (trunk_vector, mean_trunk_vector, square_trunk_vector),
            (head_weight, mean_head_weight, square_head_weight),
            (head_vector, mean_head_vector, square_head_vector),
            (critic_input, mean_critic_input, square_critic_input),
            (critic_middle, mean_critic_middle, square_critic_middle),
            (critic_vector, mean_critic_vector, square_critic_vector),
        )
    ]
    targets = tuple(turned(array) for array in (target_input, target_middle, target_vector))
    own = tuple(params[i][0] for i in (0, 1, 2, 5, 6, 7)) + targets
    lines = (states.shape[1] // 128, 128)
    data = (states, next_states, actions, rewards.reshape(lines), finished.reshape(lines))
    heads = (params[3][0], params[4][0])
    weights, message = run_pack(valid_counts, data, own)
    size = lax.axis_size("batch")
    both = (weights, across(weights))
    arrived = lax.ppermute(message, "batch", [(i, size - 1 - i) for i in range(size // 2, size)])
    own_part, other_part = run_main(data, heads, both, valid_counts)
    own_part, other_part = run_main((arrived, own_part, other_part), heads, both)
    results = list(run_lamb(summed(own_part + across(other_part)), params, targets))
    likes = (
        trunk_input, trunk_middle, trunk_vector, head_weight, head_vector,
        critic_input, critic_middle, critic_vector,
    ) * 3 + (target_input, target_middle, target_vector)
    final = [back(array, like) for array, like in zip(results, likes)]
    return tuple(final) + (jnp.transpose(results[27], (0, 2, 1)), results[28].reshape(5))


def solution(mesh):
    rows, matrix, vector, none = P(None, "batch"), P("net", None, None), P("net", None), P()
    line = P("batch")
    params = (matrix, matrix, vector, none, none, matrix, matrix, vector)
    moments = tuple(spec for entry in params for spec in (entry, entry))
    target = (matrix, matrix, vector)
    return jax.shard_map(
        shards,
        mesh=mesh,
        in_specs=(rows, rows, rows, line, line, line) + params + target + moments,
        out_specs=params * 3 + target + (matrix, none),
        check_vma=False,
    )
```

```python
import functools
import math

import jax
import jax.numpy as jnp
from jax import lax
from jax.experimental import pallas as pl
from jax.experimental.pallas import tpu as pltpu
from jax.sharding import PartitionSpec as P

STEP = 10
EXPECTILE = 0.7
DISCOUNT = 0.99
BETA_TEMP = 3.0
WEIGHT_CLIP = 100.0
DECAY_FIRST = 0.9
DECAY_SECOND = 0.999
EPSILON = 1e-06
WEIGHT_DECAY = 0.01
LEARN_RATE = 0.3
TARGET_RATE = 0.005
BAND = 32
LOG_TWO_PI = math.log(2.0 * math.pi)

OBS = 17
ACT = 6
HID = 256
TILE = 256
WIDTH = 7
UNROLL = 3
UNIT = 128
ROW_TRUNK = 2 * HID
ROW_CRITIC = ROW_TRUNK + 24
ROW_VECTOR = ROW_CRITIC + 24
ROW_HEAD = ROW_VECTOR + 8
PAYLOAD = ROW_HEAD + 8
VMEM_LIMIT = 64 * 2**20 - 2**17

META_ROW = OBS + ACT
NEXT_ROW = META_ROW + 1
PACK_ROWS = NEXT_ROW + OBS + 2
TRUNK, CRITIC, TARGET = range(3)
SMALL_ROW = 3 * HID
WEIGHT_ROWS = SMALL_ROW + 3 * 32
EXTRA_ROWS = 384
HEAD_START = 0

F32 = jnp.float32
BF16 = jnp.bfloat16
NN = (((1,), (0,)), ((), ()))
NT = (((1,), (1,)), ((), ()))


def split(value):
    high = value.astype(BF16)
    return high, (value - high.astype(F32)).astype(BF16)


def dot(left, right, dims=NN):
    return lax.dot_general(left, right, dims, preferred_element_type=F32)


def fold(value):
    total = value[:, :128]
    for start in range(128, value.shape[1], 128):
        total = total + value[:, start : start + 128]
    return total


def left_parts(value):
    return jnp.concatenate(split(value), axis=0)


def column(row):
    return jnp.transpose(jnp.broadcast_to(row, (128, row.shape[1])))


def room_of(row_total):
    total, least = row_total // UNIT, -(-(row_total // 3) // UNIT)
    return max(2, -(-(total - (total + least) // 2) // 2))


def plan(count_ref, size, row_total):
    group, index = lax.axis_index("net"), lax.axis_index("batch")
    used = count_ref[0]
    units = (used + UNIT - 1) // UNIT
    total, room, lowest = row_total // UNIT, room_of(row_total), row_total // 3
    guess = (
        lowest
        + (size - 1 - index) * (row_total - lowest - row_total // 8) // max(size - 1, 1)
        + row_total // 16
    )
    kept = (used + guess + EXTRA_ROWS + 2 * UNIT - 1) // (2 * UNIT)
    kept = jnp.minimum(jnp.maximum(kept, units - 2 * room), units)
    kept = jnp.where(units - kept < 4, units, kept)
    kept = jnp.where(2 * index >= size, kept, units)
    sent = units - kept
    first = (sent + 1) // 2
    mine = jnp.minimum((kept + HEAD_START) // 2, kept)
    leading = group == 0
    start = kept + jnp.where(leading, 0, first)
    return dict(
        group=group, used=used,
        own_start=jnp.where(leading, 0, mine), own_count=jnp.where(leading, mine, kept - mine),
        sent_start=start, sent_count=jnp.where(leading, first, sent - first),
        window=jnp.minimum(start, total - room),
    )


def pack_kernel(size, count_ref, states, next_states, actions, rewards, finished, *refs):
    weights, (weight_out, row_out), (state_part, next_part, action_part, small_part, matrix_part, arrive) = (
        refs[:9], refs[9:11], refs[11:],
    )
    row_total = states.shape[1]
    room = room_of(row_total)
    here = plan(count_ref, size, row_total)
    at = pl.ds(pl.multiple_of(here["window"] * UNIT, UNIT), room * UNIT)
    copies = [
        pltpu.make_async_copy(source.at[:, at], target, arrive.at[k])
        for k, (source, target) in enumerate(
            ((states, state_part), (next_states, next_part), (actions, action_part))
        )
    ]
    matrices = [
        pltpu.make_async_copy(weights[3 * net + 1].at[0], matrix_part.at[net], arrive.at[3 + net])
        for net in range(3)
    ]
    leaving = [
        pltpu.make_async_copy(
            matrix_part.at[net], weight_out.at[net * HID : (net + 1) * HID, :], arrive.at[7 + net]
        )
        for net in range(3)
    ]
    for copy in matrices + copies:
        copy.start()
    for net in range(3):
        rows, _, vector = weights[3 * net : 3 * net + 3]
        row = 32 * net
        width = rows.shape[0]
        pieces = [rows[:, 0, :]]
        if width < META_ROW:
            pieces.append(jnp.zeros((META_ROW - width, HID), F32))
        pieces.append(vector[:, :HID])
        small_part[row : row + 24, :] = jnp.concatenate(pieces, axis=0)
        pieces = [vector[:, HID : 2 * HID]]
        if vector.shape[1] > 2 * HID:
            pieces.append(vector[:, 2 * HID : 3 * HID])
            pieces.append(jnp.broadcast_to(vector[:, 3 * HID : 3 * HID + 1], (1, HID)))
        pieces.append(jnp.zeros((8 - len(pieces), HID), F32))
        small_part[row + 24 : row + 32, :] = jnp.concatenate(pieces, axis=0)
    small = pltpu.make_async_copy(small_part, weight_out.at[SMALL_ROW:, :], arrive.at[6])
    small.start()
    for arriving, copy in zip(matrices, leaving):
        arriving.wait()
        copy.start()

    def line(ref):
        first = here["window"] * (UNIT // 128)
        return jnp.concatenate(
            [ref[pl.ds(first + k, 1), :] for k in range(room * UNIT // 128)], axis=1
        )

    lane = lax.broadcasted_iota(jnp.int32, (1, room * UNIT), 1)
    meta = jnp.zeros((1, room * UNIT), F32)
    for k, number in enumerate(
        (
            here["sent_start"] - here["window"], here["sent_count"],
            here["used"] - here["window"] * UNIT,
        )
    ):
        meta = jnp.where(lane == k, number.astype(F32), meta)
    for copy in copies:
        copy.wait()
    row_out[: META_ROW + 1, :] = jnp.concatenate([state_part[...], action_part[...], meta], axis=0)
    row_out[NEXT_ROW:, :] = jnp.concatenate(
        [next_part[...], line(rewards), line(finished).astype(F32)], axis=0
    )
    for copy in leaving + [small]:
        copy.wait()


def run_pack(counts, data, weights):
    vmem = pl.BlockSpec(memory_space=pltpu.VMEM)
    smem = pl.BlockSpec(memory_space=pltpu.SMEM)
    hbm = pl.BlockSpec(memory_space=pl.ANY)
    span = room_of(data[0].shape[1]) * UNIT
    return pl.pallas_call(
        functools.partial(pack_kernel, lax.axis_size("batch")),
        out_shape=[
            jax.ShapeDtypeStruct((WEIGHT_ROWS, HID), F32),
            jax.ShapeDtypeStruct((PACK_ROWS, span), F32),
        ],
        in_specs=[smem] + [hbm] * 3 + [vmem] * 2 + [vmem, hbm, vmem] * 3,
        out_specs=[hbm, vmem],
        scratch_shapes=[
            pltpu.VMEM((OBS, span), F32),
            pltpu.VMEM((OBS, span), F32),
            pltpu.VMEM((ACT, span), F32),
            pltpu.VMEM((WEIGHT_ROWS - SMALL_ROW, HID), F32),
            pltpu.VMEM((3, HID, HID), F32),
            pltpu.SemaphoreType.DMA((10,)),
        ],
        compiler_params=pltpu.CompilerParams(vmem_limit_bytes=VMEM_LIMIT),
        name="messages",
    )(counts, *data, *weights)


def load(pairs, sems):
    copies = [
        pltpu.make_async_copy(source, target, sems.at[k])
        for k, (source, target) in enumerate(pairs)
    ]
    for copy in copies:
        copy.start()
    return copies


def weight_pairs(sources, targets):
    heads = list(zip(sources[:2], targets[:2]))
    parts = [slice(SMALL_ROW, WEIGHT_ROWS)]
    parts += [slice(net * HID, (net + 1) * HID) for net in (CRITIC, TARGET, TRUNK)]
    return heads + [
        (source.at[part, :], target.at[part, :])
        for part in parts
        for source, target in zip(sources[2:], targets[2:])
    ]


def main_kernel(size, count_ref, *refs):
    sources, outs, (arrive, leave, *refs) = refs[:9], refs[9:11], refs[11:]
    buffers, sums, scratch = refs[:9], refs[9:11], refs[11:]
    states, next_states, actions, rewards, finished = buffers[:5]
    pairs = weight_pairs(sources[5:], buffers[5:]) + list(zip(sources[:5], buffers[:5]))
    copies = load(pairs, arrive)

    def line(ref, start, width):
        return jnp.concatenate(
            [ref[pl.ds(start // 128 + part, 1), :] for part in range(width // 128)], axis=1
        )

    def rows_of(start, width):
        at = pl.ds(start, width)
        return (
            states[:, at], next_states[:, at], actions[:, at],
            line(rewards, start, width), line(finished, start, width).astype(F32),
        )

    here = plan(count_ref, size, states.shape[1])
    gradients(
        here["group"], here["own_start"], here["own_count"], here["used"], rows_of, copies, False,
        outs, leave, *buffers[5:], *sums, *scratch,
    )


def moved_kernel(size, packed_ref, *refs):
    inputs, outs, (arrive, leave, *refs) = refs[:6], refs[6:8], refs[8:]
    meta_part, packed, *buffers = refs[:6]
    sums, scratch = refs[6:8], refs[8:]

    def add(start, count, used):
        pairs = weight_pairs(inputs[2:], buffers)
        pairs += [(packed_ref, packed)] + list(zip(inputs[:2], sums))
        copies = load(pairs, arrive)

        def rows_of(start, width):
            at = pl.ds(start, width)
            return (
                packed[:OBS, at], packed[NEXT_ROW : NEXT_ROW + OBS, at], packed[OBS:META_ROW, at],
                packed[NEXT_ROW + OBS : NEXT_ROW + OBS + 1, at], packed[PACK_ROWS - 1 : PACK_ROWS, at],
            )

        gradients(
            lax.axis_index("net"), start, count, used, rows_of, copies, True, outs, leave,
            *buffers, *sums, *scratch,
        )

    @pl.when(2 * lax.axis_index("batch") < size)
    def _():
        copy = pltpu.make_async_copy(
            packed_ref.at[META_ROW - 7 : META_ROW + 1, :128], meta_part, arrive.at[0]
        )
        copy.start()
        copy.wait()
        meta = meta_part[7:8, :]
        place = lax.broadcasted_iota(jnp.int32, (1, 128), 1)
        start, count, used = (
            jnp.sum(jnp.where(place == k, meta, 0.0)).astype(jnp.int32) for k in range(3)
        )
        pl.when(count > 0)(lambda: add(start, count, used))


def gradients(
    group, start_unit, unit_count, used, rows_of, copies, adding, outs, leave,
    head_weight, head_vector, own, other, out_own, out_other, *scratch
):
    (
        first, second, back, bias_two, out_weight, head_pack, head_back, head_bias,
        acc_second, acc_first, acc_bias, acc_out, acc_head, acc_rows,
    ) = scratch

    def await_next(count):
        for _ in range(count):
            copies.pop(0).wait()

    copies = list(copies)
    await_next(4)

    head_columns = jnp.concatenate([head_weight[...], jnp.zeros((1, HID), F32)], axis=0)
    value_row = head_columns[0:1]
    action_rows = jnp.concatenate(
        [head_columns[1:7], jnp.zeros((2, HID), F32)], axis=0
    )
    row_high, row_low = split(jnp.concatenate([action_rows, jnp.zeros((8, HID), F32)], axis=0))
    head_pack[...] = jnp.concatenate([row_high, row_low], axis=0)
    mean_columns = jnp.transpose(
        jnp.concatenate([action_rows * 0.5, jnp.zeros((120, HID), F32)], axis=0)
    )[:, :16]
    mean_high, mean_low = split(mean_columns)
    head_back[...] = jnp.concatenate(
        [mean_high, mean_low, mean_high], axis=1
    )
    bias_column = jnp.transpose(
        jnp.concatenate(
            [
                jnp.concatenate([head_vector[...], jnp.zeros((1, 128 - 13), F32)], axis=1),
                jnp.zeros((127, 128), F32),
            ],
            axis=0,
        )
    )[:16, 0:1]
    head_bias[...] = jnp.broadcast_to(bias_column, (16, 128))

    is_value = group == 0

    def prepare(slot, net, take, out_row, with_back):
        row = SMALL_ROW + 32 * net
        packed = take(row, 24) * 0.5
        high = packed.astype(BF16).astype(F32)
        stack = jnp.concatenate(
            [high, high, packed - high, jnp.zeros((128 - 72, HID), F32)], axis=0
        )
        first[slot] = jnp.transpose(stack).astype(BF16)
        matrix = take(net * HID, HID)
        second[slot] = left_parts(jnp.transpose(matrix) * 0.5)
        bias_two[slot] = column(take(row + 24, 1) * 0.5)
        if out_row is not None:
            out_weight[slot] = column(out_row)
        if with_back:
            back[slot] = left_parts(matrix * (0.25 * out_row if out_row is not None else 0.5))

    def picked(first_ref, second_ref):
        return lambda row, count: jnp.where(
            is_value, first_ref[row : row + count, :], second_ref[row : row + count, :]
        )

    def small(ref, net, row):
        return ref[SMALL_ROW + 32 * net + 24 + row : SMALL_ROW + 32 * net + 25 + row, :]

    for slot, ref, net in (
        (2, own, CRITIC), (3, other, CRITIC), (4, own, TARGET), (5, other, TARGET),
    ):
        if slot % 2 == 0:
            await_next(2)
        take = lambda row, count, ref=ref: ref[row : row + count, :]
        prepare(slot, net, take, small(ref, net, 1), slot < 4)
    await_next(2)
    prepare(0, TRUNK, picked(own, other), value_row, True)
    prepare(1, TRUNK, picked(other, own), None, True)
    target_bias = [small(ref, TARGET, 2)[:, :1] for ref in (own, other)]
    critic_bias = [small(ref, CRITIC, 2)[:, :1] for ref in (own, other)]
    value_bias = head_vector[0:1, 0:1]

    acc_second[...] = jnp.zeros_like(acc_second)
    acc_first[...] = jnp.zeros_like(acc_first)
    acc_bias[...] = jnp.zeros_like(acc_bias)
    acc_out[...] = jnp.zeros_like(acc_out)
    acc_head[...] = jnp.zeros_like(acc_head)
    acc_rows[...] = jnp.zeros_like(acc_rows)

    def chains(start, width):
        start = pl.multiple_of(start, UNIT)
        states_t, next_t, actions_t, reward, done = rows_of(start, width)
        ones = jnp.ones((1, width), F32)
        place = start + lax.broadcasted_iota(jnp.int32, (1, width), 1)

        def wide(value):
            return jnp.concatenate([value] * (width // 128), axis=1)

        valid = (place < used).astype(F32)

        def pack(rows):
            full = jnp.concatenate([rows, actions_t, ones], axis=0)
            high = full.astype(BF16).astype(F32)
            low = full - high
            return jnp.concatenate(
                [high, low, high, jnp.zeros((128 - 72, width), F32)], axis=0
            ).astype(BF16)

        pairs = pack(states_t)
        pairs_next = pack(next_t)

        def product(ref, slot, high, low):
            both = dot(ref[slot], high)
            return both[:HID] + both[HID:] + dot(ref[slot, :HID], low)

        def layer(half):
            t = jnp.tanh(half)
            u = t + 1.0
            a = half * u
            return a, t, u

        def forward(slot, inputs, keep):
            half = dot(first[slot], inputs)
            yield
            a_one, t, u = layer(half)
            slope_one = u + a_one * (1.0 - t) if keep else None
            parts = split(a_one)
            yield
            z = product(second, slot, parts[0], parts[1])
            yield
            a_two, t, u = layer(z + wide(bias_two[slot]))
            slope_two = u + a_two * (1.0 - t) if keep else None
            return parts, slope_one, a_two, slope_two

        def weighted(slot, hidden):
            return jnp.sum(hidden * wide(out_weight[slot]), axis=0, keepdims=True)

        def backward(slot, parts, slope_one, delta_two):
            acc_bias[slot] += fold(delta_two)
            high, low = split(delta_two)
            yield
            delta_one = product(back, slot, high, low)
            acc_second[slot] += dot(
                jnp.concatenate([parts[0], parts[1], parts[0]], axis=1),
                jnp.concatenate([high, high, low], axis=1),
                NT,
            )
            yield
            high, low = split(delta_one * slope_one)
            yield
            rows = pairs[:48]
            acc_first[slot] += dot(
                jnp.concatenate([rows, rows], axis=1), jnp.concatenate([high, low], axis=1), NT
            )

        known = {}

        def next_chain():
            _, _, hidden, _ = yield from forward(0, pairs_next, False)
            value_next = weighted(0, hidden) + value_bias
            known["goal"] = reward + DISCOUNT * (1.0 - done) * value_next

        def target_chain(member):
            _, _, hidden, _ = yield from forward(4 + member, pairs, False)
            known["target", member] = weighted(4 + member, hidden) + target_bias[member]

        def critic_chain(member):
            slot = 2 + member
            parts, slope_one, hidden, slope_two = yield from forward(slot, pairs, True)
            error = (weighted(slot, hidden) + critic_bias[member] - known["goal"]) * valid
            grad = 2.0 * error
            known["critic", member] = (error * error, grad)
            acc_out[slot] += fold(hidden * grad)
            yield from backward(slot, parts, slope_one, slope_two * grad)

        def value_chain():
            parts, slope_one, hidden, slope_two = yield from forward(0, pairs, True)
            target_min = jnp.minimum(known["target", 0], known["target", 1])
            gap = target_min - (weighted(0, hidden) + value_bias)
            expect = jnp.where(gap < 0.0, 1.0 - EXPECTILE, EXPECTILE) * valid
            grad = -2.0 * expect * gap
            known["gap"] = gap
            known["value"] = (grad, expect * gap * gap)
            acc_out[0] += fold(hidden * grad)
            yield from backward(0, parts, slope_one, slope_two * grad)

        def actor_chain():
            parts, slope_one, hidden, slope_two = yield from forward(1, pairs, True)
            hidden_high, hidden_low = split(hidden)
            both = dot(head_pack[...], hidden_high)
            head = both[:8] + both[16:24] + dot(head_pack[:16], hidden_low)[:8]
            yield
            bias = wide(head_bias[...])
            mean = jnp.tanh(head[:6] + bias[1:7])
            log_std = bias[7:13]
            inverse = jnp.exp(-log_std)
            scaled = (actions_t - mean) * inverse
            log_prob = jnp.sum(
                -0.5 * scaled * scaled - log_std - 0.5 * LOG_TWO_PI, axis=0, keepdims=True
            )
            weight = jnp.minimum(jnp.exp(BETA_TEMP * known["gap"]), WEIGHT_CLIP) * valid
            grad_mean = -weight * scaled * inverse * (1.0 - mean * mean)
            grad_std = -weight * (scaled * scaled - 1.0)
            known["actor"] = (grad_mean, grad_std, -weight * log_prob)
            grads = jnp.concatenate([grad_mean, jnp.zeros((10, width), F32)], axis=0)
            grads_high, grads_low = split(grads)
            acc_head[...] += dot(jnp.concatenate([grads_high, grads_low], axis=0), hidden_high, NT)
            acc_head[:16] += dot(grads_high, hidden_low, NT)
            up = dot(
                head_back[...], jnp.concatenate([grads_high, grads_high, grads_low], axis=0)
            )
            yield
            yield from backward(1, parts, slope_one, up * slope_two)

        def finish():
            rows = jnp.concatenate(
                [known["value"][0], known["actor"][0], known["actor"][1], known["value"][1]]
                + [known["critic", 0][0], known["critic", 1][0], known["actor"][2], valid]
                + [known["critic", 0][1], known["critic", 1][1]]
                + [jnp.zeros((4, width), F32)],
                axis=0,
            )
            acc_rows[...] += fold(rows)

        return [
            next_chain(), target_chain(0), target_chain(1), critic_chain(0), value_chain(),
            actor_chain(), critic_chain(1),
        ], finish

    def tiles(starts, width=TILE):
        parts = [chains(start, width) for start in starts]
        waiting = [(chain, part) for part in parts for chain in part[0]]
        left = {id(part): len(part[0]) for part in parts}
        active = []
        while waiting or active:
            while waiting and len(active) < WIDTH:
                active.append(waiting.pop(0))
            for entry in list(active):
                chain, part = entry
                try:
                    next(chain)
                except StopIteration:
                    active.remove(entry)
                    left[id(part)] -= 1
                    if left[id(part)] == 0:
                        part[1]()

    base = start_unit * UNIT
    tile_count = unit_count * UNIT // TILE

    def several(i, carry):
        tiles([base + (UNROLL * i + k) * TILE for k in range(UNROLL)])
        return carry

    def single(i, carry):
        tiles([base + i * TILE])
        return carry

    await_next(len(copies) - (2 if adding else 0))
    rounds = tile_count // UNROLL
    lax.fori_loop(0, rounds, several, 0)
    lax.fori_loop(rounds * UNROLL, tile_count, single, 0)

    @pl.when(unit_count * UNIT > tile_count * TILE)
    def _():
        tiles([base + tile_count * TILE], UNIT)


    def store(out, row, value):
        count = value.shape[0]
        for half in range(2):
            at = slice(half * PAYLOAD + row, half * PAYLOAD + row + count)
            part = value[:, half * 128 : half * 128 + 128]
            out[at, :] = part + out[at, :] if adding else part

    def first_grad(slot):
        return acc_first[slot, :24] + acc_first[slot, 24:]

    def lanes(value):
        return jnp.sum(jnp.transpose(value), axis=0, keepdims=True)

    zero_row = jnp.zeros((1, HID), F32)
    row_sums = jnp.sum(
        jnp.transpose(jnp.concatenate([acc_rows[...], jnp.zeros((104, 128), F32)], axis=0)),
        axis=0,
        keepdims=True,
    )
    lane = lax.broadcasted_iota(jnp.int32, (1, 128), 1)
    swapped = jnp.where(
        lane == 14,
        pltpu.roll(row_sums, 127, 1),
        jnp.where(lane == 15, pltpu.roll(row_sums, 1, 1), row_sums),
    )
    shared_row = jnp.where(is_value, row_sums, swapped)
    head_actions = acc_head[:6] + acc_head[16:22]
    head_rows = jnp.concatenate([lanes(acc_out[0]), head_actions, zero_row], axis=0)
    out_rows = (
        value_row * 0.5, None, small(own, CRITIC, 1) * 0.5, small(other, CRITIC, 1) * 0.5,
    )

    def second_grad(slot):
        matrix, bias = acc_second[slot], lanes(acc_bias[slot])
        scale = out_rows[slot]
        return (matrix, bias) if scale is None else (matrix * scale, bias * scale)

    sent = []

    def send(row, count):
        for out, target in zip((out_own, out_other), outs):
            for half in range(2):
                at = slice(half * PAYLOAD + row, half * PAYLOAD + row + count)
                sent.append(
                    pltpu.make_async_copy(out.at[at, :], target.at[at, :], leave.at[len(sent)])
                )
                sent[-1].start()

    await_next(len(copies))
    trunk = [second_grad(slot) + (first_grad(slot),) for slot in range(2)]
    critic = [second_grad(2 + which) for which in range(2)]
    mixed = [
        [jnp.where(is_value, trunk[which][k], trunk[1 - which][k]) for k in range(3)]
        for which in range(2)
    ]
    for which, out in enumerate((out_own, out_other)):
        store(out, 0, mixed[which][0])
    send(0, HID)
    for which, out in enumerate((out_own, out_other)):
        store(out, HID, critic[which][0])
    send(HID, HID)
    for which, out in enumerate((out_own, out_other)):
        store(out, ROW_TRUNK, mixed[which][2])
        store(out, ROW_CRITIC, first_grad(2 + which))
        bias_grad = pltpu.roll(row_sums, 128 - 18 - which, 1)
        last = jnp.concatenate([shared_row, jnp.where(lane == 0, bias_grad, 0.0)], axis=1)
        store(
            out,
            ROW_VECTOR,
            jnp.concatenate(
                [mixed[which][1], critic[which][1], lanes(acc_out[2 + which]), last]
                + [zero_row] * 4,
                axis=0,
            ),
        )
        store(out, ROW_HEAD, head_rows)
    send(2 * HID, PAYLOAD - 2 * HID)
    for copy in sent:
        copy.wait()


def run_main(data, heads, weights, counts=None):
    hbm = pl.BlockSpec(memory_space=pl.ANY)
    size = lax.axis_size("batch")
    operands = (*data, *heads, *weights)
    payload = jax.ShapeDtypeStruct((2 * PAYLOAD, 128), F32)
    held = [pltpu.VMEM(array.shape, array.dtype) for array in (*heads, *weights)]
    semaphores = [pltpu.SemaphoreType.DMA((16,)), pltpu.SemaphoreType.DMA((12,))]
    if counts is None:
        name, body, specs, aliases = "moved_gradients", moved_kernel, [], {1: 0, 2: 1}
        buffers = [pltpu.VMEM((8, 128), F32), pltpu.VMEM(data[0].shape, F32)] + held
    else:
        name, body, aliases = "gradients", main_kernel, {}
        specs = [pl.BlockSpec(memory_space=pltpu.SMEM)]
        buffers = [pltpu.VMEM(array.shape, array.dtype) for array in data] + held
        operands = (counts,) + operands
    return pl.pallas_call(
        functools.partial(body, size),
        out_shape=[payload, payload],
        in_specs=specs + [hbm] * (len(operands) - len(specs)),
        out_specs=[hbm, hbm],
        input_output_aliases=aliases,
        scratch_shapes=semaphores + buffers + [pltpu.VMEM(payload.shape, F32)] * 2 + [
            pltpu.VMEM((6, HID, 128), BF16),
            pltpu.VMEM((6, 2 * HID, HID), BF16),
            pltpu.VMEM((4, 2 * HID, HID), BF16),
            pltpu.VMEM((6, HID, 128), F32),
            pltpu.VMEM((6, HID, 128), F32),
            pltpu.VMEM((32, HID), BF16),
            pltpu.VMEM((HID, 48), BF16),
            pltpu.VMEM((16, 128), F32),
            pltpu.VMEM((4, HID, HID), F32),
            pltpu.VMEM((4, 48, HID), F32),
            pltpu.VMEM((4, HID, 128), F32),
            pltpu.VMEM((4, HID, 128), F32),
            pltpu.VMEM((32, HID), F32),
            pltpu.VMEM((24, 128), F32),
        ],
        compiler_params=pltpu.CompilerParams(vmem_limit_bytes=VMEM_LIMIT),
        cost_estimate=pl.CostEstimate(
            flops=10**10, bytes_accessed=5 * 10**6, transcendentals=10**7
        ),
        name=name,
    )(*operands)


def read(ref):
    if len(ref.shape) == 2:
        return ref[...]
    return ref[:, 0, :] if ref.shape[1] == 1 else ref[0]


def write(ref, value):
    if len(ref.shape) == 2:
        ref[...] = value
    elif ref.shape[1] == 1:
        ref[:, 0, :] = value
    else:
        ref[0] = value


def lamb_kernel(*refs):
    count = 1 + 3 * len(NAMES) + 3
    sources, targets_out, buffers = refs[:count], refs[count : count + 29], refs[count + 29 :]
    inputs, outs = buffers[:count], buffers[count : count + 29]
    steps, arrive, leave = buffers[count + 29 :]
    copies = [
        pltpu.make_async_copy(source, target, arrive.at[k])
        for k, (source, target) in enumerate(zip(sources, inputs))
    ]
    stages = ([0, 4, 5, 6], [19, 20, 21], [1, 2, 3, *range(7, 19), *range(22, count)])
    for stage in stages:
        for k in stage:
            copies[k].start()
    for k in stages[0]:
        copies[k].wait()
    sent = []

    def send(places):
        for at in places:
            copy = pltpu.make_async_copy(outs[at], targets_out[at], leave.at[at])
            copy.start()
            sent.append(copy)

    payload = inputs[0]
    params = [inputs[1 + 3 * i : 4 + 3 * i] for i in range(len(NAMES))]
    targets = inputs[count - 3 :]

    def rows(start, count):
        return jnp.concatenate(
            [payload[start : start + count, :], payload[PAYLOAD + start : PAYLOAD + start + count, :]],
            axis=1,
        )

    trunk_first = rows(ROW_TRUNK, 24)
    critic_first = rows(ROW_CRITIC, 24)
    vectors = rows(ROW_VECTOR, 8)
    head = rows(ROW_HEAD, 8)
    shared = vectors[3:4, :128]
    after = 1.0 / shared[:, 17:18]
    gradients = (
        trunk_first[:OBS],
        None,
        jnp.concatenate([trunk_first[23:24], vectors[0:1]], axis=1),
        head[:7],
        shared[:, :13],
        critic_first[: OBS + ACT],
        None,
        jnp.concatenate(
            [critic_first[23:24], vectors[1:2], vectors[2:3], vectors[3:4, 128:129]], axis=1
        ),
    )
    def moments(weight, gradient, mean_old, square_old):
        mean_new = DECAY_FIRST * mean_old + (1.0 - DECAY_FIRST) * gradient
        square_new = DECAY_SECOND * square_old + (1.0 - DECAY_SECOND) * gradient * gradient
        mean_hat = mean_new * (1.0 / (1.0 - DECAY_FIRST**STEP))
        square_hat = square_new * (1.0 / (1.0 - DECAY_SECOND**STEP))
        update = mean_hat / (jnp.sqrt(square_hat) + EPSILON) + WEIGHT_DECAY * weight
        return mean_new, square_new, update

    def total(value):
        return jnp.sum(jnp.sum(value * value, axis=0, keepdims=True), axis=1, keepdims=True)

    norms = {}
    updates = {}
    for i in (1, 6, 0, 2, 3, 4, 5, 7):
        if i in (6, 0):
            for k in stages[1 if i == 6 else 2]:
                copies[k].wait()
        weight_ref, mean_ref, square_ref = params[i]
        if i in (1, 6):
            weight_sum, update_sum = jnp.zeros((8, HID), F32), jnp.zeros((8, HID), F32)
            for band in range(0, HID, BAND):
                at = slice(band, band + BAND)
                weight = weight_ref[0, at, :]
                gradient = rows((0 if i == 1 else HID) + band, BAND) * after
                mean_new, square_new, update = moments(
                    weight, gradient, mean_ref[0, at, :], square_ref[0, at, :]
                )
                outs[8 + i][0, at, :] = mean_new
                outs[16 + i][0, at, :] = square_new
                steps[0 if i == 1 else 1, at, :] = update
                for k in range(0, BAND, 8):
                    weight_sum += weight[k : k + 8] * weight[k : k + 8]
                    update_sum += update[k : k + 8] * update[k : k + 8]
            over = lambda part: jnp.sum(
                jnp.sum(part, axis=0, keepdims=True), axis=1, keepdims=True
            )
            norms[i] = (jnp.sqrt(over(weight_sum)), jnp.sqrt(over(update_sum)))
            send((8 + i, 16 + i))
        else:
            weight = read(weight_ref)
            mean_new, square_new, updates[i] = moments(
                weight, gradients[i] * after, read(mean_ref), read(square_ref)
            )
            write(outs[8 + i], mean_new)
            write(outs[16 + i], square_new)
            norms[i] = (jnp.sqrt(total(weight)), jnp.sqrt(total(updates[i])))
    send([8 + k + i for i in (0, 2, 3, 4, 5, 7) for k in (0, 8)])
    for i, name in enumerate(NAMES):
        scale = LEARN_RATE * (norms[i][0] / norms[i][1])
        if i in (1, 6):
            for band in range(0, HID, BAND):
                at = slice(band, band + BAND)
                new = params[i][0][0, at, :] - scale * steps[0 if i == 1 else 1, at, :]
                outs[i][0, at, :] = new
                if i == 6:
                    outs[25][0, at, :] = (
                        (1.0 - TARGET_RATE) * targets[1][0, at, :] + TARGET_RATE * new
                    )
        else:
            new = read(params[i][0]) - scale * updates[i]
            write(outs[i], new)
            if i >= 5:
                write(
                    outs[19 + i], (1.0 - TARGET_RATE) * read(targets[i - 5]) + TARGET_RATE * new
                )
    lane = lax.broadcasted_iota(jnp.int32, (1, 8), 1)
    for row in range(2):
        line = jnp.zeros((1, 8), F32)
        for i, pair in norms.items():
            line = jnp.where(lane == i, pair[row], line)
        outs[27][0, row : row + 1, :] = line
    outs[28][...] = pltpu.roll(shared, 128 - 13, 1)[:, :5]
    send([*range(8), *range(24, 29)])
    for copy in sent:
        copy.wait()


NAMES = (
    "trunk_input", "trunk_middle", "trunk_vector", "head_weight", "head_vector",
    "critic_input", "critic_middle", "critic_vector",
)


def run_lamb(payload, params, targets):
    hbm = pl.BlockSpec(memory_space=pl.ANY)
    flat = [array for triple in params for array in triple]
    shapes = [jax.ShapeDtypeStruct(triple[0].shape, F32) for triple in params]
    outs = shapes * 3 + [jax.ShapeDtypeStruct(t.shape, F32) for t in targets]
    outs += [jax.ShapeDtypeStruct((1, 2, 8), F32), jax.ShapeDtypeStruct((1, 5), F32)]
    operands = (payload, *flat, *targets)
    return pl.pallas_call(
        lamb_kernel,
        out_shape=outs,
        in_specs=[hbm] * len(operands),
        out_specs=[hbm] * len(outs),
        scratch_shapes=[pltpu.VMEM(array.shape, array.dtype) for array in (*operands, *outs)]
        + [
            pltpu.VMEM((2, HID, HID), F32),
            pltpu.SemaphoreType.DMA((len(operands),)),
            pltpu.SemaphoreType.DMA((len(outs),)),
        ],
        compiler_params=pltpu.CompilerParams(vmem_limit_bytes=VMEM_LIMIT),
        name="update",
    )(*operands)


def across(value):
    size = lax.axis_size("net")
    return lax.ppermute(value, "net", [(i, size - 1 - i) for i in range(size)])


def summed(value):
    size = lax.axis_size("batch")
    if size % 2:
        return lax.psum(value, "batch")
    half = size // 2
    groups = [list(range(half)), list(range(half, size))]
    rows = value.shape[0]
    each = -(-rows // half)
    if each * half != rows:
        value = jnp.concatenate([value, jnp.zeros((each * half - rows, 128), F32)], axis=0)
    pieces = lax.all_to_all(
        value.reshape(half, each, 128), "batch", 0, 0, axis_index_groups=groups, tiled=True
    )
    mine = jnp.sum(pieces, axis=0)
    mine = mine + lax.ppermute(
        mine, "batch", [pair for a, b in zip(*groups) for pair in ((a, b), (b, a))]
    )
    full = lax.all_to_all(
        jnp.broadcast_to(mine[None], (half, each, 128)), "batch", 0, 0,
        axis_index_groups=groups, tiled=True,
    )
    return full.reshape(each * half, 128)[:rows]


def shards(
    states, next_states, actions, rewards, finished, valid_counts,
    trunk_input, trunk_middle, trunk_vector, head_weight, head_vector,
    critic_input, critic_middle, critic_vector,
    target_input, target_middle, target_vector,
    mean_trunk_input, square_trunk_input, mean_trunk_middle, square_trunk_middle,
    mean_trunk_vector, square_trunk_vector, mean_head_weight, square_head_weight,
    mean_head_vector, square_head_vector, mean_critic_input, square_critic_input,
    mean_critic_middle, square_critic_middle, mean_critic_vector, square_critic_vector,
):
    def turned(array):
        if array.ndim == 3 and array.shape[1] != HID:
            return jnp.transpose(array, (1, 0, 2))
        if array.ndim == 2 and array.shape[0] == HID:
            return array.T
        return array.reshape(1, -1) if array.ndim == 1 else array

    def back(array, like):
        if like.ndim == 3 and like.shape[1] != HID:
            return jnp.transpose(array, (1, 0, 2))
        if like.ndim == 2 and like.shape[0] == HID:
            return array.T
        return array.reshape(like.shape)

    params = [
        tuple(turned(array) for array in triple)
        for triple in (
            (trunk_input, mean_trunk_input, square_trunk_input),
            (trunk_middle, mean_trunk_middle, square_trunk_middle),
            (trunk_vector, mean_trunk_vector, square_trunk_vector),
            (head_weight, mean_head_weight, square_head_weight),
            (head_vector, mean_head_vector, square_head_vector),
            (critic_input, mean_critic_input, square_critic_input),
            (critic_middle, mean_critic_middle, square_critic_middle),
            (critic_vector, mean_critic_vector, square_critic_vector),
        )
    ]
    targets = tuple(turned(array) for array in (target_input, target_middle, target_vector))
    own = tuple(params[i][0] for i in (0, 1, 2, 5, 6, 7)) + targets
    lines = (states.shape[1] // 128, 128)
    data = (states, next_states, actions, rewards.reshape(lines), finished.reshape(lines))
    heads = (params[3][0], params[4][0])
    weights, message = run_pack(valid_counts, data, own)
    size = lax.axis_size("batch")
    both = (weights, across(weights))
    arrived = lax.ppermute(message, "batch", [(i, size - 1 - i) for i in range(size // 2, size)])
    own_part, other_part = run_main(data, heads, both, valid_counts)
    own_part, other_part = run_main((arrived, own_part, other_part), heads, both)
    results = list(run_lamb(summed(own_part + across(other_part)), params, targets))
    likes = (
        trunk_input, trunk_middle, trunk_vector, head_weight, head_vector,
        critic_input, critic_middle, critic_vector,
    ) * 3 + (target_input, target_middle, target_vector)
    final = [back(array, like) for array, like in zip(results, likes)]
    return tuple(final) + (jnp.transpose(results[27], (0, 2, 1)), results[28].reshape(5))


def solution(mesh):
    rows, matrix, vector, none = P(None, "batch"), P("net", None, None), P("net", None), P()
    line = P("batch")
    params = (matrix, matrix, vector, none, none, matrix, matrix, vector)
    moments = tuple(spec for entry in params for spec in (entry, entry))
    target = (matrix, matrix, vector)
    return jax.shard_map(
        shards,
        mesh=mesh,
        in_specs=(rows, rows, rows, line, line, line) + params + target + moments,
        out_specs=params * 3 + target + (matrix, none),
        check_vma=False,
    )
```

```python
import functools
import math

import jax
import jax.numpy as jnp
from jax import lax
from jax.experimental import pallas as pl
from jax.experimental.pallas import tpu as pltpu
from jax.sharding import PartitionSpec as P

STEP = 10
EXPECTILE = 0.7
DISCOUNT = 0.99
BETA_TEMP = 3.0
WEIGHT_CLIP = 100.0
DECAY_FIRST = 0.9
DECAY_SECOND = 0.999
EPSILON = 1e-06
WEIGHT_DECAY = 0.01
LEARN_RATE = 0.3
TARGET_RATE = 0.005
BAND = 32
LOG_TWO_PI = math.log(2.0 * math.pi)

OBS = 17
ACT = 6
HID = 256
TILE = 256
WIDTH = 7
UNROLL = 3
UNIT = 128
ROW_TRUNK = 2 * HID
ROW_CRITIC = ROW_TRUNK + 24
ROW_VECTOR = ROW_CRITIC + 24
ROW_HEAD = ROW_VECTOR + 8
PAYLOAD = ROW_HEAD + 8
VMEM_LIMIT = 64 * 2**20 - 2**17

META_ROW = OBS + ACT
NEXT_ROW = META_ROW + 1
PACK_ROWS = NEXT_ROW + OBS + 2
TRUNK, CRITIC, TARGET = range(3)
SMALL_ROW = 3 * HID
WEIGHT_ROWS = SMALL_ROW + 3 * 32
EXTRA_ROWS = 640
HEAD_START = 0

F32 = jnp.float32
BF16 = jnp.bfloat16
NN = (((1,), (0,)), ((), ()))
NT = (((1,), (1,)), ((), ()))


def split(value):
    high = value.astype(BF16)
    return high, (value - high.astype(F32)).astype(BF16)


def dot(left, right, dims=NN):
    return lax.dot_general(left, right, dims, preferred_element_type=F32)


def fold(value):
    total = value[:, :128]
    for start in range(128, value.shape[1], 128):
        total = total + value[:, start : start + 128]
    return total


def left_parts(value):
    return jnp.concatenate(split(value), axis=0)


def column(row):
    return jnp.transpose(jnp.broadcast_to(row, (128, row.shape[1])))


def room_of(row_total):
    total, least = row_total // UNIT, -(-(row_total // 3) // UNIT)
    return max(2, -(-(total - (total + least) // 2) // 2))


def plan(count_ref, size, row_total):
    group, index = lax.axis_index("net"), lax.axis_index("batch")
    used = count_ref[0]
    units = (used + UNIT - 1) // UNIT
    total, room, lowest = row_total // UNIT, room_of(row_total), row_total // 3
    guess = (
        lowest
        + (size - 1 - index) * (row_total - lowest - row_total // 8) // max(size - 1, 1)
        + row_total // 16
    )
    kept = (used + guess + EXTRA_ROWS + 2 * UNIT - 1) // (2 * UNIT)
    kept = jnp.minimum(jnp.maximum(kept, units - 2 * room), units)
    kept = jnp.where(units - kept < 4, units, kept)
    kept = jnp.where(2 * index >= size, kept, units)
    sent = units - kept
    first = (sent + 1) // 2
    mine = jnp.minimum((kept + HEAD_START) // 2, kept)
    leading = group == 0
    start = kept + jnp.where(leading, 0, first)
    return dict(
        group=group, used=used,
        own_start=jnp.where(leading, 0, mine), own_count=jnp.where(leading, mine, kept - mine),
        sent_start=start, sent_count=jnp.where(leading, first, sent - first),
        window=jnp.minimum(start, total - room),
    )


def load(pairs, sems):
    copies = [
        pltpu.make_async_copy(source, target, sems.at[k])
        for k, (source, target) in enumerate(pairs)
    ]
    for copy in copies:
        copy.start()
    return copies


def pack_kernel(size, row_total, count_ref, *refs):
    sources, (weight_out, row_out), (arrive, leave, *parts) = refs[:14], refs[14:16], refs[16:]
    state_part, next_part, action_part, rewards, finished = parts[:5]
    weights, (small_part, row_part) = parts[5:14], parts[14:]
    room = room_of(row_total)
    copies = load(list(zip(sources[5:], weights)) + list(zip(sources[3:5], parts[3:5])), arrive)
    here = plan(count_ref, size, row_total)
    at = pl.ds(pl.multiple_of(here["window"] * UNIT, UNIT), room * UNIT)
    for k in range(3):
        copies.append(
            pltpu.make_async_copy(sources[k].at[:, at], parts[k], arrive.at[len(copies)])
        )
        copies[-1].start()
    sent = []

    def send(source, target):
        sent.append(pltpu.make_async_copy(source, target, leave.at[len(sent)]))
        sent[-1].start()

    for net in range(3):
        copies[3 * net + 1].wait()
        send(weights[3 * net + 1].at[0], weight_out.at[net * HID : (net + 1) * HID, :])
    for net in range(3):
        copies[3 * net].wait()
        copies[3 * net + 2].wait()
        rows, _, vector = weights[3 * net : 3 * net + 3]
        row = 32 * net
        width = rows.shape[0]
        pieces = [rows[:, 0, :]]
        if width < META_ROW:
            pieces.append(jnp.zeros((META_ROW - width, HID), F32))
        pieces.append(vector[:, :HID])
        small_part[row : row + 24, :] = jnp.concatenate(pieces, axis=0)
        pieces = [vector[:, HID : 2 * HID]]
        if vector.shape[1] > 2 * HID:
            pieces.append(vector[:, 2 * HID : 3 * HID])
            pieces.append(jnp.broadcast_to(vector[:, 3 * HID : 3 * HID + 1], (1, HID)))
        pieces.append(jnp.zeros((8 - len(pieces), HID), F32))
        small_part[row + 24 : row + 32, :] = jnp.concatenate(pieces, axis=0)
    send(small_part, weight_out.at[SMALL_ROW:, :])

    def line(ref):
        first = here["window"] * (UNIT // 128)
        return jnp.concatenate(
            [ref[pl.ds(first + k, 1), :] for k in range(room * UNIT // 128)], axis=1
        )

    lane = lax.broadcasted_iota(jnp.int32, (1, room * UNIT), 1)
    meta = jnp.zeros((1, room * UNIT), F32)
    for k, number in enumerate(
        (
            here["sent_start"] - here["window"], here["sent_count"],
            here["used"] - here["window"] * UNIT,
        )
    ):
        meta = jnp.where(lane == k, number.astype(F32), meta)
    for copy in copies[9:]:
        copy.wait()
    row_part[: META_ROW + 1, :] = jnp.concatenate([state_part[...], action_part[...], meta], axis=0)
    row_part[NEXT_ROW:, :] = jnp.concatenate(
        [next_part[...], line(rewards), line(finished).astype(F32)], axis=0
    )
    send(row_part, row_out)
    for copy in sent:
        copy.wait()


def run_pack(counts, data, weights):
    hbm = pl.BlockSpec(memory_space=pl.ANY)
    row_total = data[0].shape[1]
    span = room_of(row_total) * UNIT
    row_out = jax.ShapeDtypeStruct((PACK_ROWS, span), F32)
    held = [pltpu.VMEM((array.shape[0], span), F32) for array in data[:3]]
    held += [pltpu.VMEM(array.shape, array.dtype) for array in (*data[3:], *weights)]
    return pl.pallas_call(
        functools.partial(pack_kernel, lax.axis_size("batch"), row_total),
        out_shape=[jax.ShapeDtypeStruct((WEIGHT_ROWS, HID), F32), row_out],
        in_specs=[pl.BlockSpec(memory_space=pltpu.SMEM)] + [hbm] * (len(data) + len(weights)),
        out_specs=[hbm, hbm],
        scratch_shapes=[pltpu.SemaphoreType.DMA((14,)), pltpu.SemaphoreType.DMA((5,))]
        + held
        + [pltpu.VMEM((WEIGHT_ROWS - SMALL_ROW, HID), F32), pltpu.VMEM(row_out.shape, F32)],
        compiler_params=pltpu.CompilerParams(vmem_limit_bytes=VMEM_LIMIT),
        name="messages",
    )(counts, *data, *weights)


def weight_pairs(sources, targets):
    heads = list(zip(sources[:2], targets[:2]))
    parts = [slice(SMALL_ROW, WEIGHT_ROWS)]
    parts += [slice(net * HID, (net + 1) * HID) for net in (CRITIC, TARGET, TRUNK)]
    return heads + [
        (source.at[part, :], target.at[part, :])
        for part in parts
        for source, target in zip(sources[2:], targets[2:])
    ]


def main_kernel(size, count_ref, *refs):
    sources, outs, (arrive, leave, *refs) = refs[:9], refs[9:11], refs[11:]
    buffers, sums, scratch = refs[:9], refs[9:11], refs[11:]
    states, next_states, actions, rewards, finished = buffers[:5]
    pairs = weight_pairs(sources[5:], buffers[5:]) + list(zip(sources[:5], buffers[:5]))
    copies = load(pairs, arrive)

    def line(ref, start, width):
        return jnp.concatenate(
            [ref[pl.ds(start // 128 + part, 1), :] for part in range(width // 128)], axis=1
        )

    def rows_of(start, width):
        at = pl.ds(start, width)
        return (
            states[:, at], next_states[:, at], actions[:, at],
            line(rewards, start, width), line(finished, start, width).astype(F32),
        )

    here = plan(count_ref, size, states.shape[1])
    gradients(
        here["group"], here["own_start"], here["own_count"], here["used"], rows_of, copies, False,
        outs, leave, *buffers[5:], *sums, *scratch,
    )


def moved_kernel(size, packed_ref, *refs):
    inputs, outs, (arrive, leave, *refs) = refs[:6], refs[6:8], refs[8:]
    meta_part, packed, *buffers = refs[:6]
    sums, scratch = refs[6:8], refs[8:]

    def add(start, count, used):
        pairs = weight_pairs(inputs[2:], buffers)
        pairs += [(packed_ref, packed)] + list(zip(inputs[:2], sums))
        copies = load(pairs, arrive)

        def rows_of(start, width):
            at = pl.ds(start, width)
            return (
                packed[:OBS, at], packed[NEXT_ROW : NEXT_ROW + OBS, at], packed[OBS:META_ROW, at],
                packed[NEXT_ROW + OBS : NEXT_ROW + OBS + 1, at], packed[PACK_ROWS - 1 : PACK_ROWS, at],
            )

        gradients(
            lax.axis_index("net"), start, count, used, rows_of, copies, True, outs, leave,
            *buffers, *sums, *scratch,
        )

    @pl.when(2 * lax.axis_index("batch") < size)
    def _():
        copy = pltpu.make_async_copy(
            packed_ref.at[META_ROW - 7 : META_ROW + 1, :128], meta_part, arrive.at[0]
        )
        copy.start()
        copy.wait()
        meta = meta_part[7:8, :]
        place = lax.broadcasted_iota(jnp.int32, (1, 128), 1)
        start, count, used = (
            jnp.sum(jnp.where(place == k, meta, 0.0)).astype(jnp.int32) for k in range(3)
        )
        pl.when(count > 0)(lambda: add(start, count, used))


def gradients(
    group, start_unit, unit_count, used, rows_of, copies, adding, outs, leave,
    head_weight, head_vector, own, other, out_own, out_other, *scratch
):
    (
        first, second, back, bias_two, out_weight, head_pack, head_back, head_bias,
        acc_second, acc_first, acc_bias, acc_out, acc_head, acc_rows,
    ) = scratch

    def await_next(count):
        for _ in range(count):
            copies.pop(0).wait()

    copies = list(copies)
    await_next(4)

    head_columns = jnp.concatenate([head_weight[...], jnp.zeros((1, HID), F32)], axis=0)
    value_row = head_columns[0:1]
    action_rows = jnp.concatenate(
        [head_columns[1:7], jnp.zeros((2, HID), F32)], axis=0
    )
    row_high, row_low = split(jnp.concatenate([action_rows, jnp.zeros((8, HID), F32)], axis=0))
    head_pack[...] = jnp.concatenate([row_high, row_low], axis=0)
    mean_columns = jnp.transpose(
        jnp.concatenate([action_rows * 0.5, jnp.zeros((120, HID), F32)], axis=0)
    )[:, :16]
    mean_high, mean_low = split(mean_columns)
    head_back[...] = jnp.concatenate(
        [mean_high, mean_low, mean_high], axis=1
    )
    bias_column = jnp.transpose(
        jnp.concatenate(
            [
                jnp.concatenate([head_vector[...], jnp.zeros((1, 128 - 13), F32)], axis=1),
                jnp.zeros((127, 128), F32),
            ],
            axis=0,
        )
    )[:16, 0:1]
    head_bias[...] = jnp.broadcast_to(bias_column, (16, 128))

    is_value = group == 0

    def prepare(slot, net, take, out_row, with_back):
        row = SMALL_ROW + 32 * net
        packed = take(row, 24) * 0.5
        high = packed.astype(BF16).astype(F32)
        stack = jnp.concatenate(
            [high, high, packed - high, jnp.zeros((128 - 72, HID), F32)], axis=0
        )
        first[slot] = jnp.transpose(stack).astype(BF16)
        matrix = take(net * HID, HID)
        second[slot] = left_parts(jnp.transpose(matrix) * 0.5)
        bias_two[slot] = column(take(row + 24, 1) * 0.5)
        if out_row is not None:
            out_weight[slot] = column(out_row)
        if with_back:
            back[slot] = left_parts(matrix * (0.25 * out_row if out_row is not None else 0.5))

    def picked(first_ref, second_ref):
        return lambda row, count: jnp.where(
            is_value, first_ref[row : row + count, :], second_ref[row : row + count, :]
        )

    def small(ref, net, row):
        return ref[SMALL_ROW + 32 * net + 24 + row : SMALL_ROW + 32 * net + 25 + row, :]

    for slot, ref, net in (
        (2, own, CRITIC), (3, other, CRITIC), (4, own, TARGET), (5, other, TARGET),
    ):
        if slot % 2 == 0:
            await_next(2)
        take = lambda row, count, ref=ref: ref[row : row + count, :]
        prepare(slot, net, take, small(ref, net, 1), slot < 4)
    await_next(2)
    prepare(0, TRUNK, picked(own, other), value_row, True)
    prepare(1, TRUNK, picked(other, own), None, True)
    target_bias = [small(ref, TARGET, 2)[:, :1] for ref in (own, other)]
    critic_bias = [small(ref, CRITIC, 2)[:, :1] for ref in (own, other)]
    value_bias = head_vector[0:1, 0:1]

    acc_second[...] = jnp.zeros_like(acc_second)
    acc_first[...] = jnp.zeros_like(acc_first)
    acc_bias[...] = jnp.zeros_like(acc_bias)
    acc_out[...] = jnp.zeros_like(acc_out)
    acc_head[...] = jnp.zeros_like(acc_head)
    acc_rows[...] = jnp.zeros_like(acc_rows)

    def chains(start, width):
        start = pl.multiple_of(start, UNIT)
        states_t, next_t, actions_t, reward, done = rows_of(start, width)
        ones = jnp.ones((1, width), F32)
        place = start + lax.broadcasted_iota(jnp.int32, (1, width), 1)

        def wide(value):
            return jnp.concatenate([value] * (width // 128), axis=1)

        valid = (place < used).astype(F32)

        def pack(rows):
            full = jnp.concatenate([rows, actions_t, ones], axis=0)
            high = full.astype(BF16).astype(F32)
            low = full - high
            return jnp.concatenate(
                [high, low, high, jnp.zeros((128 - 72, width), F32)], axis=0
            ).astype(BF16)

        pairs = pack(states_t)
        pairs_next = pack(next_t)

        def product(ref, slot, high, low):
            both = dot(ref[slot], high)
            return both[:HID] + both[HID:] + dot(ref[slot, :HID], low)

        def layer(half):
            t = jnp.tanh(half)
            u = t + 1.0
            a = half * u
            return a, t, u

        def forward(slot, inputs, keep):
            half = dot(first[slot], inputs)
            yield
            a_one, t, u = layer(half)
            slope_one = u + a_one * (1.0 - t) if keep else None
            parts = split(a_one)
            yield
            z = product(second, slot, parts[0], parts[1])
            yield
            a_two, t, u = layer(z + wide(bias_two[slot]))
            slope_two = u + a_two * (1.0 - t) if keep else None
            return parts, slope_one, a_two, slope_two

        def weighted(slot, hidden):
            return jnp.sum(hidden * wide(out_weight[slot]), axis=0, keepdims=True)

        def backward(slot, parts, slope_one, delta_two):
            acc_bias[slot] += fold(delta_two)
            high, low = split(delta_two)
            yield
            delta_one = product(back, slot, high, low)
            acc_second[slot] += dot(
                jnp.concatenate([parts[0], parts[1], parts[0]], axis=1),
                jnp.concatenate([high, high, low], axis=1),
                NT,
            )
            yield
            high, low = split(delta_one * slope_one)
            yield
            rows = pairs[:48]
            acc_first[slot] += dot(
                jnp.concatenate([rows, rows], axis=1), jnp.concatenate([high, low], axis=1), NT
            )

        known = {}

        def next_chain():
            _, _, hidden, _ = yield from forward(0, pairs_next, False)
            value_next = weighted(0, hidden) + value_bias
            known["goal"] = reward + DISCOUNT * (1.0 - done) * value_next

        def target_chain(member):
            _, _, hidden, _ = yield from forward(4 + member, pairs, False)
            known["target", member] = weighted(4 + member, hidden) + target_bias[member]

        def critic_chain(member):
            slot = 2 + member
            parts, slope_one, hidden, slope_two = yield from forward(slot, pairs, True)
            error = (weighted(slot, hidden) + critic_bias[member] - known["goal"]) * valid
            grad = 2.0 * error
            known["critic", member] = (error * error, grad)
            acc_out[slot] += fold(hidden * grad)
            yield from backward(slot, parts, slope_one, slope_two * grad)

        def value_chain():
            parts, slope_one, hidden, slope_two = yield from forward(0, pairs, True)
            target_min = jnp.minimum(known["target", 0], known["target", 1])
            gap = target_min - (weighted(0, hidden) + value_bias)
            expect = jnp.where(gap < 0.0, 1.0 - EXPECTILE, EXPECTILE) * valid
            grad = -2.0 * expect * gap
            known["gap"] = gap
            known["value"] = (grad, expect * gap * gap)
            acc_out[0] += fold(hidden * grad)
            yield from backward(0, parts, slope_one, slope_two * grad)

        def actor_chain():
            parts, slope_one, hidden, slope_two = yield from forward(1, pairs, True)
            hidden_high, hidden_low = split(hidden)
            both = dot(head_pack[...], hidden_high)
            head = both[:8] + both[16:24] + dot(head_pack[:16], hidden_low)[:8]
            yield
            bias = wide(head_bias[...])
            mean = jnp.tanh(head[:6] + bias[1:7])
            log_std = bias[7:13]
            inverse = jnp.exp(-log_std)
            scaled = (actions_t - mean) * inverse
            log_prob = jnp.sum(
                -0.5 * scaled * scaled - log_std - 0.5 * LOG_TWO_PI, axis=0, keepdims=True
            )
            weight = jnp.minimum(jnp.exp(BETA_TEMP * known["gap"]), WEIGHT_CLIP) * valid
            grad_mean = -weight * scaled * inverse * (1.0 - mean * mean)
            grad_std = -weight * (scaled * scaled - 1.0)
            known["actor"] = (grad_mean, grad_std, -weight * log_prob)
            grads = jnp.concatenate([grad_mean, jnp.zeros((10, width), F32)], axis=0)
            grads_high, grads_low = split(grads)
            acc_head[...] += dot(jnp.concatenate([grads_high, grads_low], axis=0), hidden_high, NT)
            acc_head[:16] += dot(grads_high, hidden_low, NT)
            up = dot(
                head_back[...], jnp.concatenate([grads_high, grads_high, grads_low], axis=0)
            )
            yield
            yield from backward(1, parts, slope_one, up * slope_two)

        def finish():
            rows = jnp.concatenate(
                [known["value"][0], known["actor"][0], known["actor"][1], known["value"][1]]
                + [known["critic", 0][0], known["critic", 1][0], known["actor"][2], valid]
                + [known["critic", 0][1], known["critic", 1][1]]
                + [jnp.zeros((4, width), F32)],
                axis=0,
            )
            acc_rows[...] += fold(rows)

        return [
            next_chain(), target_chain(0), target_chain(1), critic_chain(0), value_chain(),
            actor_chain(), critic_chain(1),
        ], finish

    def tiles(starts, width=TILE):
        parts = [chains(start, width) for start in starts]
        waiting = [(chain, part) for part in parts for chain in part[0]]
        left = {id(part): len(part[0]) for part in parts}
        active = []
        while waiting or active:
            while waiting and len(active) < WIDTH:
                active.append(waiting.pop(0))
            for entry in list(active):
                chain, part = entry
                try:
                    next(chain)
                except StopIteration:
                    active.remove(entry)
                    left[id(part)] -= 1
                    if left[id(part)] == 0:
                        part[1]()

    base = start_unit * UNIT
    tile_count = unit_count * UNIT // TILE

    def several(i, carry):
        tiles([base + (UNROLL * i + k) * TILE for k in range(UNROLL)])
        return carry

    def single(i, carry):
        tiles([base + i * TILE])
        return carry

    await_next(len(copies) - (2 if adding else 0))
    rounds = tile_count // UNROLL
    lax.fori_loop(0, rounds, several, 0)
    lax.fori_loop(rounds * UNROLL, tile_count, single, 0)

    @pl.when(unit_count * UNIT > tile_count * TILE)
    def _():
        tiles([base + tile_count * TILE], UNIT)


    def store(out, row, value):
        count = value.shape[0]
        for half in range(2):
            at = slice(half * PAYLOAD + row, half * PAYLOAD + row + count)
            part = value[:, half * 128 : half * 128 + 128]
            out[at, :] = part + out[at, :] if adding else part

    def first_grad(slot):
        return acc_first[slot, :24] + acc_first[slot, 24:]

    def lanes(value):
        return jnp.sum(jnp.transpose(value), axis=0, keepdims=True)

    zero_row = jnp.zeros((1, HID), F32)
    row_sums = jnp.sum(
        jnp.transpose(jnp.concatenate([acc_rows[...], jnp.zeros((104, 128), F32)], axis=0)),
        axis=0,
        keepdims=True,
    )
    lane = lax.broadcasted_iota(jnp.int32, (1, 128), 1)
    swapped = jnp.where(
        lane == 14,
        pltpu.roll(row_sums, 127, 1),
        jnp.where(lane == 15, pltpu.roll(row_sums, 1, 1), row_sums),
    )
    shared_row = jnp.where(is_value, row_sums, swapped)
    head_actions = acc_head[:6] + acc_head[16:22]
    head_rows = jnp.concatenate([lanes(acc_out[0]), head_actions, zero_row], axis=0)
    out_rows = (
        value_row * 0.5, None, small(own, CRITIC, 1) * 0.5, small(other, CRITIC, 1) * 0.5,
    )

    def second_grad(slot):
        matrix, bias = acc_second[slot], lanes(acc_bias[slot])
        scale = out_rows[slot]
        return (matrix, bias) if scale is None else (matrix * scale, bias * scale)

    sent = []

    def send(row, count):
        for out, target in zip((out_own, out_other), outs):
            for half in range(2):
                at = slice(half * PAYLOAD + row, half * PAYLOAD + row + count)
                sent.append(
                    pltpu.make_async_copy(out.at[at, :], target.at[at, :], leave.at[len(sent)])
                )
                sent[-1].start()

    await_next(len(copies))
    trunk = [second_grad(slot) + (first_grad(slot),) for slot in range(2)]
    critic = [second_grad(2 + which) for which in range(2)]
    mixed = [
        [jnp.where(is_value, trunk[which][k], trunk[1 - which][k]) for k in range(3)]
        for which in range(2)
    ]
    for which, out in enumerate((out_own, out_other)):
        store(out, 0, mixed[which][0])
    send(0, HID)
    for which, out in enumerate((out_own, out_other)):
        store(out, HID, critic[which][0])
    send(HID, HID)
    for which, out in enumerate((out_own, out_other)):
        store(out, ROW_TRUNK, mixed[which][2])
        store(out, ROW_CRITIC, first_grad(2 + which))
        bias_grad = pltpu.roll(row_sums, 128 - 18 - which, 1)
        last = jnp.concatenate([shared_row, jnp.where(lane == 0, bias_grad, 0.0)], axis=1)
        store(
            out,
            ROW_VECTOR,
            jnp.concatenate(
                [mixed[which][1], critic[which][1], lanes(acc_out[2 + which]), last]
                + [zero_row] * 4,
                axis=0,
            ),
        )
        store(out, ROW_HEAD, head_rows)
    send(2 * HID, PAYLOAD - 2 * HID)
    for copy in sent:
        copy.wait()


def run_main(data, heads, weights, counts=None):
    hbm = pl.BlockSpec(memory_space=pl.ANY)
    size = lax.axis_size("batch")
    operands = (*data, *heads, *weights)
    payload = jax.ShapeDtypeStruct((2 * PAYLOAD, 128), F32)
    held = [pltpu.VMEM(array.shape, array.dtype) for array in (*heads, *weights)]
    semaphores = [pltpu.SemaphoreType.DMA((16,)), pltpu.SemaphoreType.DMA((12,))]
    if counts is None:
        name, body, specs, aliases = "moved_gradients", moved_kernel, [], {1: 0, 2: 1}
        buffers = [pltpu.VMEM((8, 128), F32), pltpu.VMEM(data[0].shape, F32)] + held
    else:
        name, body, aliases = "gradients", main_kernel, {}
        specs = [pl.BlockSpec(memory_space=pltpu.SMEM)]
        buffers = [pltpu.VMEM(array.shape, array.dtype) for array in data] + held
        operands = (counts,) + operands
    return pl.pallas_call(
        functools.partial(body, size),
        out_shape=[payload, payload],
        in_specs=specs + [hbm] * (len(operands) - len(specs)),
        out_specs=[hbm, hbm],
        input_output_aliases=aliases,
        scratch_shapes=semaphores + buffers + [pltpu.VMEM(payload.shape, F32)] * 2 + [
            pltpu.VMEM((6, HID, 128), BF16),
            pltpu.VMEM((6, 2 * HID, HID), BF16),
            pltpu.VMEM((4, 2 * HID, HID), BF16),
            pltpu.VMEM((6, HID, 128), F32),
            pltpu.VMEM((6, HID, 128), F32),
            pltpu.VMEM((32, HID), BF16),
            pltpu.VMEM((HID, 48), BF16),
            pltpu.VMEM((16, 128), F32),
            pltpu.VMEM((4, HID, HID), F32),
            pltpu.VMEM((4, 48, HID), F32),
            pltpu.VMEM((4, HID, 128), F32),
            pltpu.VMEM((4, HID, 128), F32),
            pltpu.VMEM((32, HID), F32),
            pltpu.VMEM((24, 128), F32),
        ],
        compiler_params=pltpu.CompilerParams(vmem_limit_bytes=VMEM_LIMIT),
        cost_estimate=pl.CostEstimate(
            flops=10**10, bytes_accessed=5 * 10**6, transcendentals=10**7
        ),
        name=name,
    )(*operands)


def read(ref):
    if len(ref.shape) == 2:
        return ref[...]
    return ref[:, 0, :] if ref.shape[1] == 1 else ref[0]


def write(ref, value):
    if len(ref.shape) == 2:
        ref[...] = value
    elif ref.shape[1] == 1:
        ref[:, 0, :] = value
    else:
        ref[0] = value


def lamb_kernel(*refs):
    count = 1 + 3 * len(NAMES) + 3
    sources, targets_out, buffers = refs[:count], refs[count : count + 29], refs[count + 29 :]
    inputs, outs = buffers[:count], buffers[count : count + 29]
    steps, arrive, leave = buffers[count + 29 :]
    copies = [
        pltpu.make_async_copy(source, target, arrive.at[k])
        for k, (source, target) in enumerate(zip(sources, inputs))
    ]
    stages = ([0, 4, 5, 6], [19, 20, 21], [1, 2, 3, *range(7, 19), *range(22, count)])
    for stage in stages:
        for k in stage:
            copies[k].start()
    for k in stages[0]:
        copies[k].wait()
    sent = []

    def send(places):
        for at in places:
            copy = pltpu.make_async_copy(outs[at], targets_out[at], leave.at[at])
            copy.start()
            sent.append(copy)

    payload = inputs[0]
    params = [inputs[1 + 3 * i : 4 + 3 * i] for i in range(len(NAMES))]
    targets = inputs[count - 3 :]

    def rows(start, count):
        return jnp.concatenate(
            [payload[start : start + count, :], payload[PAYLOAD + start : PAYLOAD + start + count, :]],
            axis=1,
        )

    trunk_first = rows(ROW_TRUNK, 24)
    critic_first = rows(ROW_CRITIC, 24)
    vectors = rows(ROW_VECTOR, 8)
    head = rows(ROW_HEAD, 8)
    shared = vectors[3:4, :128]
    after = 1.0 / shared[:, 17:18]
    gradients = (
        trunk_first[:OBS],
        None,
        jnp.concatenate([trunk_first[23:24], vectors[0:1]], axis=1),
        head[:7],
        shared[:, :13],
        critic_first[: OBS + ACT],
        None,
        jnp.concatenate(
            [critic_first[23:24], vectors[1:2], vectors[2:3], vectors[3:4, 128:129]], axis=1
        ),
    )
    def moments(weight, gradient, mean_old, square_old):
        mean_new = DECAY_FIRST * mean_old + (1.0 - DECAY_FIRST) * gradient
        square_new = DECAY_SECOND * square_old + (1.0 - DECAY_SECOND) * gradient * gradient
        mean_hat = mean_new * (1.0 / (1.0 - DECAY_FIRST**STEP))
        square_hat = square_new * (1.0 / (1.0 - DECAY_SECOND**STEP))
        update = mean_hat / (jnp.sqrt(square_hat) + EPSILON) + WEIGHT_DECAY * weight
        return mean_new, square_new, update

    def total(value):
        return jnp.sum(jnp.sum(value * value, axis=0, keepdims=True), axis=1, keepdims=True)

    norms = {}
    updates = {}
    for i in (1, 6, 0, 2, 3, 4, 5, 7):
        if i in (6, 0):
            for k in stages[1 if i == 6 else 2]:
                copies[k].wait()
        weight_ref, mean_ref, square_ref = params[i]
        if i in (1, 6):
            weight_sum, update_sum = jnp.zeros((8, HID), F32), jnp.zeros((8, HID), F32)
            for band in range(0, HID, BAND):
                at = slice(band, band + BAND)
                weight = weight_ref[0, at, :]
                gradient = rows((0 if i == 1 else HID) + band, BAND) * after
                mean_new, square_new, update = moments(
                    weight, gradient, mean_ref[0, at, :], square_ref[0, at, :]
                )
                outs[8 + i][0, at, :] = mean_new
                outs[16 + i][0, at, :] = square_new
                steps[0 if i == 1 else 1, at, :] = update
                for k in range(0, BAND, 8):
                    weight_sum += weight[k : k + 8] * weight[k : k + 8]
                    update_sum += update[k : k + 8] * update[k : k + 8]
            over = lambda part: jnp.sum(
                jnp.sum(part, axis=0, keepdims=True), axis=1, keepdims=True
            )
            norms[i] = (jnp.sqrt(over(weight_sum)), jnp.sqrt(over(update_sum)))
            send((8 + i, 16 + i))
        else:
            weight = read(weight_ref)
            mean_new, square_new, updates[i] = moments(
                weight, gradients[i] * after, read(mean_ref), read(square_ref)
            )
            write(outs[8 + i], mean_new)
            write(outs[16 + i], square_new)
            norms[i] = (jnp.sqrt(total(weight)), jnp.sqrt(total(updates[i])))
    send([8 + k + i for i in (0, 2, 3, 4, 5, 7) for k in (0, 8)])
    for i, name in enumerate(NAMES):
        scale = LEARN_RATE * (norms[i][0] / norms[i][1])
        if i in (1, 6):
            for band in range(0, HID, BAND):
                at = slice(band, band + BAND)
                new = params[i][0][0, at, :] - scale * steps[0 if i == 1 else 1, at, :]
                outs[i][0, at, :] = new
                if i == 6:
                    outs[25][0, at, :] = (
                        (1.0 - TARGET_RATE) * targets[1][0, at, :] + TARGET_RATE * new
                    )
        else:
            new = read(params[i][0]) - scale * updates[i]
            write(outs[i], new)
            if i >= 5:
                write(
                    outs[19 + i], (1.0 - TARGET_RATE) * read(targets[i - 5]) + TARGET_RATE * new
                )
    lane = lax.broadcasted_iota(jnp.int32, (1, 8), 1)
    for row in range(2):
        line = jnp.zeros((1, 8), F32)
        for i, pair in norms.items():
            line = jnp.where(lane == i, pair[row], line)
        outs[27][0, row : row + 1, :] = line
    outs[28][...] = pltpu.roll(shared, 128 - 13, 1)[:, :5]
    send([*range(8), *range(24, 29)])
    for copy in sent:
        copy.wait()


NAMES = (
    "trunk_input", "trunk_middle", "trunk_vector", "head_weight", "head_vector",
    "critic_input", "critic_middle", "critic_vector",
)


def run_lamb(payload, params, targets):
    hbm = pl.BlockSpec(memory_space=pl.ANY)
    flat = [array for triple in params for array in triple]
    shapes = [jax.ShapeDtypeStruct(triple[0].shape, F32) for triple in params]
    outs = shapes * 3 + [jax.ShapeDtypeStruct(t.shape, F32) for t in targets]
    outs += [jax.ShapeDtypeStruct((1, 2, 8), F32), jax.ShapeDtypeStruct((1, 5), F32)]
    operands = (payload, *flat, *targets)
    return pl.pallas_call(
        lamb_kernel,
        out_shape=outs,
        in_specs=[hbm] * len(operands),
        out_specs=[hbm] * len(outs),
        scratch_shapes=[pltpu.VMEM(array.shape, array.dtype) for array in (*operands, *outs)]
        + [
            pltpu.VMEM((2, HID, HID), F32),
            pltpu.SemaphoreType.DMA((len(operands),)),
            pltpu.SemaphoreType.DMA((len(outs),)),
        ],
        compiler_params=pltpu.CompilerParams(vmem_limit_bytes=VMEM_LIMIT),
        name="update",
    )(*operands)


def across(value):
    size = lax.axis_size("net")
    return lax.ppermute(value, "net", [(i, size - 1 - i) for i in range(size)])


def summed(value):
    size = lax.axis_size("batch")
    if size % 2:
        return lax.psum(value, "batch")
    half = size // 2
    groups = [list(range(half)), list(range(half, size))]
    rows = value.shape[0]
    each = -(-rows // half)
    if each * half != rows:
        value = jnp.concatenate([value, jnp.zeros((each * half - rows, 128), F32)], axis=0)
    pieces = lax.all_to_all(
        value.reshape(half, each, 128), "batch", 0, 0, axis_index_groups=groups, tiled=True
    )
    mine = jnp.sum(pieces, axis=0)
    mine = mine + lax.ppermute(
        mine, "batch", [pair for a, b in zip(*groups) for pair in ((a, b), (b, a))]
    )
    full = lax.all_to_all(
        jnp.broadcast_to(mine[None], (half, each, 128)), "batch", 0, 0,
        axis_index_groups=groups, tiled=True,
    )
    return full.reshape(each * half, 128)[:rows]


def shards(
    states, next_states, actions, rewards, finished, valid_counts,
    trunk_input, trunk_middle, trunk_vector, head_weight, head_vector,
    critic_input, critic_middle, critic_vector,
    target_input, target_middle, target_vector,
    mean_trunk_input, square_trunk_input, mean_trunk_middle, square_trunk_middle,
    mean_trunk_vector, square_trunk_vector, mean_head_weight, square_head_weight,
    mean_head_vector, square_head_vector, mean_critic_input, square_critic_input,
    mean_critic_middle, square_critic_middle, mean_critic_vector, square_critic_vector,
):
    def turned(array):
        if array.ndim == 3 and array.shape[1] != HID:
            return jnp.transpose(array, (1, 0, 2))
        if array.ndim == 2 and array.shape[0] == HID:
            return array.T
        return array.reshape(1, -1) if array.ndim == 1 else array

    def back(array, like):
        if like.ndim == 3 and like.shape[1] != HID:
            return jnp.transpose(array, (1, 0, 2))
        if like.ndim == 2 and like.shape[0] == HID:
            return array.T
        return array.reshape(like.shape)

    params = [
        tuple(turned(array) for array in triple)
        for triple in (
            (trunk_input, mean_trunk_input, square_trunk_input),
            (trunk_middle, mean_trunk_middle, square_trunk_middle),
            (trunk_vector, mean_trunk_vector, square_trunk_vector),
            (head_weight, mean_head_weight, square_head_weight),
            (head_vector, mean_head_vector, square_head_vector),
            (critic_input, mean_critic_input, square_critic_input),
            (critic_middle, mean_critic_middle, square_critic_middle),
            (critic_vector, mean_critic_vector, square_critic_vector),
        )
    ]
    targets = tuple(turned(array) for array in (target_input, target_middle, target_vector))
    own = tuple(params[i][0] for i in (0, 1, 2, 5, 6, 7)) + targets
    lines = (states.shape[1] // 128, 128)
    data = (states, next_states, actions, rewards.reshape(lines), finished.reshape(lines))
    heads = (params[3][0], params[4][0])
    weights, message = run_pack(valid_counts, data, own)
    size = lax.axis_size("batch")
    both = (weights, across(weights))
    arrived = lax.ppermute(message, "batch", [(i, size - 1 - i) for i in range(size // 2, size)])
    own_part, other_part = run_main(data, heads, both, valid_counts)
    own_part, other_part = run_main((arrived, own_part, other_part), heads, both)
    results = list(run_lamb(summed(own_part + across(other_part)), params, targets))
    likes = (
        trunk_input, trunk_middle, trunk_vector, head_weight, head_vector,
        critic_input, critic_middle, critic_vector,
    ) * 3 + (target_input, target_middle, target_vector)
    final = [back(array, like) for array, like in zip(results, likes)]
    return tuple(final) + (jnp.transpose(results[27], (0, 2, 1)), results[28].reshape(5))


def solution(mesh):
    rows, matrix, vector, none = P(None, "batch"), P("net", None, None), P("net", None), P()
    line = P("batch")
    params = (matrix, matrix, vector, none, none, matrix, matrix, vector)
    moments = tuple(spec for entry in params for spec in (entry, entry))
    target = (matrix, matrix, vector)
    return jax.shard_map(
        shards,
        mesh=mesh,
        in_specs=(rows, rows, rows, line, line, line) + params + target + moments,
        out_specs=params * 3 + target + (matrix, none),
        check_vma=False,
    )
```

```python
import functools
import math

import jax
import jax.numpy as jnp
from jax import lax
from jax.experimental import pallas as pl
from jax.experimental.pallas import tpu as pltpu
from jax.sharding import PartitionSpec as P

STEP = 10
EXPECTILE = 0.7
DISCOUNT = 0.99
BETA_TEMP = 3.0
WEIGHT_CLIP = 100.0
DECAY_FIRST = 0.9
DECAY_SECOND = 0.999
EPSILON = 1e-06
WEIGHT_DECAY = 0.01
LEARN_RATE = 0.3
TARGET_RATE = 0.005
BAND = 32
LOG_TWO_PI = math.log(2.0 * math.pi)

OBS = 17
ACT = 6
HID = 256
TILE = 256
WIDTH = 7
UNROLL = 3
UNIT = 128
ROW_TRUNK = 2 * HID
ROW_CRITIC = ROW_TRUNK + 24
ROW_VECTOR = ROW_CRITIC + 24
ROW_HEAD = ROW_VECTOR + 8
PAYLOAD = ROW_HEAD + 8
VMEM_LIMIT = 64 * 2**20 - 2**17

META_ROW = OBS + ACT
NEXT_ROW = META_ROW + 1
PACK_ROWS = NEXT_ROW + OBS + 2
TRUNK, CRITIC, TARGET = range(3)
SMALL_ROW = 3 * HID
WEIGHT_ROWS = SMALL_ROW + 3 * 32
EXTRA_ROWS = 512
HEAD_START = 0

F32 = jnp.float32
BF16 = jnp.bfloat16
NN = (((1,), (0,)), ((), ()))
NT = (((1,), (1,)), ((), ()))


def split(value):
    high = value.astype(BF16)
    return high, (value - high.astype(F32)).astype(BF16)


def dot(left, right, dims=NN):
    return lax.dot_general(left, right, dims, preferred_element_type=F32)


def fold(value):
    total = value[:, :128]
    for start in range(128, value.shape[1], 128):
        total = total + value[:, start : start + 128]
    return total


def left_parts(value):
    return jnp.concatenate(split(value), axis=0)


def column(row):
    return jnp.transpose(jnp.broadcast_to(row, (128, row.shape[1])))


def room_of(row_total):
    total, least = row_total // UNIT, -(-(row_total // 3) // UNIT)
    return max(2, -(-(total - (total + least) // 2) // 2))


def plan(count_ref, size, row_total):
    group, index = lax.axis_index("net"), lax.axis_index("batch")
    used = count_ref[0]
    units = (used + UNIT - 1) // UNIT
    total, room, lowest = row_total // UNIT, room_of(row_total), row_total // 3
    guess = (
        lowest
        + (size - 1 - index) * (row_total - lowest - row_total // 8) // max(size - 1, 1)
        + row_total // 16
    )
    kept = (used + guess + EXTRA_ROWS + 2 * UNIT - 1) // (2 * UNIT)
    kept = jnp.minimum(jnp.maximum(kept, units - 2 * room), units)
    kept = jnp.where(units - kept < 4, units, kept)
    kept = jnp.where(2 * index >= size, kept, units)
    sent = units - kept
    first = (sent + 1) // 2
    mine = jnp.minimum((kept + HEAD_START) // 2, kept)
    leading = group == 0
    start = kept + jnp.where(leading, 0, first)
    return dict(
        group=group, used=used,
        own_start=jnp.where(leading, 0, mine), own_count=jnp.where(leading, mine, kept - mine),
        sent_start=start, sent_count=jnp.where(leading, first, sent - first),
        window=jnp.minimum(start, total - room),
    )


def load(pairs, sems):
    copies = [
        pltpu.make_async_copy(source, target, sems.at[k])
        for k, (source, target) in enumerate(pairs)
    ]
    for copy in copies:
        copy.start()
    return copies


def pack_kernel(size, row_total, count_ref, *refs):
    sources, (weight_out, row_out), (arrive, leave, *parts) = refs[:14], refs[14:16], refs[16:]
    state_part, next_part, action_part, rewards, finished = parts[:5]
    weights, (small_part, row_part) = parts[5:14], parts[14:]
    room = room_of(row_total)
    copies = load(list(zip(sources[5:], weights)) + list(zip(sources[3:5], parts[3:5])), arrive)
    here = plan(count_ref, size, row_total)
    at = pl.ds(pl.multiple_of(here["window"] * UNIT, UNIT), room * UNIT)
    for k in range(3):
        copies.append(
            pltpu.make_async_copy(sources[k].at[:, at], parts[k], arrive.at[len(copies)])
        )
        copies[-1].start()
    sent = []

    def send(source, target):
        sent.append(pltpu.make_async_copy(source, target, leave.at[len(sent)]))
        sent[-1].start()

    for net in range(3):
        copies[3 * net + 1].wait()
        send(weights[3 * net + 1].at[0], weight_out.at[net * HID : (net + 1) * HID, :])
    for net in range(3):
        copies[3 * net].wait()
        copies[3 * net + 2].wait()
        rows, _, vector = weights[3 * net : 3 * net + 3]
        row = 32 * net
        width = rows.shape[0]
        pieces = [rows[:, 0, :]]
        if width < META_ROW:
            pieces.append(jnp.zeros((META_ROW - width, HID), F32))
        pieces.append(vector[:, :HID])
        small_part[row : row + 24, :] = jnp.concatenate(pieces, axis=0)
        pieces = [vector[:, HID : 2 * HID]]
        if vector.shape[1] > 2 * HID:
            pieces.append(vector[:, 2 * HID : 3 * HID])
            pieces.append(jnp.broadcast_to(vector[:, 3 * HID : 3 * HID + 1], (1, HID)))
        pieces.append(jnp.zeros((8 - len(pieces), HID), F32))
        small_part[row + 24 : row + 32, :] = jnp.concatenate(pieces, axis=0)
    send(small_part, weight_out.at[SMALL_ROW:, :])

    def line(ref):
        first = here["window"] * (UNIT // 128)
        return jnp.concatenate(
            [ref[pl.ds(first + k, 1), :] for k in range(room * UNIT // 128)], axis=1
        )

    lane = lax.broadcasted_iota(jnp.int32, (1, room * UNIT), 1)
    meta = jnp.zeros((1, room * UNIT), F32)
    for k, number in enumerate(
        (
            here["sent_start"] - here["window"], here["sent_count"],
            here["used"] - here["window"] * UNIT,
        )
    ):
        meta = jnp.where(lane == k, number.astype(F32), meta)
    for copy in copies[9:]:
        copy.wait()
    row_part[: META_ROW + 1, :] = jnp.concatenate([state_part[...], action_part[...], meta], axis=0)
    row_part[NEXT_ROW:, :] = jnp.concatenate(
        [next_part[...], line(rewards), line(finished).astype(F32)], axis=0
    )
    send(row_part, row_out)
    for copy in sent:
        copy.wait()


def run_pack(counts, data, weights):
    hbm = pl.BlockSpec(memory_space=pl.ANY)
    row_total = data[0].shape[1]
    span = room_of(row_total) * UNIT
    row_out = jax.ShapeDtypeStruct((PACK_ROWS, span), F32)
    held = [pltpu.VMEM((array.shape[0], span), F32) for array in data[:3]]
    held += [pltpu.VMEM(array.shape, array.dtype) for array in (*data[3:], *weights)]
    return pl.pallas_call(
        functools.partial(pack_kernel, lax.axis_size("batch"), row_total),
        out_shape=[jax.ShapeDtypeStruct((WEIGHT_ROWS, HID), F32), row_out],
        in_specs=[pl.BlockSpec(memory_space=pltpu.SMEM)] + [hbm] * (len(data) + len(weights)),
        out_specs=[hbm, hbm],
        scratch_shapes=[pltpu.SemaphoreType.DMA((14,)), pltpu.SemaphoreType.DMA((5,))]
        + held
        + [pltpu.VMEM((WEIGHT_ROWS - SMALL_ROW, HID), F32), pltpu.VMEM(row_out.shape, F32)],
        compiler_params=pltpu.CompilerParams(vmem_limit_bytes=VMEM_LIMIT),
        name="messages",
    )(counts, *data, *weights)


def weight_pairs(sources, targets):
    heads = list(zip(sources[:2], targets[:2]))
    parts = [slice(SMALL_ROW, WEIGHT_ROWS)]
    parts += [slice(net * HID, (net + 1) * HID) for net in (CRITIC, TARGET, TRUNK)]
    return heads + [
        (source.at[part, :], target.at[part, :])
        for part in parts
        for source, target in zip(sources[2:], targets[2:])
    ]


def main_kernel(size, count_ref, *refs):
    sources, outs, (arrive, leave, *refs) = refs[:9], refs[9:11], refs[11:]
    buffers, sums, scratch = refs[:9], refs[9:11], refs[11:]
    states, next_states, actions, rewards, finished = buffers[:5]
    pairs = weight_pairs(sources[5:], buffers[5:]) + list(zip(sources[:5], buffers[:5]))
    copies = load(pairs, arrive)

    def line(ref, start, width):
        return jnp.concatenate(
            [ref[pl.ds(start // 128 + part, 1), :] for part in range(width // 128)], axis=1
        )

    def rows_of(start, width):
        at = pl.ds(start, width)
        return (
            states[:, at], next_states[:, at], actions[:, at],
            line(rewards, start, width), line(finished, start, width).astype(F32),
        )

    here = plan(count_ref, size, states.shape[1])
    gradients(
        here["group"], here["own_start"], here["own_count"], here["used"], rows_of, copies, False,
        outs, leave, *buffers[5:], *sums, *scratch,
    )


def moved_kernel(size, packed_ref, *refs):
    inputs, outs, (arrive, leave, *refs) = refs[:6], refs[6:8], refs[8:]
    meta_part, packed, *buffers = refs[:6]
    sums, scratch = refs[6:8], refs[8:]

    def add(start, count, used):
        pairs = weight_pairs(inputs[2:], buffers)
        pairs += [(packed_ref, packed)] + list(zip(inputs[:2], sums))
        copies = load(pairs, arrive)

        def rows_of(start, width):
            at = pl.ds(start, width)
            return (
                packed[:OBS, at], packed[NEXT_ROW : NEXT_ROW + OBS, at], packed[OBS:META_ROW, at],
                packed[NEXT_ROW + OBS : NEXT_ROW + OBS + 1, at], packed[PACK_ROWS - 1 : PACK_ROWS, at],
            )

        gradients(
            lax.axis_index("net"), start, count, used, rows_of, copies, True, outs, leave,
            *buffers, *sums, *scratch,
        )

    @pl.when(2 * lax.axis_index("batch") < size)
    def _():
        copy = pltpu.make_async_copy(
            packed_ref.at[META_ROW - 7 : META_ROW + 1, :128], meta_part, arrive.at[0]
        )
        copy.start()
        copy.wait()
        meta = meta_part[7:8, :]
        place = lax.broadcasted_iota(jnp.int32, (1, 128), 1)
        start, count, used = (
            jnp.sum(jnp.where(place == k, meta, 0.0)).astype(jnp.int32) for k in range(3)
        )
        pl.when(count > 0)(lambda: add(start, count, used))


def gradients(
    group, start_unit, unit_count, used, rows_of, copies, adding, outs, leave,
    head_weight, head_vector, own, other, out_own, out_other, *scratch
):
    (
        first, second, back, bias_two, out_weight, head_pack, head_back, head_bias,
        acc_second, acc_first, acc_bias, acc_out, acc_head, acc_rows,
    ) = scratch

    def await_next(count):
        for _ in range(count):
            copies.pop(0).wait()

    copies = list(copies)
    await_next(4)

    head_columns = jnp.concatenate([head_weight[...], jnp.zeros((1, HID), F32)], axis=0)
    value_row = head_columns[0:1]
    action_rows = jnp.concatenate(
        [head_columns[1:7], jnp.zeros((2, HID), F32)], axis=0
    )
    row_high, row_low = split(jnp.concatenate([action_rows, jnp.zeros((8, HID), F32)], axis=0))
    head_pack[...] = jnp.concatenate([row_high, row_low], axis=0)
    mean_columns = jnp.transpose(
        jnp.concatenate([action_rows * 0.5, jnp.zeros((120, HID), F32)], axis=0)
    )[:, :16]
    mean_high, mean_low = split(mean_columns)
    head_back[...] = jnp.concatenate(
        [mean_high, mean_low, mean_high], axis=1
    )
    bias_column = jnp.transpose(
        jnp.concatenate(
            [
                jnp.concatenate([head_vector[...], jnp.zeros((1, 128 - 13), F32)], axis=1),
                jnp.zeros((127, 128), F32),
            ],
            axis=0,
        )
    )[:16, 0:1]
    head_bias[...] = jnp.broadcast_to(bias_column, (16, 128))

    is_value = group == 0

    def prepare(slot, net, take, out_row, with_back):
        row = SMALL_ROW + 32 * net
        packed = take(row, 24) * 0.5
        high = packed.astype(BF16).astype(F32)
        stack = jnp.concatenate(
            [high, high, packed - high, jnp.zeros((128 - 72, HID), F32)], axis=0
        )
        first[slot] = jnp.transpose(stack).astype(BF16)
        matrix = take(net * HID, HID)
        second[slot] = left_parts(jnp.transpose(matrix) * 0.5)
        bias_two[slot] = column(take(row + 24, 1) * 0.5)
        if out_row is not None:
            out_weight[slot] = column(out_row)
        if with_back:
            back[slot] = left_parts(matrix * (0.25 * out_row if out_row is not None else 0.5))

    def picked(first_ref, second_ref):
        return lambda row, count: jnp.where(
            is_value, first_ref[row : row + count, :], second_ref[row : row + count, :]
        )

    def small(ref, net, row):
        return ref[SMALL_ROW + 32 * net + 24 + row : SMALL_ROW + 32 * net + 25 + row, :]

    for slot, ref, net in (
        (2, own, CRITIC), (3, other, CRITIC), (4, own, TARGET), (5, other, TARGET),
    ):
        if slot % 2 == 0:
            await_next(2)
        take = lambda row, count, ref=ref: ref[row : row + count, :]
        prepare(slot, net, take, small(ref, net, 1), slot < 4)
    await_next(2)
    prepare(0, TRUNK, picked(own, other), value_row, True)
    prepare(1, TRUNK, picked(other, own), None, True)
    target_bias = [small(ref, TARGET, 2)[:, :1] for ref in (own, other)]
    critic_bias = [small(ref, CRITIC, 2)[:, :1] for ref in (own, other)]
    value_bias = head_vector[0:1, 0:1]

    acc_second[...] = jnp.zeros_like(acc_second)
    acc_first[...] = jnp.zeros_like(acc_first)
    acc_bias[...] = jnp.zeros_like(acc_bias)
    acc_out[...] = jnp.zeros_like(acc_out)
    acc_head[...] = jnp.zeros_like(acc_head)
    acc_rows[...] = jnp.zeros_like(acc_rows)

    def chains(start, width):
        start = pl.multiple_of(start, UNIT)
        states_t, next_t, actions_t, reward, done = rows_of(start, width)
        ones = jnp.ones((1, width), F32)
        place = start + lax.broadcasted_iota(jnp.int32, (1, width), 1)

        def wide(value):
            return jnp.concatenate([value] * (width // 128), axis=1)

        valid = (place < used).astype(F32)

        def pack(rows):
            full = jnp.concatenate([rows, actions_t, ones], axis=0)
            high = full.astype(BF16).astype(F32)
            low = full - high
            return jnp.concatenate(
                [high, low, high, jnp.zeros((128 - 72, width), F32)], axis=0
            ).astype(BF16)

        pairs = pack(states_t)
        pairs_next = pack(next_t)

        def product(ref, slot, high, low):
            both = dot(ref[slot], high)
            return both[:HID] + both[HID:] + dot(ref[slot, :HID], low)

        def layer(half):
            t = jnp.tanh(half)
            u = t + 1.0
            a = half * u
            return a, t, u

        def forward(slot, inputs, keep):
            half = dot(first[slot], inputs)
            yield
            a_one, t, u = layer(half)
            slope_one = u + a_one * (1.0 - t) if keep else None
            parts = split(a_one)
            yield
            z = product(second, slot, parts[0], parts[1])
            yield
            a_two, t, u = layer(z + wide(bias_two[slot]))
            slope_two = u + a_two * (1.0 - t) if keep else None
            return parts, slope_one, a_two, slope_two

        def weighted(slot, hidden):
            return jnp.sum(hidden * wide(out_weight[slot]), axis=0, keepdims=True)

        def backward(slot, parts, slope_one, delta_two):
            acc_bias[slot] += fold(delta_two)
            high, low = split(delta_two)
            yield
            delta_one = product(back, slot, high, low)
            acc_second[slot] += dot(
                jnp.concatenate([parts[0], parts[1], parts[0]], axis=1),
                jnp.concatenate([high, high, low], axis=1),
                NT,
            )
            yield
            high, low = split(delta_one * slope_one)
            yield
            rows = pairs[:48]
            acc_first[slot] += dot(
                jnp.concatenate([rows, rows], axis=1), jnp.concatenate([high, low], axis=1), NT
            )

        known = {}

        def next_chain():
            _, _, hidden, _ = yield from forward(0, pairs_next, False)
            value_next = weighted(0, hidden) + value_bias
            known["goal"] = reward + DISCOUNT * (1.0 - done) * value_next

        def target_chain(member):
            _, _, hidden, _ = yield from forward(4 + member, pairs, False)
            known["target", member] = weighted(4 + member, hidden) + target_bias[member]

        def critic_chain(member):
            slot = 2 + member
            parts, slope_one, hidden, slope_two = yield from forward(slot, pairs, True)
            error = (weighted(slot, hidden) + critic_bias[member] - known["goal"]) * valid
            grad = 2.0 * error
            known["critic", member] = (error * error, grad)
            acc_out[slot] += fold(hidden * grad)
            yield from backward(slot, parts, slope_one, slope_two * grad)

        def value_chain():
            parts, slope_one, hidden, slope_two = yield from forward(0, pairs, True)
            target_min = jnp.minimum(known["target", 0], known["target", 1])
            gap = target_min - (weighted(0, hidden) + value_bias)
            expect = jnp.where(gap < 0.0, 1.0 - EXPECTILE, EXPECTILE) * valid
            grad = -2.0 * expect * gap
            known["gap"] = gap
            known["value"] = (grad, expect * gap * gap)
            acc_out[0] += fold(hidden * grad)
            yield from backward(0, parts, slope_one, slope_two * grad)

        def actor_chain():
            parts, slope_one, hidden, slope_two = yield from forward(1, pairs, True)
            hidden_high, hidden_low = split(hidden)
            both = dot(head_pack[...], hidden_high)
            head = both[:8] + both[16:24] + dot(head_pack[:16], hidden_low)[:8]
            yield
            bias = wide(head_bias[...])
            mean = jnp.tanh(head[:6] + bias[1:7])
            log_std = bias[7:13]
            inverse = jnp.exp(-log_std)
            scaled = (actions_t - mean) * inverse
            log_prob = jnp.sum(
                -0.5 * scaled * scaled - log_std - 0.5 * LOG_TWO_PI, axis=0, keepdims=True
            )
            weight = jnp.minimum(jnp.exp(BETA_TEMP * known["gap"]), WEIGHT_CLIP) * valid
            grad_mean = -weight * scaled * inverse * (1.0 - mean * mean)
            grad_std = -weight * (scaled * scaled - 1.0)
            known["actor"] = (grad_mean, grad_std, -weight * log_prob)
            grads = jnp.concatenate([grad_mean, jnp.zeros((10, width), F32)], axis=0)
            grads_high, grads_low = split(grads)
            acc_head[...] += dot(jnp.concatenate([grads_high, grads_low], axis=0), hidden_high, NT)
            acc_head[:16] += dot(grads_high, hidden_low, NT)
            up = dot(
                head_back[...], jnp.concatenate([grads_high, grads_high, grads_low], axis=0)
            )
            yield
            yield from backward(1, parts, slope_one, up * slope_two)

        def finish():
            rows = jnp.concatenate(
                [known["value"][0], known["actor"][0], known["actor"][1], known["value"][1]]
                + [known["critic", 0][0], known["critic", 1][0], known["actor"][2], valid]
                + [known["critic", 0][1], known["critic", 1][1]]
                + [jnp.zeros((4, width), F32)],
                axis=0,
            )
            acc_rows[...] += fold(rows)

        return [
            next_chain(), target_chain(0), target_chain(1), critic_chain(0), value_chain(),
            actor_chain(), critic_chain(1),
        ], finish

    def tiles(starts, width=TILE):
        parts = [chains(start, width) for start in starts]
        waiting = [(chain, part) for part in parts for chain in part[0]]
        left = {id(part): len(part[0]) for part in parts}
        active = []
        while waiting or active:
            while waiting and len(active) < WIDTH:
                active.append(waiting.pop(0))
            for entry in list(active):
                chain, part = entry
                try:
                    next(chain)
                except StopIteration:
                    active.remove(entry)
                    left[id(part)] -= 1
                    if left[id(part)] == 0:
                        part[1]()

    base = start_unit * UNIT
    tile_count = unit_count * UNIT // TILE

    def several(i, carry):
        tiles([base + (UNROLL * i + k) * TILE for k in range(UNROLL)])
        return carry

    def single(i, carry):
        tiles([base + i * TILE])
        return carry

    await_next(len(copies) - (2 if adding else 0))
    rounds = tile_count // UNROLL
    lax.fori_loop(0, rounds, several, 0)
    lax.fori_loop(rounds * UNROLL, tile_count, single, 0)

    @pl.when(unit_count * UNIT > tile_count * TILE)
    def _():
        tiles([base + tile_count * TILE], UNIT)


    def store(out, row, value):
        count = value.shape[0]
        for half in range(2):
            at = slice(half * PAYLOAD + row, half * PAYLOAD + row + count)
            part = value[:, half * 128 : half * 128 + 128]
            out[at, :] = part + out[at, :] if adding else part

    def first_grad(slot):
        return acc_first[slot, :24] + acc_first[slot, 24:]

    def lanes(value):
        return jnp.sum(jnp.transpose(value), axis=0, keepdims=True)

    zero_row = jnp.zeros((1, HID), F32)
    row_sums = jnp.sum(
        jnp.transpose(jnp.concatenate([acc_rows[...], jnp.zeros((104, 128), F32)], axis=0)),
        axis=0,
        keepdims=True,
    )
    lane = lax.broadcasted_iota(jnp.int32, (1, 128), 1)
    swapped = jnp.where(
        lane == 14,
        pltpu.roll(row_sums, 127, 1),
        jnp.where(lane == 15, pltpu.roll(row_sums, 1, 1), row_sums),
    )
    shared_row = jnp.where(is_value, row_sums, swapped)
    head_actions = acc_head[:6] + acc_head[16:22]
    head_rows = jnp.concatenate([lanes(acc_out[0]), head_actions, zero_row], axis=0)
    out_rows = (
        value_row * 0.5, None, small(own, CRITIC, 1) * 0.5, small(other, CRITIC, 1) * 0.5,
    )

    def second_grad(slot):
        matrix, bias = acc_second[slot], lanes(acc_bias[slot])
        scale = out_rows[slot]
        return (matrix, bias) if scale is None else (matrix * scale, bias * scale)

    sent = []

    def send(row, count):
        for out, target in zip((out_own, out_other), outs):
            for half in range(2):
                at = slice(half * PAYLOAD + row, half * PAYLOAD + row + count)
                sent.append(
                    pltpu.make_async_copy(out.at[at, :], target.at[at, :], leave.at[len(sent)])
                )
                sent[-1].start()

    await_next(len(copies))
    trunk = [second_grad(slot) + (first_grad(slot),) for slot in range(2)]
    critic = [second_grad(2 + which) for which in range(2)]
    mixed = [
        [jnp.where(is_value, trunk[which][k], trunk[1 - which][k]) for k in range(3)]
        for which in range(2)
    ]
    for which, out in enumerate((out_own, out_other)):
        store(out, 0, mixed[which][0])
    send(0, HID)
    for which, out in enumerate((out_own, out_other)):
        store(out, HID, critic[which][0])
    send(HID, HID)
    for which, out in enumerate((out_own, out_other)):
        store(out, ROW_TRUNK, mixed[which][2])
        store(out, ROW_CRITIC, first_grad(2 + which))
        bias_grad = pltpu.roll(row_sums, 128 - 18 - which, 1)
        last = jnp.concatenate([shared_row, jnp.where(lane == 0, bias_grad, 0.0)], axis=1)
        store(
            out,
            ROW_VECTOR,
            jnp.concatenate(
                [mixed[which][1], critic[which][1], lanes(acc_out[2 + which]), last]
                + [zero_row] * 4,
                axis=0,
            ),
        )
        store(out, ROW_HEAD, head_rows)
    send(2 * HID, PAYLOAD - 2 * HID)
    for copy in sent:
        copy.wait()


def run_main(data, heads, weights, counts=None):
    hbm = pl.BlockSpec(memory_space=pl.ANY)
    size = lax.axis_size("batch")
    operands = (*data, *heads, *weights)
    payload = jax.ShapeDtypeStruct((2 * PAYLOAD, 128), F32)
    held = [pltpu.VMEM(array.shape, array.dtype) for array in (*heads, *weights)]
    semaphores = [pltpu.SemaphoreType.DMA((16,)), pltpu.SemaphoreType.DMA((12,))]
    if counts is None:
        name, body, specs, aliases = "moved_gradients", moved_kernel, [], {1: 0, 2: 1}
        buffers = [pltpu.VMEM((8, 128), F32), pltpu.VMEM(data[0].shape, F32)] + held
    else:
        name, body, aliases = "gradients", main_kernel, {}
        specs = [pl.BlockSpec(memory_space=pltpu.SMEM)]
        buffers = [pltpu.VMEM(array.shape, array.dtype) for array in data] + held
        operands = (counts,) + operands
    return pl.pallas_call(
        functools.partial(body, size),
        out_shape=[payload, payload],
        in_specs=specs + [hbm] * (len(operands) - len(specs)),
        out_specs=[hbm, hbm],
        input_output_aliases=aliases,
        scratch_shapes=semaphores + buffers + [pltpu.VMEM(payload.shape, F32)] * 2 + [
            pltpu.VMEM((6, HID, 128), BF16),
            pltpu.VMEM((6, 2 * HID, HID), BF16),
            pltpu.VMEM((4, 2 * HID, HID), BF16),
            pltpu.VMEM((6, HID, 128), F32),
            pltpu.VMEM((6, HID, 128), F32),
            pltpu.VMEM((32, HID), BF16),
            pltpu.VMEM((HID, 48), BF16),
            pltpu.VMEM((16, 128), F32),
            pltpu.VMEM((4, HID, HID), F32),
            pltpu.VMEM((4, 48, HID), F32),
            pltpu.VMEM((4, HID, 128), F32),
            pltpu.VMEM((4, HID, 128), F32),
            pltpu.VMEM((32, HID), F32),
            pltpu.VMEM((24, 128), F32),
        ],
        compiler_params=pltpu.CompilerParams(vmem_limit_bytes=VMEM_LIMIT),
        cost_estimate=pl.CostEstimate(
            flops=10**10, bytes_accessed=5 * 10**6, transcendentals=10**7
        ),
        name=name,
    )(*operands)


def read(ref):
    if len(ref.shape) == 2:
        return ref[...]
    return ref[:, 0, :] if ref.shape[1] == 1 else ref[0]


def write(ref, value):
    if len(ref.shape) == 2:
        ref[...] = value
    elif ref.shape[1] == 1:
        ref[:, 0, :] = value
    else:
        ref[0] = value


def lamb_kernel(*refs):
    count = 1 + 3 * len(NAMES) + 3
    inputs, targets_out = refs[:count], refs[count : count + 29]
    outs = refs[count + 29 : count + 58]
    steps, leave = refs[count + 58 :]
    sent = []

    def send(places):
        for at in places:
            copy = pltpu.make_async_copy(outs[at], targets_out[at], leave.at[at])
            copy.start()
            sent.append(copy)

    payload = inputs[0]
    params = [inputs[1 + 3 * i : 4 + 3 * i] for i in range(len(NAMES))]
    targets = inputs[count - 3 :]

    def rows(start, count):
        return jnp.concatenate(
            [payload[start : start + count, :], payload[PAYLOAD + start : PAYLOAD + start + count, :]],
            axis=1,
        )

    trunk_first = rows(ROW_TRUNK, 24)
    critic_first = rows(ROW_CRITIC, 24)
    vectors = rows(ROW_VECTOR, 8)
    head = rows(ROW_HEAD, 8)
    shared = vectors[3:4, :128]
    after = 1.0 / shared[:, 17:18]
    gradients = (
        trunk_first[:OBS],
        None,
        jnp.concatenate([trunk_first[23:24], vectors[0:1]], axis=1),
        head[:7],
        shared[:, :13],
        critic_first[: OBS + ACT],
        None,
        jnp.concatenate(
            [critic_first[23:24], vectors[1:2], vectors[2:3], vectors[3:4, 128:129]], axis=1
        ),
    )
    def moments(weight, gradient, mean_old, square_old):
        mean_new = DECAY_FIRST * mean_old + (1.0 - DECAY_FIRST) * gradient
        square_new = DECAY_SECOND * square_old + (1.0 - DECAY_SECOND) * gradient * gradient
        mean_hat = mean_new * (1.0 / (1.0 - DECAY_FIRST**STEP))
        square_hat = square_new * (1.0 / (1.0 - DECAY_SECOND**STEP))
        update = mean_hat / (jnp.sqrt(square_hat) + EPSILON) + WEIGHT_DECAY * weight
        return mean_new, square_new, update

    def total(value):
        return jnp.sum(jnp.sum(value * value, axis=0, keepdims=True), axis=1, keepdims=True)

    norms = {}
    updates = {}
    for i in (1, 6, 0, 2, 3, 4, 5, 7):
        weight_ref, mean_ref, square_ref = params[i]
        if i in (1, 6):
            weight_sum, update_sum = jnp.zeros((8, HID), F32), jnp.zeros((8, HID), F32)
            for band in range(0, HID, BAND):
                at = slice(band, band + BAND)
                weight = weight_ref[0, at, :]
                gradient = rows((0 if i == 1 else HID) + band, BAND) * after
                mean_new, square_new, update = moments(
                    weight, gradient, mean_ref[0, at, :], square_ref[0, at, :]
                )
                outs[8 + i][0, at, :] = mean_new
                outs[16 + i][0, at, :] = square_new
                steps[0 if i == 1 else 1, at, :] = update
                for k in range(0, BAND, 8):
                    weight_sum += weight[k : k + 8] * weight[k : k + 8]
                    update_sum += update[k : k + 8] * update[k : k + 8]
            over = lambda part: jnp.sum(
                jnp.sum(part, axis=0, keepdims=True), axis=1, keepdims=True
            )
            norms[i] = (jnp.sqrt(over(weight_sum)), jnp.sqrt(over(update_sum)))
            send((8 + i, 16 + i))
        else:
            weight = read(weight_ref)
            mean_new, square_new, updates[i] = moments(
                weight, gradients[i] * after, read(mean_ref), read(square_ref)
            )
            write(outs[8 + i], mean_new)
            write(outs[16 + i], square_new)
            norms[i] = (jnp.sqrt(total(weight)), jnp.sqrt(total(updates[i])))
    send([8 + k + i for i in (0, 2, 3, 4, 5, 7) for k in (0, 8)])
    for i, name in enumerate(NAMES):
        scale = LEARN_RATE * (norms[i][0] / norms[i][1])
        if i in (1, 6):
            for band in range(0, HID, BAND):
                at = slice(band, band + BAND)
                new = params[i][0][0, at, :] - scale * steps[0 if i == 1 else 1, at, :]
                outs[i][0, at, :] = new
                if i == 6:
                    outs[25][0, at, :] = (
                        (1.0 - TARGET_RATE) * targets[1][0, at, :] + TARGET_RATE * new
                    )
        else:
            new = read(params[i][0]) - scale * updates[i]
            write(outs[i], new)
            if i >= 5:
                write(
                    outs[19 + i], (1.0 - TARGET_RATE) * read(targets[i - 5]) + TARGET_RATE * new
                )
    lane = lax.broadcasted_iota(jnp.int32, (1, 8), 1)
    for row in range(2):
        line = jnp.zeros((1, 8), F32)
        for i, pair in norms.items():
            line = jnp.where(lane == i, pair[row], line)
        outs[27][0, row : row + 1, :] = line
    outs[28][...] = pltpu.roll(shared, 128 - 13, 1)[:, :5]
    send([*range(8), *range(24, 29)])
    for copy in sent:
        copy.wait()


NAMES = (
    "trunk_input", "trunk_middle", "trunk_vector", "head_weight", "head_vector",
    "critic_input", "critic_middle", "critic_vector",
)


def run_lamb(payload, params, targets):
    hbm = pl.BlockSpec(memory_space=pl.ANY)
    flat = [array for triple in params for array in triple]
    shapes = [jax.ShapeDtypeStruct(triple[0].shape, F32) for triple in params]
    outs = shapes * 3 + [jax.ShapeDtypeStruct(t.shape, F32) for t in targets]
    outs += [jax.ShapeDtypeStruct((1, 2, 8), F32), jax.ShapeDtypeStruct((1, 5), F32)]
    operands = (payload, *flat, *targets)
    return pl.pallas_call(
        lamb_kernel,
        out_shape=outs,
        in_specs=[pl.BlockSpec(memory_space=pltpu.VMEM)] * len(operands),
        out_specs=[hbm] * len(outs),
        scratch_shapes=[pltpu.VMEM(array.shape, array.dtype) for array in outs]
        + [
            pltpu.VMEM((2, HID, HID), F32),
            pltpu.SemaphoreType.DMA((len(outs),)),
        ],
        compiler_params=pltpu.CompilerParams(vmem_limit_bytes=16 * 2**20),
        name="update",
    )(*operands)


def across(value):
    size = lax.axis_size("net")
    return lax.ppermute(value, "net", [(i, size - 1 - i) for i in range(size)])


def summed(value):
    size = lax.axis_size("batch")
    if size % 2:
        return lax.psum(value, "batch")
    half = size // 2
    groups = [list(range(half)), list(range(half, size))]
    rows = value.shape[0]
    each = -(-rows // half)
    if each * half != rows:
        value = jnp.concatenate([value, jnp.zeros((each * half - rows, 128), F32)], axis=0)
    pieces = lax.all_to_all(
        value.reshape(half, each, 128), "batch", 0, 0, axis_index_groups=groups, tiled=True
    )
    mine = jnp.sum(pieces, axis=0)
    mine = mine + lax.ppermute(
        mine, "batch", [pair for a, b in zip(*groups) for pair in ((a, b), (b, a))]
    )
    full = lax.all_to_all(
        jnp.broadcast_to(mine[None], (half, each, 128)), "batch", 0, 0,
        axis_index_groups=groups, tiled=True,
    )
    return full.reshape(each * half, 128)[:rows]


def shards(
    states, next_states, actions, rewards, finished, valid_counts,
    trunk_input, trunk_middle, trunk_vector, head_weight, head_vector,
    critic_input, critic_middle, critic_vector,
    target_input, target_middle, target_vector,
    mean_trunk_input, square_trunk_input, mean_trunk_middle, square_trunk_middle,
    mean_trunk_vector, square_trunk_vector, mean_head_weight, square_head_weight,
    mean_head_vector, square_head_vector, mean_critic_input, square_critic_input,
    mean_critic_middle, square_critic_middle, mean_critic_vector, square_critic_vector,
):
    def turned(array):
        if array.ndim == 3 and array.shape[1] != HID:
            return jnp.transpose(array, (1, 0, 2))
        if array.ndim == 2 and array.shape[0] == HID:
            return array.T
        return array.reshape(1, -1) if array.ndim == 1 else array

    def back(array, like):
        if like.ndim == 3 and like.shape[1] != HID:
            return jnp.transpose(array, (1, 0, 2))
        if like.ndim == 2 and like.shape[0] == HID:
            return array.T
        return array.reshape(like.shape)

    params = [
        tuple(turned(array) for array in triple)
        for triple in (
            (trunk_input, mean_trunk_input, square_trunk_input),
            (trunk_middle, mean_trunk_middle, square_trunk_middle),
            (trunk_vector, mean_trunk_vector, square_trunk_vector),
            (head_weight, mean_head_weight, square_head_weight),
            (head_vector, mean_head_vector, square_head_vector),
            (critic_input, mean_critic_input, square_critic_input),
            (critic_middle, mean_critic_middle, square_critic_middle),
            (critic_vector, mean_critic_vector, square_critic_vector),
        )
    ]
    targets = tuple(turned(array) for array in (target_input, target_middle, target_vector))
    own = tuple(params[i][0] for i in (0, 1, 2, 5, 6, 7)) + targets
    lines = (states.shape[1] // 128, 128)
    data = (states, next_states, actions, rewards.reshape(lines), finished.reshape(lines))
    heads = (params[3][0], params[4][0])
    weights, message = run_pack(valid_counts, data, own)
    size = lax.axis_size("batch")
    both = (weights, across(weights))
    arrived = lax.ppermute(message, "batch", [(i, size - 1 - i) for i in range(size // 2, size)])
    own_part, other_part = run_main(data, heads, both, valid_counts)
    own_part, other_part = run_main((arrived, own_part, other_part), heads, both)
    results = list(run_lamb(summed(own_part + across(other_part)), params, targets))
    likes = (
        trunk_input, trunk_middle, trunk_vector, head_weight, head_vector,
        critic_input, critic_middle, critic_vector,
    ) * 3 + (target_input, target_middle, target_vector)
    final = [back(array, like) for array, like in zip(results, likes)]
    return tuple(final) + (jnp.transpose(results[27], (0, 2, 1)), results[28].reshape(5))


def solution(mesh):
    rows, matrix, vector, none = P(None, "batch"), P("net", None, None), P("net", None), P()
    line = P("batch")
    params = (matrix, matrix, vector, none, none, matrix, matrix, vector)
    moments = tuple(spec for entry in params for spec in (entry, entry))
    target = (matrix, matrix, vector)
    return jax.shard_map(
        shards,
        mesh=mesh,
        in_specs=(rows, rows, rows, line, line, line) + params + target + moments,
        out_specs=params * 3 + target + (matrix, none),
        check_vma=False,
    )
```

```python
import functools
import math

import jax
import jax.numpy as jnp
from jax import lax
from jax.experimental import pallas as pl
from jax.experimental.pallas import tpu as pltpu
from jax.sharding import PartitionSpec as P

STEP = 10
EXPECTILE = 0.7
DISCOUNT = 0.99
BETA_TEMP = 3.0
WEIGHT_CLIP = 100.0
DECAY_FIRST = 0.9
DECAY_SECOND = 0.999
EPSILON = 1e-06
WEIGHT_DECAY = 0.01
LEARN_RATE = 0.3
TARGET_RATE = 0.005
BAND = 32
LOG_TWO_PI = math.log(2.0 * math.pi)

OBS = 17
ACT = 6
HID = 256
TILE = 256
WIDTH = 7
UNROLL = 3
UNIT = 128
ROW_TRUNK = 2 * HID
ROW_CRITIC = ROW_TRUNK + 24
ROW_VECTOR = ROW_CRITIC + 24
ROW_HEAD = ROW_VECTOR + 8
PAYLOAD = ROW_HEAD + 8
VMEM_LIMIT = 64 * 2**20 - 2**17

META_ROW = OBS + ACT
NEXT_ROW = META_ROW + 1
PACK_ROWS = NEXT_ROW + OBS + 2
TRUNK, CRITIC, TARGET = range(3)
SMALL_ROW = 3 * HID
WEIGHT_ROWS = SMALL_ROW + 3 * 32
EXTRA_ROWS = 1024
HEAD_START = 0

F32 = jnp.float32
BF16 = jnp.bfloat16
NN = (((1,), (0,)), ((), ()))
NT = (((1,), (1,)), ((), ()))


def split(value):
    high = value.astype(BF16)
    return high, (value - high.astype(F32)).astype(BF16)


def dot(left, right, dims=NN):
    return lax.dot_general(left, right, dims, preferred_element_type=F32)


def fold(value):
    total = value[:, :128]
    for start in range(128, value.shape[1], 128):
        total = total + value[:, start : start + 128]
    return total


def left_parts(value):
    return jnp.concatenate(split(value), axis=0)


def column(row):
    return jnp.transpose(jnp.broadcast_to(row, (128, row.shape[1])))


def room_of(row_total):
    total, least = row_total // UNIT, -(-(row_total // 3) // UNIT)
    return max(2, -(-(total - (total + least) // 2) // 2))


def plan(count_ref, size, row_total):
    group, index = lax.axis_index("net"), lax.axis_index("batch")
    used = count_ref[0]
    units = (used + UNIT - 1) // UNIT
    total, room, lowest = row_total // UNIT, room_of(row_total), row_total // 3
    guess = (
        lowest
        + (size - 1 - index) * (row_total - lowest - row_total // 8) // max(size - 1, 1)
        + row_total // 16
    )
    kept = (used + guess + EXTRA_ROWS + 2 * UNIT - 1) // (2 * UNIT)
    kept = jnp.minimum(jnp.maximum(kept, units - 2 * room), units)
    kept = jnp.where(units - kept < 4, units, kept)
    kept = jnp.where(2 * index >= size, kept, units)
    sent = units - kept
    first = (sent + 1) // 2
    mine = jnp.minimum((kept + HEAD_START) // 2, kept)
    leading = group == 0
    start = kept + jnp.where(leading, 0, first)
    return dict(
        group=group, used=used,
        own_start=jnp.where(leading, 0, mine), own_count=jnp.where(leading, mine, kept - mine),
        sent_start=start, sent_count=jnp.where(leading, first, sent - first),
        window=jnp.minimum(start, total - room),
    )


def load(pairs, sems):
    copies = [
        pltpu.make_async_copy(source, target, sems.at[k])
        for k, (source, target) in enumerate(pairs)
    ]
    for copy in copies:
        copy.start()
    return copies


def pack_kernel(size, row_total, count_ref, *refs):
    sources, (weight_out, row_out), (arrive, leave, *parts) = refs[:14], refs[14:16], refs[16:]
    state_part, next_part, action_part, rewards, finished = parts[:5]
    weights, (small_part, row_part) = parts[5:14], parts[14:]
    room = room_of(row_total)
    copies = load(list(zip(sources[5:], weights)) + list(zip(sources[3:5], parts[3:5])), arrive)
    here = plan(count_ref, size, row_total)
    at = pl.ds(pl.multiple_of(here["window"] * UNIT, UNIT), room * UNIT)
    for k in range(3):
        copies.append(
            pltpu.make_async_copy(sources[k].at[:, at], parts[k], arrive.at[len(copies)])
        )
        copies[-1].start()
    sent = []

    def send(source, target):
        sent.append(pltpu.make_async_copy(source, target, leave.at[len(sent)]))
        sent[-1].start()

    for net in range(3):
        copies[3 * net + 1].wait()
        send(weights[3 * net + 1].at[0], weight_out.at[net * HID : (net + 1) * HID, :])
    for net in range(3):
        copies[3 * net].wait()
        copies[3 * net + 2].wait()
        rows, _, vector = weights[3 * net : 3 * net + 3]
        row = 32 * net
        width = rows.shape[0]
        pieces = [rows[:, 0, :]]
        if width < META_ROW:
            pieces.append(jnp.zeros((META_ROW - width, HID), F32))
        pieces.append(vector[:, :HID])
        small_part[row : row + 24, :] = jnp.concatenate(pieces, axis=0)
        pieces = [vector[:, HID : 2 * HID]]
        if vector.shape[1] > 2 * HID:
            pieces.append(vector[:, 2 * HID : 3 * HID])
            pieces.append(jnp.broadcast_to(vector[:, 3 * HID : 3 * HID + 1], (1, HID)))
        pieces.append(jnp.zeros((8 - len(pieces), HID), F32))
        small_part[row + 24 : row + 32, :] = jnp.concatenate(pieces, axis=0)
    send(small_part, weight_out.at[SMALL_ROW:, :])

    def line(ref):
        first = here["window"] * (UNIT // 128)
        return jnp.concatenate(
            [ref[pl.ds(first + k, 1), :] for k in range(room * UNIT // 128)], axis=1
        )

    lane = lax.broadcasted_iota(jnp.int32, (1, room * UNIT), 1)
    meta = jnp.zeros((1, room * UNIT), F32)
    for k, number in enumerate(
        (
            here["sent_start"] - here["window"], here["sent_count"],
            here["used"] - here["window"] * UNIT,
        )
    ):
        meta = jnp.where(lane == k, number.astype(F32), meta)
    for copy in copies[9:]:
        copy.wait()
    row_part[: META_ROW + 1, :] = jnp.concatenate([state_part[...], action_part[...], meta], axis=0)
    row_part[NEXT_ROW:, :] = jnp.concatenate(
        [next_part[...], line(rewards), line(finished).astype(F32)], axis=0
    )
    send(row_part, row_out)
    for copy in sent:
        copy.wait()


def run_pack(counts, data, weights):
    hbm = pl.BlockSpec(memory_space=pl.ANY)
    row_total = data[0].shape[1]
    span = room_of(row_total) * UNIT
    row_out = jax.ShapeDtypeStruct((PACK_ROWS, span), F32)
    held = [pltpu.VMEM((array.shape[0], span), F32) for array in data[:3]]
    held += [pltpu.VMEM(array.shape, array.dtype) for array in (*data[3:], *weights)]
    return pl.pallas_call(
        functools.partial(pack_kernel, lax.axis_size("batch"), row_total),
        out_shape=[jax.ShapeDtypeStruct((WEIGHT_ROWS, HID), F32), row_out],
        in_specs=[pl.BlockSpec(memory_space=pltpu.SMEM)] + [hbm] * (len(data) + len(weights)),
        out_specs=[hbm, hbm],
        scratch_shapes=[pltpu.SemaphoreType.DMA((14,)), pltpu.SemaphoreType.DMA((5,))]
        + held
        + [pltpu.VMEM((WEIGHT_ROWS - SMALL_ROW, HID), F32), pltpu.VMEM(row_out.shape, F32)],
        compiler_params=pltpu.CompilerParams(vmem_limit_bytes=VMEM_LIMIT),
        name="messages",
    )(counts, *data, *weights)


def weight_pairs(sources, targets):
    heads = list(zip(sources[:2], targets[:2]))
    parts = [slice(SMALL_ROW, WEIGHT_ROWS)]
    parts += [slice(net * HID, (net + 1) * HID) for net in (CRITIC, TARGET, TRUNK)]
    return heads + [
        (source.at[part, :], target.at[part, :])
        for part in parts
        for source, target in zip(sources[2:], targets[2:])
    ]


def main_kernel(size, count_ref, *refs):
    sources, outs, (arrive, leave, *refs) = refs[:9], refs[9:11], refs[11:]
    buffers, sums, scratch = refs[:9], refs[9:11], refs[11:]
    states, next_states, actions, rewards, finished = buffers[:5]
    pairs = weight_pairs(sources[5:], buffers[5:]) + list(zip(sources[:5], buffers[:5]))
    copies = load(pairs, arrive)

    def line(ref, start, width):
        return jnp.concatenate(
            [ref[pl.ds(start // 128 + part, 1), :] for part in range(width // 128)], axis=1
        )

    def rows_of(start, width):
        at = pl.ds(start, width)
        return (
            states[:, at], next_states[:, at], actions[:, at],
            line(rewards, start, width), line(finished, start, width).astype(F32),
        )

    here = plan(count_ref, size, states.shape[1])
    gradients(
        here["group"], here["own_start"], here["own_count"], here["used"], rows_of, copies, False,
        outs, leave, *buffers[5:], *sums, *scratch,
    )


def moved_kernel(size, packed_ref, *refs):
    inputs, outs, (arrive, leave, *refs) = refs[:6], refs[6:8], refs[8:]
    meta_part, packed, *buffers = refs[:6]
    sums, scratch = refs[6:8], refs[8:]

    def add(start, count, used):
        pairs = weight_pairs(inputs[2:], buffers)
        pairs += [(packed_ref, packed)] + list(zip(inputs[:2], sums))
        copies = load(pairs, arrive)

        def rows_of(start, width):
            at = pl.ds(start, width)
            return (
                packed[:OBS, at], packed[NEXT_ROW : NEXT_ROW + OBS, at], packed[OBS:META_ROW, at],
                packed[NEXT_ROW + OBS : NEXT_ROW + OBS + 1, at], packed[PACK_ROWS - 1 : PACK_ROWS, at],
            )

        gradients(
            lax.axis_index("net"), start, count, used, rows_of, copies, True, outs, leave,
            *buffers, *sums, *scratch,
        )

    @pl.when(2 * lax.axis_index("batch") < size)
    def _():
        copy = pltpu.make_async_copy(
            packed_ref.at[META_ROW - 7 : META_ROW + 1, :128], meta_part, arrive.at[0]
        )
        copy.start()
        copy.wait()
        meta = meta_part[7:8, :]
        place = lax.broadcasted_iota(jnp.int32, (1, 128), 1)
        start, count, used = (
            jnp.sum(jnp.where(place == k, meta, 0.0)).astype(jnp.int32) for k in range(3)
        )
        pl.when(count > 0)(lambda: add(start, count, used))


def gradients(
    group, start_unit, unit_count, used, rows_of, copies, adding, outs, leave,
    head_weight, head_vector, own, other, out_own, out_other, *scratch
):
    (
        first, second, back, bias_two, out_weight, head_pack, head_back, head_bias,
        acc_second, acc_first, acc_bias, acc_out, acc_head, acc_rows,
    ) = scratch

    def await_next(count):
        for _ in range(count):
            copies.pop(0).wait()

    copies = list(copies)
    await_next(4)

    head_columns = jnp.concatenate([head_weight[...], jnp.zeros((1, HID), F32)], axis=0)
    value_row = head_columns[0:1]
    action_rows = jnp.concatenate(
        [head_columns[1:7], jnp.zeros((2, HID), F32)], axis=0
    )
    row_high, row_low = split(jnp.concatenate([action_rows, jnp.zeros((8, HID), F32)], axis=0))
    head_pack[...] = jnp.concatenate([row_high, row_low], axis=0)
    mean_columns = jnp.transpose(
        jnp.concatenate([action_rows * 0.5, jnp.zeros((120, HID), F32)], axis=0)
    )[:, :16]
    mean_high, mean_low = split(mean_columns)
    head_back[...] = jnp.concatenate(
        [mean_high, mean_low, mean_high], axis=1
    )
    bias_column = jnp.transpose(
        jnp.concatenate(
            [
                jnp.concatenate([head_vector[...], jnp.zeros((1, 128 - 13), F32)], axis=1),
                jnp.zeros((127, 128), F32),
            ],
            axis=0,
        )
    )[:16, 0:1]
    head_bias[...] = jnp.broadcast_to(bias_column, (16, 128))

    is_value = group == 0

    def prepare(slot, net, take, out_row, with_back):
        row = SMALL_ROW + 32 * net
        packed = take(row, 24) * 0.5
        high = packed.astype(BF16).astype(F32)
        stack = jnp.concatenate(
            [high, high, packed - high, jnp.zeros((128 - 72, HID), F32)], axis=0
        )
        first[slot] = jnp.transpose(stack).astype(BF16)
        matrix = take(net * HID, HID)
        second[slot] = left_parts(jnp.transpose(matrix) * 0.5)
        bias_two[slot] = column(take(row + 24, 1) * 0.5)
        if out_row is not None:
            out_weight[slot] = column(out_row)
        if with_back:
            back[slot] = left_parts(matrix * (0.25 * out_row if out_row is not None else 0.5))

    def picked(first_ref, second_ref):
        return lambda row, count: jnp.where(
            is_value, first_ref[row : row + count, :], second_ref[row : row + count, :]
        )

    def small(ref, net, row):
        return ref[SMALL_ROW + 32 * net + 24 + row : SMALL_ROW + 32 * net + 25 + row, :]

    for slot, ref, net in (
        (2, own, CRITIC), (3, other, CRITIC), (4, own, TARGET), (5, other, TARGET),
    ):
        if slot % 2 == 0:
            await_next(2)
        take = lambda row, count, ref=ref: ref[row : row + count, :]
        prepare(slot, net, take, small(ref, net, 1), slot < 4)
    await_next(2)
    prepare(0, TRUNK, picked(own, other), value_row, True)
    prepare(1, TRUNK, picked(other, own), None, True)
    target_bias = [small(ref, TARGET, 2)[:, :1] for ref in (own, other)]
    critic_bias = [small(ref, CRITIC, 2)[:, :1] for ref in (own, other)]
    value_bias = head_vector[0:1, 0:1]

    acc_second[...] = jnp.zeros_like(acc_second)
    acc_first[...] = jnp.zeros_like(acc_first)
    acc_bias[...] = jnp.zeros_like(acc_bias)
    acc_out[...] = jnp.zeros_like(acc_out)
    acc_head[...] = jnp.zeros_like(acc_head)
    acc_rows[...] = jnp.zeros_like(acc_rows)

    def chains(start, width):
        start = pl.multiple_of(start, UNIT)
        states_t, next_t, actions_t, reward, done = rows_of(start, width)
        ones = jnp.ones((1, width), F32)
        place = start + lax.broadcasted_iota(jnp.int32, (1, width), 1)

        def wide(value):
            return jnp.concatenate([value] * (width // 128), axis=1)

        valid = (place < used).astype(F32)

        def pack(rows):
            full = jnp.concatenate([rows, actions_t, ones], axis=0)
            high = full.astype(BF16).astype(F32)
            low = full - high
            return jnp.concatenate(
                [high, low, high, jnp.zeros((128 - 72, width), F32)], axis=0
            ).astype(BF16)

        pairs = pack(states_t)
        pairs_next = pack(next_t)

        def product(ref, slot, high, low):
            both = dot(ref[slot], high)
            return both[:HID] + both[HID:] + dot(ref[slot, :HID], low)

        def layer(half):
            t = jnp.tanh(half)
            u = t + 1.0
            a = half * u
            return a, t, u

        def forward(slot, inputs, keep):
            half = dot(first[slot], inputs)
            yield
            a_one, t, u = layer(half)
            slope_one = u + a_one * (1.0 - t) if keep else None
            parts = split(a_one)
            yield
            z = product(second, slot, parts[0], parts[1])
            yield
            a_two, t, u = layer(z + wide(bias_two[slot]))
            slope_two = u + a_two * (1.0 - t) if keep else None
            return parts, slope_one, a_two, slope_two

        def weighted(slot, hidden):
            return jnp.sum(hidden * wide(out_weight[slot]), axis=0, keepdims=True)

        def backward(slot, parts, slope_one, delta_two):
            acc_bias[slot] += fold(delta_two)
            high, low = split(delta_two)
            yield
            delta_one = product(back, slot, high, low)
            acc_second[slot] += dot(
                jnp.concatenate([parts[0], parts[1], parts[0]], axis=1),
                jnp.concatenate([high, high, low], axis=1),
                NT,
            )
            yield
            high, low = split(delta_one * slope_one)
            yield
            rows = pairs[:48]
            acc_first[slot] += dot(
                jnp.concatenate([rows, rows], axis=1), jnp.concatenate([high, low], axis=1), NT
            )

        known = {}

        def next_chain():
            _, _, hidden, _ = yield from forward(0, pairs_next, False)
            value_next = weighted(0, hidden) + value_bias
            known["goal"] = reward + DISCOUNT * (1.0 - done) * value_next

        def target_chain(member):
            _, _, hidden, _ = yield from forward(4 + member, pairs, False)
            known["target", member] = weighted(4 + member, hidden) + target_bias[member]

        def critic_chain(member):
            slot = 2 + member
            parts, slope_one, hidden, slope_two = yield from forward(slot, pairs, True)
            error = (weighted(slot, hidden) + critic_bias[member] - known["goal"]) * valid
            grad = 2.0 * error
            known["critic", member] = (error * error, grad)
            acc_out[slot] += fold(hidden * grad)
            yield from backward(slot, parts, slope_one, slope_two * grad)

        def value_chain():
            parts, slope_one, hidden, slope_two = yield from forward(0, pairs, True)
            target_min = jnp.minimum(known["target", 0], known["target", 1])
            gap = target_min - (weighted(0, hidden) + value_bias)
            expect = jnp.where(gap < 0.0, 1.0 - EXPECTILE, EXPECTILE) * valid
            grad = -2.0 * expect * gap
            known["gap"] = gap
            known["value"] = (grad, expect * gap * gap)
            acc_out[0] += fold(hidden * grad)
            yield from backward(0, parts, slope_one, slope_two * grad)

        def actor_chain():
            parts, slope_one, hidden, slope_two = yield from forward(1, pairs, True)
            hidden_high, hidden_low = split(hidden)
            both = dot(head_pack[...], hidden_high)
            head = both[:8] + both[16:24] + dot(head_pack[:16], hidden_low)[:8]
            yield
            bias = wide(head_bias[...])
            mean = jnp.tanh(head[:6] + bias[1:7])
            log_std = bias[7:13]
            inverse = jnp.exp(-log_std)
            scaled = (actions_t - mean) * inverse
            log_prob = jnp.sum(
                -0.5 * scaled * scaled - log_std - 0.5 * LOG_TWO_PI, axis=0, keepdims=True
            )
            weight = jnp.minimum(jnp.exp(BETA_TEMP * known["gap"]), WEIGHT_CLIP) * valid
            grad_mean = -weight * scaled * inverse * (1.0 - mean * mean)
            grad_std = -weight * (scaled * scaled - 1.0)
            known["actor"] = (grad_mean, grad_std, -weight * log_prob)
            grads = jnp.concatenate([grad_mean, jnp.zeros((10, width), F32)], axis=0)
            grads_high, grads_low = split(grads)
            acc_head[...] += dot(jnp.concatenate([grads_high, grads_low], axis=0), hidden_high, NT)
            acc_head[:16] += dot(grads_high, hidden_low, NT)
            up = dot(
                head_back[...], jnp.concatenate([grads_high, grads_high, grads_low], axis=0)
            )
            yield
            yield from backward(1, parts, slope_one, up * slope_two)

        def finish():
            rows = jnp.concatenate(
                [known["value"][0], known["actor"][0], known["actor"][1], known["value"][1]]
                + [known["critic", 0][0], known["critic", 1][0], known["actor"][2], valid]
                + [known["critic", 0][1], known["critic", 1][1]]
                + [jnp.zeros((4, width), F32)],
                axis=0,
            )
            acc_rows[...] += fold(rows)

        return [
            next_chain(), target_chain(0), target_chain(1), critic_chain(0), value_chain(),
            actor_chain(), critic_chain(1),
        ], finish

    def tiles(starts, width=TILE):
        parts = [chains(start, width) for start in starts]
        waiting = [(chain, part) for part in parts for chain in part[0]]
        left = {id(part): len(part[0]) for part in parts}
        active = []
        while waiting or active:
            while waiting and len(active) < WIDTH:
                active.append(waiting.pop(0))
            for entry in list(active):
                chain, part = entry
                try:
                    next(chain)
                except StopIteration:
                    active.remove(entry)
                    left[id(part)] -= 1
                    if left[id(part)] == 0:
                        part[1]()

    base = start_unit * UNIT
    tile_count = unit_count * UNIT // TILE

    def several(i, carry):
        tiles([base + (UNROLL * i + k) * TILE for k in range(UNROLL)])
        return carry

    def single(i, carry):
        tiles([base + i * TILE])
        return carry

    await_next(len(copies) - (2 if adding else 0))
    rounds = tile_count // UNROLL
    lax.fori_loop(0, rounds, several, 0)
    if UNROLL > 1:
        lax.fori_loop(rounds * UNROLL, tile_count, single, 0)

    @pl.when(unit_count * UNIT > tile_count * TILE)
    def _():
        tiles([base + tile_count * TILE], UNIT)


    def store(out, row, value):
        count = value.shape[0]
        for half in range(2):
            at = slice(half * PAYLOAD + row, half * PAYLOAD + row + count)
            part = value[:, half * 128 : half * 128 + 128]
            out[at, :] = part + out[at, :] if adding else part

    def first_grad(slot):
        return acc_first[slot, :24] + acc_first[slot, 24:]

    def lanes(value):
        return jnp.sum(jnp.transpose(value), axis=0, keepdims=True)

    zero_row = jnp.zeros((1, HID), F32)
    row_sums = jnp.sum(
        jnp.transpose(jnp.concatenate([acc_rows[...], jnp.zeros((104, 128), F32)], axis=0)),
        axis=0,
        keepdims=True,
    )
    lane = lax.broadcasted_iota(jnp.int32, (1, 128), 1)
    swapped = jnp.where(
        lane == 14,
        pltpu.roll(row_sums, 127, 1),
        jnp.where(lane == 15, pltpu.roll(row_sums, 1, 1), row_sums),
    )
    shared_row = jnp.where(is_value, row_sums, swapped)
    head_actions = acc_head[:6] + acc_head[16:22]
    head_rows = jnp.concatenate([lanes(acc_out[0]), head_actions, zero_row], axis=0)
    out_rows = (
        value_row * 0.5, None, small(own, CRITIC, 1) * 0.5, small(other, CRITIC, 1) * 0.5,
    )

    def second_grad(slot):
        matrix, bias = acc_second[slot], lanes(acc_bias[slot])
        scale = out_rows[slot]
        return (matrix, bias) if scale is None else (matrix * scale, bias * scale)

    sent = []

    def send(row, count):
        for out, target in zip((out_own, out_other), outs):
            for half in range(2):
                at = slice(half * PAYLOAD + row, half * PAYLOAD + row + count)
                sent.append(
                    pltpu.make_async_copy(out.at[at, :], target.at[at, :], leave.at[len(sent)])
                )
                sent[-1].start()

    await_next(len(copies))
    trunk = [second_grad(slot) + (first_grad(slot),) for slot in range(2)]
    critic = [second_grad(2 + which) for which in range(2)]
    mixed = [
        [jnp.where(is_value, trunk[which][k], trunk[1 - which][k]) for k in range(3)]
        for which in range(2)
    ]
    for which, out in enumerate((out_own, out_other)):
        store(out, 0, mixed[which][0])
    send(0, HID)
    for which, out in enumerate((out_own, out_other)):
        store(out, HID, critic[which][0])
    send(HID, HID)
    for which, out in enumerate((out_own, out_other)):
        store(out, ROW_TRUNK, mixed[which][2])
        store(out, ROW_CRITIC, first_grad(2 + which))
        bias_grad = pltpu.roll(row_sums, 128 - 18 - which, 1)
        last = jnp.concatenate([shared_row, jnp.where(lane == 0, bias_grad, 0.0)], axis=1)
        store(
            out,
            ROW_VECTOR,
            jnp.concatenate(
                [mixed[which][1], critic[which][1], lanes(acc_out[2 + which]), last]
                + [zero_row] * 4,
                axis=0,
            ),
        )
        store(out, ROW_HEAD, head_rows)
    send(2 * HID, PAYLOAD - 2 * HID)
    for copy in sent:
        copy.wait()


def run_main(data, heads, weights, counts=None):
    hbm = pl.BlockSpec(memory_space=pl.ANY)
    size = lax.axis_size("batch")
    operands = (*data, *heads, *weights)
    payload = jax.ShapeDtypeStruct((2 * PAYLOAD, 128), F32)
    held = [pltpu.VMEM(array.shape, array.dtype) for array in (*heads, *weights)]
    semaphores = [pltpu.SemaphoreType.DMA((16,)), pltpu.SemaphoreType.DMA((12,))]
    if counts is None:
        name, body, specs, aliases = "moved_gradients", moved_kernel, [], {1: 0, 2: 1}
        buffers = [pltpu.VMEM((8, 128), F32), pltpu.VMEM(data[0].shape, F32)] + held
    else:
        name, body, aliases = "gradients", main_kernel, {}
        specs = [pl.BlockSpec(memory_space=pltpu.SMEM)]
        buffers = [pltpu.VMEM(array.shape, array.dtype) for array in data] + held
        operands = (counts,) + operands
    return pl.pallas_call(
        functools.partial(body, size),
        out_shape=[payload, payload],
        in_specs=specs + [hbm] * (len(operands) - len(specs)),
        out_specs=[hbm, hbm],
        input_output_aliases=aliases,
        scratch_shapes=semaphores + buffers + [pltpu.VMEM(payload.shape, F32)] * 2 + [
            pltpu.VMEM((6, HID, 128), BF16),
            pltpu.VMEM((6, 2 * HID, HID), BF16),
            pltpu.VMEM((4, 2 * HID, HID), BF16),
            pltpu.VMEM((6, HID, 128), F32),
            pltpu.VMEM((6, HID, 128), F32),
            pltpu.VMEM((32, HID), BF16),
            pltpu.VMEM((HID, 48), BF16),
            pltpu.VMEM((16, 128), F32),
            pltpu.VMEM((4, HID, HID), F32),
            pltpu.VMEM((4, 48, HID), F32),
            pltpu.VMEM((4, HID, 128), F32),
            pltpu.VMEM((4, HID, 128), F32),
            pltpu.VMEM((32, HID), F32),
            pltpu.VMEM((24, 128), F32),
        ],
        compiler_params=pltpu.CompilerParams(vmem_limit_bytes=VMEM_LIMIT),
        cost_estimate=pl.CostEstimate(
            flops=10**10, bytes_accessed=5 * 10**6, transcendentals=10**7
        ),
        name=name,
    )(*operands)


def read(ref):
    if len(ref.shape) == 2:
        return ref[...]
    return ref[:, 0, :] if ref.shape[1] == 1 else ref[0]


def write(ref, value):
    if len(ref.shape) == 2:
        ref[...] = value
    elif ref.shape[1] == 1:
        ref[:, 0, :] = value
    else:
        ref[0] = value


def lamb_kernel(*refs):
    count = 1 + 3 * len(NAMES) + 3
    inputs, targets_out = refs[:count], refs[count : count + 29]
    outs = refs[count + 29 : count + 58]
    steps, leave = refs[count + 58 :]
    sent = []

    def send(places):
        for at in places:
            copy = pltpu.make_async_copy(outs[at], targets_out[at], leave.at[at])
            copy.start()
            sent.append(copy)

    payload = inputs[0]
    params = [inputs[1 + 3 * i : 4 + 3 * i] for i in range(len(NAMES))]
    targets = inputs[count - 3 :]

    def rows(start, count):
        return jnp.concatenate(
            [payload[start : start + count, :], payload[PAYLOAD + start : PAYLOAD + start + count, :]],
            axis=1,
        )

    trunk_first = rows(ROW_TRUNK, 24)
    critic_first = rows(ROW_CRITIC, 24)
    vectors = rows(ROW_VECTOR, 8)
    head = rows(ROW_HEAD, 8)
    shared = vectors[3:4, :128]
    after = 1.0 / shared[:, 17:18]
    gradients = (
        trunk_first[:OBS],
        None,
        jnp.concatenate([trunk_first[23:24], vectors[0:1]], axis=1),
        head[:7],
        shared[:, :13],
        critic_first[: OBS + ACT],
        None,
        jnp.concatenate(
            [critic_first[23:24], vectors[1:2], vectors[2:3], vectors[3:4, 128:129]], axis=1
        ),
    )
    def moments(weight, gradient, mean_old, square_old):
        mean_new = DECAY_FIRST * mean_old + (1.0 - DECAY_FIRST) * gradient
        square_new = DECAY_SECOND * square_old + (1.0 - DECAY_SECOND) * gradient * gradient
        mean_hat = mean_new * (1.0 / (1.0 - DECAY_FIRST**STEP))
        square_hat = square_new * (1.0 / (1.0 - DECAY_SECOND**STEP))
        update = mean_hat / (jnp.sqrt(square_hat) + EPSILON) + WEIGHT_DECAY * weight
        return mean_new, square_new, update

    def total(value):
        return jnp.sum(jnp.sum(value * value, axis=0, keepdims=True), axis=1, keepdims=True)

    norms = {}
    updates = {}
    for i in (1, 6, 0, 2, 3, 4, 5, 7):
        weight_ref, mean_ref, square_ref = params[i]
        if i in (1, 6):
            weight_sum, update_sum = jnp.zeros((8, HID), F32), jnp.zeros((8, HID), F32)
            for band in range(0, HID, BAND):
                at = slice(band, band + BAND)
                weight = weight_ref[0, at, :]
                gradient = rows((0 if i == 1 else HID) + band, BAND) * after
                mean_new, square_new, update = moments(
                    weight, gradient, mean_ref[0, at, :], square_ref[0, at, :]
                )
                outs[8 + i][0, at, :] = mean_new
                outs[16 + i][0, at, :] = square_new
                steps[0 if i == 1 else 1, at, :] = update
                for k in range(0, BAND, 8):
                    weight_sum += weight[k : k + 8] * weight[k : k + 8]
                    update_sum += update[k : k + 8] * update[k : k + 8]
            over = lambda part: jnp.sum(
                jnp.sum(part, axis=0, keepdims=True), axis=1, keepdims=True
            )
            norms[i] = (jnp.sqrt(over(weight_sum)), jnp.sqrt(over(update_sum)))
            send((8 + i, 16 + i))
        else:
            weight = read(weight_ref)
            mean_new, square_new, updates[i] = moments(
                weight, gradients[i] * after, read(mean_ref), read(square_ref)
            )
            write(outs[8 + i], mean_new)
            write(outs[16 + i], square_new)
            norms[i] = (jnp.sqrt(total(weight)), jnp.sqrt(total(updates[i])))
    send([8 + k + i for i in (0, 2, 3, 4, 5, 7) for k in (0, 8)])
    for i, name in enumerate(NAMES):
        scale = LEARN_RATE * (norms[i][0] / norms[i][1])
        if i in (1, 6):
            for band in range(0, HID, BAND):
                at = slice(band, band + BAND)
                new = params[i][0][0, at, :] - scale * steps[0 if i == 1 else 1, at, :]
                outs[i][0, at, :] = new
                if i == 6:
                    outs[25][0, at, :] = (
                        (1.0 - TARGET_RATE) * targets[1][0, at, :] + TARGET_RATE * new
                    )
        else:
            new = read(params[i][0]) - scale * updates[i]
            write(outs[i], new)
            if i >= 5:
                write(
                    outs[19 + i], (1.0 - TARGET_RATE) * read(targets[i - 5]) + TARGET_RATE * new
                )
    lane = lax.broadcasted_iota(jnp.int32, (1, 8), 1)
    for row in range(2):
        line = jnp.zeros((1, 8), F32)
        for i, pair in norms.items():
            line = jnp.where(lane == i, pair[row], line)
        outs[27][0, row : row + 1, :] = line
    outs[28][...] = pltpu.roll(shared, 128 - 13, 1)[:, :5]
    send([*range(8), *range(24, 29)])
    for copy in sent:
        copy.wait()


NAMES = (
    "trunk_input", "trunk_middle", "trunk_vector", "head_weight", "head_vector",
    "critic_input", "critic_middle", "critic_vector",
)


def run_lamb(payload, params, targets):
    hbm = pl.BlockSpec(memory_space=pl.ANY)
    flat = [array for triple in params for array in triple]
    shapes = [jax.ShapeDtypeStruct(triple[0].shape, F32) for triple in params]
    outs = shapes * 3 + [jax.ShapeDtypeStruct(t.shape, F32) for t in targets]
    outs += [jax.ShapeDtypeStruct((1, 2, 8), F32), jax.ShapeDtypeStruct((1, 5), F32)]
    operands = (payload, *flat, *targets)
    return pl.pallas_call(
        lamb_kernel,
        out_shape=outs,
        in_specs=[pl.BlockSpec(memory_space=pltpu.VMEM)] * len(operands),
        out_specs=[hbm] * len(outs),
        scratch_shapes=[pltpu.VMEM(array.shape, array.dtype) for array in outs]
        + [
            pltpu.VMEM((2, HID, HID), F32),
            pltpu.SemaphoreType.DMA((len(outs),)),
        ],
        compiler_params=pltpu.CompilerParams(vmem_limit_bytes=16 * 2**20),
        name="update",
    )(*operands)


def across(value):
    size = lax.axis_size("net")
    return lax.ppermute(value, "net", [(i, size - 1 - i) for i in range(size)])


def summed(value):
    size = lax.axis_size("batch")
    if size % 2:
        return lax.psum(value, "batch")
    half = size // 2
    groups = [list(range(half)), list(range(half, size))]
    rows = value.shape[0]
    each = -(-rows // half)
    if each * half != rows:
        value = jnp.concatenate([value, jnp.zeros((each * half - rows, 128), F32)], axis=0)
    pieces = lax.all_to_all(
        value.reshape(half, each, 128), "batch", 0, 0, axis_index_groups=groups, tiled=True
    )
    mine = jnp.sum(pieces, axis=0)
    mine = mine + lax.ppermute(
        mine, "batch", [pair for a, b in zip(*groups) for pair in ((a, b), (b, a))]
    )
    full = lax.all_to_all(
        jnp.broadcast_to(mine[None], (half, each, 128)), "batch", 0, 0,
        axis_index_groups=groups, tiled=True,
    )
    return full.reshape(each * half, 128)[:rows]


def shards(
    states, next_states, actions, rewards, finished, valid_counts,
    trunk_input, trunk_middle, trunk_vector, head_weight, head_vector,
    critic_input, critic_middle, critic_vector,
    target_input, target_middle, target_vector,
    mean_trunk_input, square_trunk_input, mean_trunk_middle, square_trunk_middle,
    mean_trunk_vector, square_trunk_vector, mean_head_weight, square_head_weight,
    mean_head_vector, square_head_vector, mean_critic_input, square_critic_input,
    mean_critic_middle, square_critic_middle, mean_critic_vector, square_critic_vector,
):
    def turned(array):
        if array.ndim == 3 and array.shape[1] != HID:
            return jnp.transpose(array, (1, 0, 2))
        if array.ndim == 2 and array.shape[0] == HID:
            return array.T
        return array.reshape(1, -1) if array.ndim == 1 else array

    def back(array, like):
        if like.ndim == 3 and like.shape[1] != HID:
            return jnp.transpose(array, (1, 0, 2))
        if like.ndim == 2 and like.shape[0] == HID:
            return array.T
        return array.reshape(like.shape)

    params = [
        tuple(turned(array) for array in triple)
        for triple in (
            (trunk_input, mean_trunk_input, square_trunk_input),
            (trunk_middle, mean_trunk_middle, square_trunk_middle),
            (trunk_vector, mean_trunk_vector, square_trunk_vector),
            (head_weight, mean_head_weight, square_head_weight),
            (head_vector, mean_head_vector, square_head_vector),
            (critic_input, mean_critic_input, square_critic_input),
            (critic_middle, mean_critic_middle, square_critic_middle),
            (critic_vector, mean_critic_vector, square_critic_vector),
        )
    ]
    targets = tuple(turned(array) for array in (target_input, target_middle, target_vector))
    own = tuple(params[i][0] for i in (0, 1, 2, 5, 6, 7)) + targets
    lines = (states.shape[1] // 128, 128)
    data = (states, next_states, actions, rewards.reshape(lines), finished.reshape(lines))
    heads = (params[3][0], params[4][0])
    weights, message = run_pack(valid_counts, data, own)
    size = lax.axis_size("batch")
    both = (weights, across(weights))
    arrived = lax.ppermute(message, "batch", [(i, size - 1 - i) for i in range(size // 2, size)])
    own_part, other_part = run_main(data, heads, both, valid_counts)
    own_part, other_part = run_main((arrived, own_part, other_part), heads, both)
    results = list(run_lamb(summed(own_part + across(other_part)), params, targets))
    likes = (
        trunk_input, trunk_middle, trunk_vector, head_weight, head_vector,
        critic_input, critic_middle, critic_vector,
    ) * 3 + (target_input, target_middle, target_vector)
    final = [back(array, like) for array, like in zip(results, likes)]
    return tuple(final) + (jnp.transpose(results[27], (0, 2, 1)), results[28].reshape(5))


def solution(mesh):
    rows, matrix, vector, none = P(None, "batch"), P("net", None, None), P("net", None), P()
    line = P("batch")
    params = (matrix, matrix, vector, none, none, matrix, matrix, vector)
    moments = tuple(spec for entry in params for spec in (entry, entry))
    target = (matrix, matrix, vector)
    return jax.shard_map(
        shards,
        mesh=mesh,
        in_specs=(rows, rows, rows, line, line, line) + params + target + moments,
        out_specs=params * 3 + target + (matrix, none),
        check_vma=False,
    )
```

```python
import functools
import math

import jax
import jax.numpy as jnp
from jax import lax
from jax.experimental import pallas as pl
from jax.experimental.pallas import tpu as pltpu
from jax.sharding import PartitionSpec as P

STEP = 10
EXPECTILE = 0.7
DISCOUNT = 0.99
BETA_TEMP = 3.0
WEIGHT_CLIP = 100.0
DECAY_FIRST = 0.9
DECAY_SECOND = 0.999
EPSILON = 1e-06
WEIGHT_DECAY = 0.01
LEARN_RATE = 0.3
TARGET_RATE = 0.005
BAND = 32
LOG_TWO_PI = math.log(2.0 * math.pi)

OBS = 17
ACT = 6
HID = 256
TILE = 256
WIDTH = 7
UNROLL = 3
UNIT = 128
ROW_TRUNK = 2 * HID
ROW_CRITIC = ROW_TRUNK + 24
ROW_VECTOR = ROW_CRITIC + 24
ROW_HEAD = ROW_VECTOR + 8
PAYLOAD = ROW_HEAD + 8
VMEM_LIMIT = 64 * 2**20 - 2**17

META_ROW = OBS + ACT
NEXT_ROW = META_ROW + 1
PACK_ROWS = NEXT_ROW + OBS + 2
TRUNK, CRITIC, TARGET = range(3)
SMALL_ROW = 3 * HID
WEIGHT_ROWS = SMALL_ROW + 3 * 32
EXTRA_ROWS = 1024
HEAD_START = 0

F32 = jnp.float32
BF16 = jnp.bfloat16
NN = (((1,), (0,)), ((), ()))
NT = (((1,), (1,)), ((), ()))


def split(value):
    high = value.astype(BF16)
    return high, (value - high.astype(F32)).astype(BF16)


def dot(left, right, dims=NN):
    return lax.dot_general(left, right, dims, preferred_element_type=F32)


def fold(value):
    total = value[:, :128]
    for start in range(128, value.shape[1], 128):
        total = total + value[:, start : start + 128]
    return total


def left_parts(value):
    return jnp.concatenate(split(value), axis=0)


def column(row):
    return jnp.transpose(jnp.broadcast_to(row, (128, row.shape[1])))


def room_of(row_total):
    total, least = row_total // UNIT, -(-(row_total // 3) // UNIT)
    return max(2, -(-(total - (total + least) // 2) // 2))


def plan(count_ref, size, row_total):
    group, index = lax.axis_index("net"), lax.axis_index("batch")
    used = count_ref[0]
    units = (used + UNIT - 1) // UNIT
    total, room, lowest = row_total // UNIT, room_of(row_total), row_total // 3
    guess = (
        lowest
        + (size - 1 - index) * (row_total - lowest - row_total // 8) // max(size - 1, 1)
        + row_total // 16
    )
    kept = (used + guess + EXTRA_ROWS + 2 * UNIT - 1) // (2 * UNIT)
    kept = jnp.minimum(jnp.maximum(kept, units - 2 * room), units)
    kept = jnp.where(units - kept < 4, units, kept)
    kept = jnp.where(2 * index >= size, kept, units)
    sent = units - kept
    first = (sent + 1) // 2
    mine = jnp.minimum((kept + HEAD_START) // 2, kept)
    leading = group == 0
    start = kept + jnp.where(leading, 0, first)
    return dict(
        group=group, used=used,
        own_start=jnp.where(leading, 0, mine), own_count=jnp.where(leading, mine, kept - mine),
        sent_start=start, sent_count=jnp.where(leading, first, sent - first),
        window=jnp.minimum(start, total - room),
    )


def load(pairs, sems):
    copies = [
        pltpu.make_async_copy(source, target, sems.at[k])
        for k, (source, target) in enumerate(pairs)
    ]
    for copy in copies:
        copy.start()
    return copies


def pack_kernel(size, row_total, count_ref, *refs):
    sources, (weight_out, row_out), (arrive, leave, *parts) = refs[:14], refs[14:16], refs[16:]
    state_part, next_part, action_part, rewards, finished = parts[:5]
    weights, (small_part, row_part) = parts[5:14], parts[14:]
    room = room_of(row_total)
    copies = load(list(zip(sources[5:], weights)) + list(zip(sources[3:5], parts[3:5])), arrive)
    here = plan(count_ref, size, row_total)
    at = pl.ds(pl.multiple_of(here["window"] * UNIT, UNIT), room * UNIT)
    for k in range(3):
        copies.append(
            pltpu.make_async_copy(sources[k].at[:, at], parts[k], arrive.at[len(copies)])
        )
        copies[-1].start()
    sent = []

    def send(source, target):
        sent.append(pltpu.make_async_copy(source, target, leave.at[len(sent)]))
        sent[-1].start()

    for net in range(3):
        copies[3 * net + 1].wait()
        send(weights[3 * net + 1].at[0], weight_out.at[net * HID : (net + 1) * HID, :])
    for net in range(3):
        copies[3 * net].wait()
        copies[3 * net + 2].wait()
        rows, _, vector = weights[3 * net : 3 * net + 3]
        row = 32 * net
        width = rows.shape[0]
        pieces = [rows[:, 0, :]]
        if width < META_ROW:
            pieces.append(jnp.zeros((META_ROW - width, HID), F32))
        pieces.append(vector[:, :HID])
        small_part[row : row + 24, :] = jnp.concatenate(pieces, axis=0)
        pieces = [vector[:, HID : 2 * HID]]
        if vector.shape[1] > 2 * HID:
            pieces.append(vector[:, 2 * HID : 3 * HID])
            pieces.append(jnp.broadcast_to(vector[:, 3 * HID : 3 * HID + 1], (1, HID)))
        pieces.append(jnp.zeros((8 - len(pieces), HID), F32))
        small_part[row + 24 : row + 32, :] = jnp.concatenate(pieces, axis=0)
    send(small_part, weight_out.at[SMALL_ROW:, :])

    def line(ref):
        first = here["window"] * (UNIT // 128)
        return jnp.concatenate(
            [ref[pl.ds(first + k, 1), :] for k in range(room * UNIT // 128)], axis=1
        )

    lane = lax.broadcasted_iota(jnp.int32, (1, room * UNIT), 1)
    meta = jnp.zeros((1, room * UNIT), F32)
    for k, number in enumerate(
        (
            here["sent_start"] - here["window"], here["sent_count"],
            here["used"] - here["window"] * UNIT,
        )
    ):
        meta = jnp.where(lane == k, number.astype(F32), meta)
    for copy in copies[9:]:
        copy.wait()
    row_part[: META_ROW + 1, :] = jnp.concatenate([state_part[...], action_part[...], meta], axis=0)
    row_part[NEXT_ROW:, :] = jnp.concatenate(
        [next_part[...], line(rewards), line(finished).astype(F32)], axis=0
    )
    send(row_part, row_out)
    for copy in sent:
        copy.wait()


def run_pack(counts, data, weights):
    hbm = pl.BlockSpec(memory_space=pl.ANY)
    row_total = data[0].shape[1]
    span = room_of(row_total) * UNIT
    row_out = jax.ShapeDtypeStruct((PACK_ROWS, span), F32)
    held = [pltpu.VMEM((array.shape[0], span), F32) for array in data[:3]]
    held += [pltpu.VMEM(array.shape, array.dtype) for array in (*data[3:], *weights)]
    return pl.pallas_call(
        functools.partial(pack_kernel, lax.axis_size("batch"), row_total),
        out_shape=[jax.ShapeDtypeStruct((WEIGHT_ROWS, HID), F32), row_out],
        in_specs=[pl.BlockSpec(memory_space=pltpu.SMEM)] + [hbm] * (len(data) + len(weights)),
        out_specs=[hbm, hbm],
        scratch_shapes=[pltpu.SemaphoreType.DMA((14,)), pltpu.SemaphoreType.DMA((5,))]
        + held
        + [pltpu.VMEM((WEIGHT_ROWS - SMALL_ROW, HID), F32), pltpu.VMEM(row_out.shape, F32)],
        compiler_params=pltpu.CompilerParams(vmem_limit_bytes=VMEM_LIMIT),
        name="messages",
    )(counts, *data, *weights)


def weight_pairs(sources, targets):
    heads = list(zip(sources[:2], targets[:2]))
    parts = [slice(SMALL_ROW, WEIGHT_ROWS)]
    parts += [slice(net * HID, (net + 1) * HID) for net in (CRITIC, TARGET, TRUNK)]
    return heads + [
        (source.at[part, :], target.at[part, :])
        for part in parts
        for source, target in zip(sources[2:], targets[2:])
    ]


def main_kernel(size, count_ref, *refs):
    sources, outs, (arrive, leave, *refs) = refs[:9], refs[9:11], refs[11:]
    buffers, sums, scratch = refs[:9], refs[9:11], refs[11:]
    states, next_states, actions, rewards, finished = buffers[:5]
    pairs = weight_pairs(sources[5:], buffers[5:]) + list(zip(sources[:5], buffers[:5]))
    copies = load(pairs, arrive)

    def line(ref, start, width):
        return jnp.concatenate(
            [ref[pl.ds(start // 128 + part, 1), :] for part in range(width // 128)], axis=1
        )

    def rows_of(start, width):
        at = pl.ds(start, width)
        return (
            states[:, at], next_states[:, at], actions[:, at],
            line(rewards, start, width), line(finished, start, width).astype(F32),
        )

    here = plan(count_ref, size, states.shape[1])
    gradients(
        here["group"], here["own_start"], here["own_count"], here["used"], rows_of, copies, False,
        outs, leave, *buffers[5:], *sums, *scratch,
    )


def moved_kernel(size, packed_ref, *refs):
    inputs, outs, (arrive, leave, *refs) = refs[:6], refs[6:8], refs[8:]
    meta_part, packed, *buffers = refs[:6]
    sums, scratch = refs[6:8], refs[8:]

    def add(start, count, used):
        pairs = weight_pairs(inputs[2:], buffers)
        pairs += [(packed_ref, packed)] + list(zip(inputs[:2], sums))
        copies = load(pairs, arrive)

        def rows_of(start, width):
            at = pl.ds(start, width)
            return (
                packed[:OBS, at], packed[NEXT_ROW : NEXT_ROW + OBS, at], packed[OBS:META_ROW, at],
                packed[NEXT_ROW + OBS : NEXT_ROW + OBS + 1, at], packed[PACK_ROWS - 1 : PACK_ROWS, at],
            )

        gradients(
            lax.axis_index("net"), start, count, used, rows_of, copies, True, outs, leave,
            *buffers, *sums, *scratch,
        )

    @pl.when(2 * lax.axis_index("batch") < size)
    def _():
        copy = pltpu.make_async_copy(
            packed_ref.at[META_ROW - 7 : META_ROW + 1, :128], meta_part, arrive.at[0]
        )
        copy.start()
        copy.wait()
        meta = meta_part[7:8, :]
        place = lax.broadcasted_iota(jnp.int32, (1, 128), 1)
        start, count, used = (
            jnp.sum(jnp.where(place == k, meta, 0.0)).astype(jnp.int32) for k in range(3)
        )
        pl.when(count > 0)(lambda: add(start, count, used))


def gradients(
    group, start_unit, unit_count, used, rows_of, copies, adding, outs, leave,
    head_weight, head_vector, own, other, out_own, out_other, *scratch
):
    (
        first, second, back, bias_two, out_weight, head_pack, head_back, head_bias,
        acc_second, acc_first, acc_bias, acc_out, acc_head, acc_rows,
    ) = scratch

    def await_next(count):
        for _ in range(count):
            copies.pop(0).wait()

    copies = list(copies)
    await_next(4)

    head_columns = jnp.concatenate([head_weight[...], jnp.zeros((1, HID), F32)], axis=0)
    value_row = head_columns[0:1]
    action_rows = jnp.concatenate(
        [head_columns[1:7], jnp.zeros((2, HID), F32)], axis=0
    )
    row_high, row_low = split(jnp.concatenate([action_rows, jnp.zeros((8, HID), F32)], axis=0))
    head_pack[...] = jnp.concatenate([row_high, row_low], axis=0)
    mean_columns = jnp.transpose(
        jnp.concatenate([action_rows * 0.5, jnp.zeros((120, HID), F32)], axis=0)
    )[:, :16]
    mean_high, mean_low = split(mean_columns)
    head_back[...] = jnp.concatenate(
        [mean_high, mean_low, mean_high], axis=1
    )
    bias_column = jnp.transpose(
        jnp.concatenate(
            [
                jnp.concatenate([head_vector[...], jnp.zeros((1, 128 - 13), F32)], axis=1),
                jnp.zeros((127, 128), F32),
            ],
            axis=0,
        )
    )[:16, 0:1]
    head_bias[...] = jnp.broadcast_to(bias_column, (16, 128))

    is_value = group == 0

    def prepare(slot, net, take, out_row, with_back):
        row = SMALL_ROW + 32 * net
        packed = take(row, 24) * 0.5
        high = packed.astype(BF16).astype(F32)
        stack = jnp.concatenate(
            [high, high, packed - high, jnp.zeros((128 - 72, HID), F32)], axis=0
        )
        first[slot] = jnp.transpose(stack).astype(BF16)
        matrix = take(net * HID, HID)
        second[slot] = left_parts(jnp.transpose(matrix) * 0.5)
        bias_two[slot] = column(take(row + 24, 1) * 0.5)
        if out_row is not None:
            out_weight[slot] = column(out_row)
        if with_back:
            back[slot] = left_parts(matrix * (0.25 * out_row if out_row is not None else 0.5))

    def picked(first_ref, second_ref):
        return lambda row, count: jnp.where(
            is_value, first_ref[row : row + count, :], second_ref[row : row + count, :]
        )

    def small(ref, net, row):
        return ref[SMALL_ROW + 32 * net + 24 + row : SMALL_ROW + 32 * net + 25 + row, :]

    for slot, ref, net in (
        (2, own, CRITIC), (3, other, CRITIC), (4, own, TARGET), (5, other, TARGET),
    ):
        if slot % 2 == 0:
            await_next(2)
        take = lambda row, count, ref=ref: ref[row : row + count, :]
        prepare(slot, net, take, small(ref, net, 1), slot < 4)
    await_next(2)
    prepare(0, TRUNK, picked(own, other), value_row, True)
    prepare(1, TRUNK, picked(other, own), None, True)
    target_bias = [small(ref, TARGET, 2)[:, :1] for ref in (own, other)]
    critic_bias = [small(ref, CRITIC, 2)[:, :1] for ref in (own, other)]
    value_bias = head_vector[0:1, 0:1]

    acc_second[...] = jnp.zeros_like(acc_second)
    acc_first[...] = jnp.zeros_like(acc_first)
    acc_bias[...] = jnp.zeros_like(acc_bias)
    acc_out[...] = jnp.zeros_like(acc_out)
    acc_head[...] = jnp.zeros_like(acc_head)
    acc_rows[...] = jnp.zeros_like(acc_rows)

    def chains(start, width):
        start = pl.multiple_of(start, UNIT)
        states_t, next_t, actions_t, reward, done = rows_of(start, width)
        ones = jnp.ones((1, width), F32)
        place = start + lax.broadcasted_iota(jnp.int32, (1, width), 1)

        def wide(value):
            return jnp.concatenate([value] * (width // 128), axis=1)

        valid = (place < used).astype(F32)

        def pack(rows):
            full = jnp.concatenate([rows, actions_t, ones], axis=0)
            high = full.astype(BF16).astype(F32)
            low = full - high
            return jnp.concatenate(
                [high, low, high, jnp.zeros((128 - 72, width), F32)], axis=0
            ).astype(BF16)

        pairs = pack(states_t)
        pairs_next = pack(next_t)

        def product(ref, slot, high, low):
            both = dot(ref[slot], high)
            return both[:HID] + both[HID:] + dot(ref[slot, :HID], low)

        def layer(half):
            t = jnp.tanh(half)
            u = t + 1.0
            a = half * u
            return a, t, u

        def forward(slot, inputs, keep):
            half = dot(first[slot], inputs)
            yield
            a_one, t, u = layer(half)
            slope_one = u + a_one * (1.0 - t) if keep else None
            parts = split(a_one)
            yield
            z = product(second, slot, parts[0], parts[1])
            yield
            a_two, t, u = layer(z + wide(bias_two[slot]))
            slope_two = u + a_two * (1.0 - t) if keep else None
            return parts, slope_one, a_two, slope_two

        def weighted(slot, hidden):
            return jnp.sum(hidden * wide(out_weight[slot]), axis=0, keepdims=True)

        def backward(slot, parts, slope_one, delta_two):
            acc_bias[slot] += fold(delta_two)
            high, low = split(delta_two)
            yield
            delta_one = product(back, slot, high, low)
            acc_second[slot] += dot(
                jnp.concatenate([parts[0], parts[1], parts[0]], axis=1),
                jnp.concatenate([high, high, low], axis=1),
                NT,
            )
            yield
            high, low = split(delta_one * slope_one)
            yield
            rows = pairs[:48]
            acc_first[slot] += dot(
                jnp.concatenate([rows, rows], axis=1), jnp.concatenate([high, low], axis=1), NT
            )

        known = {}

        def next_chain():
            _, _, hidden, _ = yield from forward(0, pairs_next, False)
            value_next = weighted(0, hidden) + value_bias
            known["goal"] = reward + DISCOUNT * (1.0 - done) * value_next

        def target_chain(member):
            _, _, hidden, _ = yield from forward(4 + member, pairs, False)
            known["target", member] = weighted(4 + member, hidden) + target_bias[member]

        def critic_chain(member):
            slot = 2 + member
            parts, slope_one, hidden, slope_two = yield from forward(slot, pairs, True)
            error = (weighted(slot, hidden) + critic_bias[member] - known["goal"]) * valid
            grad = 2.0 * error
            known["critic", member] = (error * error, grad)
            acc_out[slot] += fold(hidden * grad)
            yield from backward(slot, parts, slope_one, slope_two * grad)

        def value_chain():
            parts, slope_one, hidden, slope_two = yield from forward(0, pairs, True)
            target_min = jnp.minimum(known["target", 0], known["target", 1])
            gap = target_min - (weighted(0, hidden) + value_bias)
            expect = jnp.where(gap < 0.0, 1.0 - EXPECTILE, EXPECTILE) * valid
            grad = -2.0 * expect * gap
            known["gap"] = gap
            known["value"] = (grad, expect * gap * gap)
            acc_out[0] += fold(hidden * grad)
            yield from backward(0, parts, slope_one, slope_two * grad)

        def actor_chain():
            parts, slope_one, hidden, slope_two = yield from forward(1, pairs, True)
            hidden_high, hidden_low = split(hidden)
            both = dot(head_pack[...], hidden_high)
            head = both[:8] + both[16:24] + dot(head_pack[:16], hidden_low)[:8]
            yield
            bias = wide(head_bias[...])
            mean = jnp.tanh(head[:6] + bias[1:7])
            log_std = bias[7:13]
            inverse = jnp.exp(-log_std)
            scaled = (actions_t - mean) * inverse
            log_prob = jnp.sum(
                -0.5 * scaled * scaled - log_std - 0.5 * LOG_TWO_PI, axis=0, keepdims=True
            )
            weight = jnp.minimum(jnp.exp(BETA_TEMP * known["gap"]), WEIGHT_CLIP) * valid
            grad_mean = -weight * scaled * inverse * (1.0 - mean * mean)
            grad_std = -weight * (scaled * scaled - 1.0)
            known["actor"] = (grad_mean, grad_std, -weight * log_prob)
            grads = jnp.concatenate([grad_mean, jnp.zeros((10, width), F32)], axis=0)
            grads_high, grads_low = split(grads)
            acc_head[...] += dot(jnp.concatenate([grads_high, grads_low], axis=0), hidden_high, NT)
            acc_head[:16] += dot(grads_high, hidden_low, NT)
            up = dot(
                head_back[...], jnp.concatenate([grads_high, grads_high, grads_low], axis=0)
            )
            yield
            yield from backward(1, parts, slope_one, up * slope_two)

        def finish():
            rows = jnp.concatenate(
                [known["value"][0], known["actor"][0], known["actor"][1], known["value"][1]]
                + [known["critic", 0][0], known["critic", 1][0], known["actor"][2], valid]
                + [known["critic", 0][1], known["critic", 1][1]]
                + [jnp.zeros((4, width), F32)],
                axis=0,
            )
            acc_rows[...] += fold(rows)

        return [
            next_chain(), target_chain(0), target_chain(1), critic_chain(0), value_chain(),
            actor_chain(), critic_chain(1),
        ], finish

    def tiles(starts, width=TILE):
        parts = [chains(start, width) for start in starts]
        waiting = [(chain, part) for part in parts for chain in part[0]]
        left = {id(part): len(part[0]) for part in parts}
        active = []
        while waiting or active:
            while waiting and len(active) < WIDTH:
                active.append(waiting.pop(0))
            for entry in list(active):
                chain, part = entry
                try:
                    next(chain)
                except StopIteration:
                    active.remove(entry)
                    left[id(part)] -= 1
                    if left[id(part)] == 0:
                        part[1]()

    base = start_unit * UNIT
    tile_count = unit_count * UNIT // TILE

    def several(i, carry):
        tiles([base + (UNROLL * i + k) * TILE for k in range(UNROLL)])
        return carry

    def single(i, carry):
        tiles([base + i * TILE])
        return carry

    await_next(len(copies) - (2 if adding else 0))
    rounds = tile_count // UNROLL
    lax.fori_loop(0, rounds, several, 0)
    if UNROLL > 1:
        lax.fori_loop(rounds * UNROLL, tile_count, single, 0)

    @pl.when(unit_count * UNIT > tile_count * TILE)
    def _():
        tiles([base + tile_count * TILE], UNIT)


    def store(out, row, value):
        count = value.shape[0]
        for half in range(2):
            at = slice(half * PAYLOAD + row, half * PAYLOAD + row + count)
            part = value[:, half * 128 : half * 128 + 128]
            out[at, :] = part + out[at, :] if adding else part

    def first_grad(slot):
        return acc_first[slot, :24] + acc_first[slot, 24:]

    def lanes(value):
        return jnp.sum(jnp.transpose(value), axis=0, keepdims=True)

    zero_row = jnp.zeros((1, HID), F32)
    row_sums = jnp.sum(
        jnp.transpose(jnp.concatenate([acc_rows[...], jnp.zeros((104, 128), F32)], axis=0)),
        axis=0,
        keepdims=True,
    )
    lane = lax.broadcasted_iota(jnp.int32, (1, 128), 1)
    swapped = jnp.where(
        lane == 14,
        pltpu.roll(row_sums, 127, 1),
        jnp.where(lane == 15, pltpu.roll(row_sums, 1, 1), row_sums),
    )
    shared_row = jnp.where(is_value, row_sums, swapped)
    head_actions = acc_head[:6] + acc_head[16:22]
    head_rows = jnp.concatenate([lanes(acc_out[0]), head_actions, zero_row], axis=0)
    out_rows = (
        value_row * 0.5, None, small(own, CRITIC, 1) * 0.5, small(other, CRITIC, 1) * 0.5,
    )

    def second_grad(slot):
        matrix, bias = acc_second[slot], lanes(acc_bias[slot])
        scale = out_rows[slot]
        return (matrix, bias) if scale is None else (matrix * scale, bias * scale)

    sent = []

    def send(row, count):
        for out, target in zip((out_own, out_other), outs):
            for half in range(2):
                at = slice(half * PAYLOAD + row, half * PAYLOAD + row + count)
                sent.append(
                    pltpu.make_async_copy(out.at[at, :], target.at[at, :], leave.at[len(sent)])
                )
                sent[-1].start()

    await_next(len(copies))
    trunk = [second_grad(slot) + (first_grad(slot),) for slot in range(2)]
    critic = [second_grad(2 + which) for which in range(2)]
    mixed = [
        [jnp.where(is_value, trunk[which][k], trunk[1 - which][k]) for k in range(3)]
        for which in range(2)
    ]
    for which, out in enumerate((out_own, out_other)):
        store(out, 0, mixed[which][0])
    send(0, HID)
    for which, out in enumerate((out_own, out_other)):
        store(out, HID, critic[which][0])
    send(HID, HID)
    for which, out in enumerate((out_own, out_other)):
        store(out, ROW_TRUNK, mixed[which][2])
        store(out, ROW_CRITIC, first_grad(2 + which))
        bias_grad = pltpu.roll(row_sums, 128 - 18 - which, 1)
        last = jnp.concatenate([shared_row, jnp.where(lane == 0, bias_grad, 0.0)], axis=1)
        store(
            out,
            ROW_VECTOR,
            jnp.concatenate(
                [mixed[which][1], critic[which][1], lanes(acc_out[2 + which]), last]
                + [zero_row] * 4,
                axis=0,
            ),
        )
        store(out, ROW_HEAD, head_rows)
    send(2 * HID, PAYLOAD - 2 * HID)
    for copy in sent:
        copy.wait()


def run_main(data, heads, weights, counts=None):
    hbm = pl.BlockSpec(memory_space=pl.ANY)
    size = lax.axis_size("batch")
    operands = (*data, *heads, *weights)
    payload = jax.ShapeDtypeStruct((2 * PAYLOAD, 128), F32)
    held = [pltpu.VMEM(array.shape, array.dtype) for array in (*heads, *weights)]
    semaphores = [pltpu.SemaphoreType.DMA((16,)), pltpu.SemaphoreType.DMA((12,))]
    if counts is None:
        name, body, specs, aliases = "moved_gradients", moved_kernel, [], {1: 0, 2: 1}
        buffers = [pltpu.VMEM((8, 128), F32), pltpu.VMEM(data[0].shape, F32)] + held
    else:
        name, body, aliases = "gradients", main_kernel, {}
        specs = [pl.BlockSpec(memory_space=pltpu.SMEM)]
        buffers = [pltpu.VMEM(array.shape, array.dtype) for array in data] + held
        operands = (counts,) + operands
    return pl.pallas_call(
        functools.partial(body, size),
        out_shape=[payload, payload],
        in_specs=specs + [hbm] * (len(operands) - len(specs)),
        out_specs=[hbm, hbm],
        input_output_aliases=aliases,
        scratch_shapes=semaphores + buffers + [pltpu.VMEM(payload.shape, F32)] * 2 + [
            pltpu.VMEM((6, HID, 128), BF16),
            pltpu.VMEM((6, 2 * HID, HID), BF16),
            pltpu.VMEM((4, 2 * HID, HID), BF16),
            pltpu.VMEM((6, HID, 128), F32),
            pltpu.VMEM((6, HID, 128), F32),
            pltpu.VMEM((32, HID), BF16),
            pltpu.VMEM((HID, 48), BF16),
            pltpu.VMEM((16, 128), F32),
            pltpu.VMEM((4, HID, HID), F32),
            pltpu.VMEM((4, 48, HID), F32),
            pltpu.VMEM((4, HID, 128), F32),
            pltpu.VMEM((4, HID, 128), F32),
            pltpu.VMEM((32, HID), F32),
            pltpu.VMEM((24, 128), F32),
        ],
        compiler_params=pltpu.CompilerParams(vmem_limit_bytes=VMEM_LIMIT),
        cost_estimate=pl.CostEstimate(
            flops=10**10, bytes_accessed=5 * 10**6, transcendentals=10**7
        ),
        name=name,
    )(*operands)


def read(ref):
    if len(ref.shape) == 2:
        return ref[...]
    return ref[:, 0, :] if ref.shape[1] == 1 else ref[0]


def write(ref, value):
    if len(ref.shape) == 2:
        ref[...] = value
    elif ref.shape[1] == 1:
        ref[:, 0, :] = value
    else:
        ref[0] = value


def lamb_kernel(*refs):
    count = 1 + 3 * len(NAMES) + 3
    inputs, targets_out = refs[:count], refs[count : count + 29]
    outs = refs[count + 29 : count + 58]
    steps, leave = refs[count + 58 :]
    sent = []

    def send(places):
        for at in places:
            copy = pltpu.make_async_copy(outs[at], targets_out[at], leave.at[at])
            copy.start()
            sent.append(copy)

    payload = inputs[0]
    params = [inputs[1 + 3 * i : 4 + 3 * i] for i in range(len(NAMES))]
    targets = inputs[count - 3 :]

    def rows(start, count):
        return jnp.concatenate(
            [payload[start : start + count, :], payload[PAYLOAD + start : PAYLOAD + start + count, :]],
            axis=1,
        )

    trunk_first = rows(ROW_TRUNK, 24)
    critic_first = rows(ROW_CRITIC, 24)
    vectors = rows(ROW_VECTOR, 8)
    head = rows(ROW_HEAD, 8)
    shared = vectors[3:4, :128]
    after = 1.0 / shared[:, 17:18]
    gradients = (
        trunk_first[:OBS],
        None,
        jnp.concatenate([trunk_first[23:24], vectors[0:1]], axis=1),
        head[:7],
        shared[:, :13],
        critic_first[: OBS + ACT],
        None,
        jnp.concatenate(
            [critic_first[23:24], vectors[1:2], vectors[2:3], vectors[3:4, 128:129]], axis=1
        ),
    )
    def moments(weight, gradient, mean_old, square_old):
        mean_new = DECAY_FIRST * mean_old + (1.0 - DECAY_FIRST) * gradient
        square_new = DECAY_SECOND * square_old + (1.0 - DECAY_SECOND) * gradient * gradient
        mean_hat = mean_new * (1.0 / (1.0 - DECAY_FIRST**STEP))
        square_hat = square_new * (1.0 / (1.0 - DECAY_SECOND**STEP))
        update = mean_hat / (jnp.sqrt(square_hat) + EPSILON) + WEIGHT_DECAY * weight
        return mean_new, square_new, update

    def total(value):
        return jnp.sum(jnp.sum(value * value, axis=0, keepdims=True), axis=1, keepdims=True)

    norms = {}
    updates = {}
    for i in (1, 6, 0, 2, 3, 4, 5, 7):
        weight_ref, mean_ref, square_ref = params[i]
        if i in (1, 6):
            weight_sum, update_sum = jnp.zeros((8, HID), F32), jnp.zeros((8, HID), F32)
            for band in range(0, HID, BAND):
                at = slice(band, band + BAND)
                weight = weight_ref[0, at, :]
                gradient = rows((0 if i == 1 else HID) + band, BAND) * after
                mean_new, square_new, update = moments(
                    weight, gradient, mean_ref[0, at, :], square_ref[0, at, :]
                )
                outs[8 + i][0, at, :] = mean_new
                outs[16 + i][0, at, :] = square_new
                steps[0 if i == 1 else 1, at, :] = update
                for k in range(0, BAND, 8):
                    weight_sum += weight[k : k + 8] * weight[k : k + 8]
                    update_sum += update[k : k + 8] * update[k : k + 8]
            over = lambda part: jnp.sum(
                jnp.sum(part, axis=0, keepdims=True), axis=1, keepdims=True
            )
            norms[i] = (jnp.sqrt(over(weight_sum)), jnp.sqrt(over(update_sum)))
            send((8 + i, 16 + i))
        else:
            weight = read(weight_ref)
            mean_new, square_new, updates[i] = moments(
                weight, gradients[i] * after, read(mean_ref), read(square_ref)
            )
            write(outs[8 + i], mean_new)
            write(outs[16 + i], square_new)
            norms[i] = (jnp.sqrt(total(weight)), jnp.sqrt(total(updates[i])))
    send([8 + k + i for i in (0, 2, 3, 4, 5, 7) for k in (0, 8)])
    for i, name in enumerate(NAMES):
        scale = LEARN_RATE * (norms[i][0] / norms[i][1])
        if i in (1, 6):
            for band in range(0, HID, BAND):
                at = slice(band, band + BAND)
                new = params[i][0][0, at, :] - scale * steps[0 if i == 1 else 1, at, :]
                outs[i][0, at, :] = new
                if i == 6:
                    outs[25][0, at, :] = (
                        (1.0 - TARGET_RATE) * targets[1][0, at, :] + TARGET_RATE * new
                    )
        else:
            new = read(params[i][0]) - scale * updates[i]
            write(outs[i], new)
            if i >= 5:
                write(
                    outs[19 + i], (1.0 - TARGET_RATE) * read(targets[i - 5]) + TARGET_RATE * new
                )
    lane = lax.broadcasted_iota(jnp.int32, (1, 8), 1)
    for row in range(2):
        line = jnp.zeros((1, 8), F32)
        for i, pair in norms.items():
            line = jnp.where(lane == i, pair[row], line)
        outs[27][0, row : row + 1, :] = line
    outs[28][...] = pltpu.roll(shared, 128 - 13, 1)[:, :5]
    send([*range(8), *range(24, 29)])
    for copy in sent:
        copy.wait()


NAMES = (
    "trunk_input", "trunk_middle", "trunk_vector", "head_weight", "head_vector",
    "critic_input", "critic_middle", "critic_vector",
)


def run_lamb(payload, params, targets):
    hbm = pl.BlockSpec(memory_space=pl.ANY)
    flat = [array for triple in params for array in triple]
    shapes = [jax.ShapeDtypeStruct(triple[0].shape, F32) for triple in params]
    outs = shapes * 3 + [jax.ShapeDtypeStruct(t.shape, F32) for t in targets]
    outs += [jax.ShapeDtypeStruct((1, 2, 8), F32), jax.ShapeDtypeStruct((1, 5), F32)]
    operands = (payload, *flat, *targets)
    return pl.pallas_call(
        lamb_kernel,
        out_shape=outs,
        in_specs=[pl.BlockSpec(memory_space=pltpu.VMEM)] * len(operands),
        out_specs=[hbm] * len(outs),
        scratch_shapes=[pltpu.VMEM(array.shape, array.dtype) for array in outs]
        + [
            pltpu.VMEM((2, HID, HID), F32),
            pltpu.SemaphoreType.DMA((len(outs),)),
        ],
        compiler_params=pltpu.CompilerParams(vmem_limit_bytes=16 * 2**20),
        name="update",
    )(*operands)


def add_kernel(left, right, out):
    for start in range(0, out.shape[0], 128):
        at = slice(start, start + 128)
        out[at, :] = left[at, :] + right[at, :]


def run_add(left, right):
    vmem = pl.BlockSpec(memory_space=pltpu.VMEM)
    return pl.pallas_call(
        add_kernel,
        out_shape=jax.ShapeDtypeStruct(left.shape, F32),
        in_specs=[vmem, vmem],
        out_specs=vmem,
        compiler_params=pltpu.CompilerParams(vmem_limit_bytes=8 * 2**20),
        name="join",
    )(left, right)


def across(value):
    size = lax.axis_size("net")
    return lax.ppermute(value, "net", [(i, size - 1 - i) for i in range(size)])


def summed(value):
    size = lax.axis_size("batch")
    if size % 2:
        return lax.psum(value, "batch")
    half = size // 2
    groups = [list(range(half)), list(range(half, size))]
    rows = value.shape[0]
    each = -(-rows // half)
    if each * half != rows:
        value = jnp.concatenate([value, jnp.zeros((each * half - rows, 128), F32)], axis=0)
    pieces = lax.all_to_all(
        value.reshape(half, each, 128), "batch", 0, 0, axis_index_groups=groups, tiled=True
    )
    mine = jnp.sum(pieces, axis=0)
    mine = mine + lax.ppermute(
        mine, "batch", [pair for a, b in zip(*groups) for pair in ((a, b), (b, a))]
    )
    full = lax.all_to_all(
        jnp.broadcast_to(mine[None], (half, each, 128)), "batch", 0, 0,
        axis_index_groups=groups, tiled=True,
    )
    return full.reshape(each * half, 128)[:rows]


def shards(
    states, next_states, actions, rewards, finished, valid_counts,
    trunk_input, trunk_middle, trunk_vector, head_weight, head_vector,
    critic_input, critic_middle, critic_vector,
    target_input, target_middle, target_vector,
    mean_trunk_input, square_trunk_input, mean_trunk_middle, square_trunk_middle,
    mean_trunk_vector, square_trunk_vector, mean_head_weight, square_head_weight,
    mean_head_vector, square_head_vector, mean_critic_input, square_critic_input,
    mean_critic_middle, square_critic_middle, mean_critic_vector, square_critic_vector,
):
    def turned(array):
        if array.ndim == 3 and array.shape[1] != HID:
            return jnp.transpose(array, (1, 0, 2))
        if array.ndim == 2 and array.shape[0] == HID:
            return array.T
        return array.reshape(1, -1) if array.ndim == 1 else array

    def back(array, like):
        if like.ndim == 3 and like.shape[1] != HID:
            return jnp.transpose(array, (1, 0, 2))
        if like.ndim == 2 and like.shape[0] == HID:
            return array.T
        return array.reshape(like.shape)

    params = [
        tuple(turned(array) for array in triple)
        for triple in (
            (trunk_input, mean_trunk_input, square_trunk_input),
            (trunk_middle, mean_trunk_middle, square_trunk_middle),
            (trunk_vector, mean_trunk_vector, square_trunk_vector),
            (head_weight, mean_head_weight, square_head_weight),
            (head_vector, mean_head_vector, square_head_vector),
            (critic_input, mean_critic_input, square_critic_input),
            (critic_middle, mean_critic_middle, square_critic_middle),
            (critic_vector, mean_critic_vector, square_critic_vector),
        )
    ]
    targets = tuple(turned(array) for array in (target_input, target_middle, target_vector))
    own = tuple(params[i][0] for i in (0, 1, 2, 5, 6, 7)) + targets
    lines = (states.shape[1] // 128, 128)
    data = (states, next_states, actions, rewards.reshape(lines), finished.reshape(lines))
    heads = (params[3][0], params[4][0])
    weights, message = run_pack(valid_counts, data, own)
    size = lax.axis_size("batch")
    both = (weights, across(weights))
    arrived = lax.ppermute(message, "batch", [(i, size - 1 - i) for i in range(size // 2, size)])
    own_part, other_part = run_main(data, heads, both, valid_counts)
    own_part, other_part = run_main((arrived, own_part, other_part), heads, both)
    results = list(run_lamb(summed(run_add(own_part, across(other_part))), params, targets))
    likes = (
        trunk_input, trunk_middle, trunk_vector, head_weight, head_vector,
        critic_input, critic_middle, critic_vector,
    ) * 3 + (target_input, target_middle, target_vector)
    final = [back(array, like) for array, like in zip(results, likes)]
    return tuple(final) + (jnp.transpose(results[27], (0, 2, 1)), results[28].reshape(5))


def solution(mesh):
    rows, matrix, vector, none = P(None, "batch"), P("net", None, None), P("net", None), P()
    line = P("batch")
    params = (matrix, matrix, vector, none, none, matrix, matrix, vector)
    moments = tuple(spec for entry in params for spec in (entry, entry))
    target = (matrix, matrix, vector)
    return jax.shard_map(
        shards,
        mesh=mesh,
        in_specs=(rows, rows, rows, line, line, line) + params + target + moments,
        out_specs=params * 3 + target + (matrix, none),
        check_vma=False,
    )
```
